256 devices in a mesh: dp: 64 (over x, z_hi, y), seq: 4 (over z_lo, core).
Axes of the slice: x: 4, y: 4, z: 8 (z_hi: 4, z_lo: 2; z = z_hi * 2 + z_lo), core: 2. Of those that a mesh axis runs over, the one named last changes fastest.
Arguments:
- features: bfloat16 [64, 4096, 512], P('dp', 'seq'), may hold values from -6 to 6
- w_five: bfloat16 [1536, 512], P('dp'), may hold values from -0.15625 to 0.15625
- w_six: bfloat16 [1024, 512], P('dp'), may hold values from -0.1875 to 0.1875
- w_seven: bfloat16 [1024, 512], P('dp'), may hold values from -0.1875 to 0.1875
- channel_params: bfloat16 [512, 11], P('dp'), may hold values from -1.2 to 1.5, as said below
- w_proj: bfloat16 [512, 1920], P('dp'), may hold values from -0.25 to 0.25
- proj_bias: bfloat16 [1920], P('dp'), may hold values from -3 to 3
- out_cotangent: bfloat16 [64, 512, 1920], P('dp', 'seq'), may hold values from -0.5 to 0.5
Outputs:
- projected: bfloat16 [64, 512, 1920], P('dp', 'seq')
- input_grad: bfloat16 [64, 4096, 512], P('dp', 'seq')
- grad_five: float32 [1536, 512], P('dp')
- grad_six: float32 [1024, 512], P('dp')
- grad_seven: float32 [1024, 512], P('dp')
- grad_channel: float32 [512, 11], P('dp')
- grad_proj: float32 [512, 1920], P('dp')
- grad_bias: float32 [1920], P('dp')
The draws below stay inside these ranges and needn't reach their ends.
Inputs may be any that keep to these rules, and one draw needn't show every extreme that they name: `channel_params`: columns 1, 4, 7 and 9 lie between 0.5 and 1.5; the other columns lie between -1.2 and 1.2.
All inputs are finite; a program needn't handle non-finite values.
Results may differ from the reference program's by a relative error of at most 0.017.
Values may be sent and summed in bfloat16 or wider, within the bound.
No kernel may reach another device: no remote copies, remote signals or barrier semaphores. Data moves between devices by JAX's collectives and lax.ppermute only.
A program may use at most 128 MiB of HBM per device.

```python
import jax
import jax.numpy as jnp
from jax import lax

CH = 512
WIDTH = 1920
SLAB = 512
SLABS = 64


def draw_channel_params(key, part):
    key = jax.random.fold_in(key, 7)
    key_gain, key_offset = jax.random.split(key)
    column = jnp.arange(11)
    is_gain = (column == 1) | (column == 4) | (column == 7) | (column == 9)
    gain_draw = jax.random.uniform(key_gain, (CH, 11), jnp.float32, 0.5, 1.5)
    offsets = jnp.clip(0.3 * jax.random.normal(key_offset, (CH, 11), jnp.float32), -1.2, 1.2)
    return jnp.where(is_gain[None, :], gain_draw, offsets).astype(jnp.bfloat16)


def block_scale(stream_key, dims, cuts, least, top_value):
    def one(position, blocks):
        draws = jax.random.uniform(jax.random.fold_in(jax.random.fold_in(stream_key, 6), position), (blocks,), jnp.float32, least / len(cuts), top_value / len(cuts))
        return jnp.repeat(jnp.exp(draws), dims[position] // blocks).reshape((-1,) + (1,) * (len(dims) - position - 1))

    loudness = one(*cuts[0])
    for cut in cuts[1:]:
        loudness = loudness * one(*cut)
    return loudness


def gaussian(rng, extent, width, limit, cuts=(), kind=jnp.bfloat16):
    drawn = jax.random.normal(rng, extent, jnp.float32) * width
    if len(cuts) > 0:
        drawn = block_scale(rng, extent, cuts, -0.22, 0.18) * drawn
    return jnp.clip(drawn, min=-limit, max=limit).astype(kind)


def setup_inputs(seed: int = 0) -> dict:
    streams_of = jax.random.split(jax.random.key(seed), 9)
    features = gaussian(streams_of[0], (SLABS, 8 * SLAB, CH), 1.0, 6.0, ((0, 64), (1, 4)))
    w_five = gaussian(streams_of[1], (3 * CH, CH), (3 * CH) ** -0.5, 0.15625, ((0, 64),))
    w_six = gaussian(streams_of[2], (2 * CH, CH), (2 * CH) ** -0.5, 0.1875, ((0, 64),))
    w_seven = gaussian(streams_of[3], (2 * CH, CH), (2 * CH) ** -0.5, 0.1875, ((0, 64),))
    channel_params = draw_channel_params(jax.random.fold_in(streams_of[8], 71), 0)
    w_proj = gaussian(streams_of[5], (CH, WIDTH), CH ** -0.5, 0.25, ((0, 64),))
    proj_bias = gaussian(streams_of[6], (WIDTH,), 0.5, 3.0, ((0, 64),))
    out_cotangent = gaussian(streams_of[7], (SLABS, SLAB, WIDTH), 0.0625, 0.5, ((0, 64), (1, 4)))
    return dict(features=features, w_five=w_five, w_six=w_six, w_seven=w_seven, channel_params=channel_params, w_proj=w_proj, proj_bias=proj_bias, out_cotangent=out_cotangent)


epsilon = 1e-05

def layer_norm(values):
    average = lax.optimization_barrier(jnp.mean(values, -1, keepdims=True))
    centred = values - average
    variance = lax.optimization_barrier(jnp.mean(centred * centred, -1, keepdims=True))
    return centred * lax.rsqrt(variance + epsilon)

def activate(preact, offset, scaling, shifting):
    return jax.nn.gelu(layer_norm(preact + offset) * scaling + shifting, approximate=False)

def finish(values, scaling, shifting):
    return layer_norm(values) * scaling + shifting

def contract_rows(left, right):
    return lax.dot_general(left, right, (((0,), (0,)), ((), ())), preferred_element_type=jnp.float32)

def contract_cols(left, right):
    return lax.dot_general(left, right, (((1,), (1,)), ((), ())), preferred_element_type=jnp.float32)

def forward_pass(inputs, next_row, weights, channel_f):
    w_five, w_six, w_seven, w_proj, bias_proj = weights
    channels = inputs.shape[1]
    frame_count = inputs.shape[0] // 2
    third_tap = jnp.concatenate([inputs[2::2], next_row], 0)
    unfold_five = jnp.concatenate([inputs.reshape(frame_count, 2 * channels), third_tap], 1)
    pre_five = jnp.dot(unfold_five, w_five, preferred_element_type=jnp.float32)
    act_five = activate(pre_five, channel_f[:, 0], channel_f[:, 1], channel_f[:, 2]).astype(jnp.bfloat16)
    unfold_six = act_five.reshape(frame_count // 2, 2 * channels)
    pre_six = jnp.dot(unfold_six, w_six, preferred_element_type=jnp.float32)
    act_six = activate(pre_six, channel_f[:, 3], channel_f[:, 4], channel_f[:, 5]).astype(jnp.bfloat16)
    unfold_seven = act_six.reshape(frame_count // 4, 2 * channels)
    pre_seven = jnp.dot(unfold_seven, w_seven, preferred_element_type=jnp.float32)
    act_seven = activate(pre_seven, channel_f[:, 6], channel_f[:, 7], channel_f[:, 8]).astype(jnp.bfloat16)
    normed = finish(act_seven.astype(jnp.float32), channel_f[:, 9], channel_f[:, 10]).astype(jnp.bfloat16)
    projected = (jnp.dot(normed, w_proj, preferred_element_type=jnp.float32) + bias_proj.astype(jnp.float32)).astype(jnp.bfloat16)
    saved = (unfold_five, pre_five, unfold_six, pre_six, unfold_seven, pre_seven, act_seven, normed)
    return (projected, saved)

def back_section(preact, columns, upstream, unfolded, weight):
    unused_out, pullback = jax.vjp(activate, preact, columns[0], columns[1], columns[2])
    pre_grad, offset_grad, scale_grad, shift_grad = pullback(upstream)
    pre_rounded = pre_grad.astype(jnp.bfloat16)
    grad_weight = contract_rows(unfolded, pre_rounded)
    unfold_grad = contract_cols(pre_rounded, weight)
    return (grad_weight, unfold_grad, jnp.stack([offset_grad, scale_grad, shift_grad], 1))

def backward_pass(saved, cotangent, weights, channel_f):
    w_five, w_six, w_seven, w_proj, bias_proj = weights
    unfold_five, pre_five, unfold_six, pre_six, unfold_seven, pre_seven, act_seven, normed = saved
    channels = pre_five.shape[1]
    grad_bias = lax.optimization_barrier(jnp.sum(cotangent.astype(jnp.float32), 0))
    grad_proj = contract_rows(normed, cotangent)
    normed_grad = contract_cols(cotangent, w_proj)
    unused_out, pullback = jax.vjp(finish, act_seven.astype(jnp.float32), channel_f[:, 9], channel_f[:, 10])
    act_grad, gain_grad, shift_grad = pullback(normed_grad)
    grad_seven, unfold_grad, stats_seven = back_section(pre_seven, (channel_f[:, 6], channel_f[:, 7], channel_f[:, 8]), act_grad, unfold_seven, w_seven)
    act_grad = unfold_grad.reshape(-1, channels)
    grad_six, unfold_grad, stats_six = back_section(pre_six, (channel_f[:, 3], channel_f[:, 4], channel_f[:, 5]), act_grad, unfold_six, w_six)
    act_grad = unfold_grad.reshape(-1, channels)
    grad_five, back_five, stats_five = back_section(pre_five, (channel_f[:, 0], channel_f[:, 1], channel_f[:, 2]), act_grad, unfold_five, w_five)
    grad_channel = jnp.concatenate([stats_five, stats_six, stats_seven, gain_grad[:, None], shift_grad[:, None]], 1)
    return (back_five, (grad_five, grad_six, grad_seven, grad_channel, grad_proj, grad_bias))

def assemble(back_five, carried):
    channels = back_five.shape[1] // 3
    third_back = back_five[:, 2 * channels:]
    shifted = jnp.concatenate([carried, third_back[:-1]], 0)
    first_half = back_five[:, :channels] + shifted
    joined = jnp.concatenate([first_half, back_five[:, channels:2 * channels]], 1)
    return joined.reshape(-1, channels).astype(jnp.bfloat16)

def reference(features, w_five, w_six, w_seven, channel_params, w_proj, proj_bias, out_cotangent):
    channel_f = channel_params.astype(jnp.float32)
    weights = (w_five, w_six, w_seven, w_proj, proj_bias)
    zero_totals = (jnp.zeros(w_five.shape, jnp.float32), jnp.zeros(w_six.shape, jnp.float32), jnp.zeros(w_seven.shape, jnp.float32), jnp.zeros(channel_params.shape, jnp.float32), jnp.zeros(w_proj.shape, jnp.float32), jnp.zeros(proj_bias.shape, jnp.float32))

    def slab_step(totals, slab_item):
        inputs, cotangent = slab_item
        next_row = jnp.zeros((1, inputs.shape[1]), inputs.dtype)
        projected, saved = forward_pass(inputs, next_row, weights, channel_f)
        back_five, grads = backward_pass(saved, cotangent, weights, channel_f)
        carried = jnp.zeros((1, inputs.shape[1]), back_five.dtype)
        input_grad = assemble(back_five, carried)
        totals = jax.tree.map(lambda left, right: left + right, totals, grads)
        return (totals, (projected, input_grad))
    totals, stacked = lax.scan(slab_step, zero_totals, (features, out_cotangent))
    return (stacked[0], stacked[1], totals[0], totals[1], totals[2], totals[3], totals[4], totals[5])
```

```python
import jax
import jax.numpy as jnp
from jax import lax
from jax.sharding import Mesh, PartitionSpec as P

epsilon = 1e-05
f32 = jnp.float32
bf16 = jnp.bfloat16
HALF = 256


def layer_norm(values):
    average = jnp.mean(values, -1, keepdims=True)
    centred = values - average
    variance = jnp.mean(centred * centred, -1, keepdims=True)
    return centred * lax.rsqrt(variance + epsilon)


def activate(preact, offset, scaling, shifting):
    return jax.nn.gelu(layer_norm(preact + offset) * scaling + shifting, approximate=False)


def finish(values, scaling, shifting):
    return layer_norm(values) * scaling + shifting


def contract_rows(left, right):
    return lax.dot_general(left, right, (((0,), (0,)), ((), ())), preferred_element_type=f32)


def contract_cols(left, right):
    return lax.dot_general(left, right, (((1,), (1,)), ((), ())), preferred_element_type=f32)


def forward_pass(inputs, next_row, weights, channel_f):
    w_five, w_six, w_seven, w_proj, bias_proj = weights
    channels = inputs.shape[1]
    frame_count = inputs.shape[0] // 2
    third_tap = jnp.concatenate([inputs[2::2], next_row], 0)
    unfold_five = jnp.concatenate([inputs.reshape(frame_count, 2 * channels), third_tap], 1)
    pre_five = jnp.dot(unfold_five, w_five, preferred_element_type=f32)
    act_five = activate(pre_five, channel_f[:, 0], channel_f[:, 1], channel_f[:, 2]).astype(bf16)
    unfold_six = act_five.reshape(frame_count // 2, 2 * channels)
    pre_six = jnp.dot(unfold_six, w_six, preferred_element_type=f32)
    act_six = activate(pre_six, channel_f[:, 3], channel_f[:, 4], channel_f[:, 5]).astype(bf16)
    unfold_seven = act_six.reshape(frame_count // 4, 2 * channels)
    pre_seven = jnp.dot(unfold_seven, w_seven, preferred_element_type=f32)
    act_seven = activate(pre_seven, channel_f[:, 6], channel_f[:, 7], channel_f[:, 8]).astype(bf16)
    normed = finish(act_seven.astype(f32), channel_f[:, 9], channel_f[:, 10]).astype(bf16)
    projected = (jnp.dot(normed, w_proj, preferred_element_type=f32) + bias_proj.astype(f32)).astype(bf16)
    saved = (unfold_five, pre_five, unfold_six, pre_six, unfold_seven, pre_seven, act_seven, normed)
    return (projected, saved)


def back_section(preact, columns, upstream, unfolded, weight):
    unused_out, pullback = jax.vjp(activate, preact, columns[0], columns[1], columns[2])
    pre_grad, offset_grad, scale_grad, shift_grad = pullback(upstream)
    pre_rounded = pre_grad.astype(bf16)
    grad_weight = contract_rows(unfolded, pre_rounded)
    unfold_grad = contract_cols(pre_rounded, weight)
    return (grad_weight, unfold_grad, jnp.stack([offset_grad, scale_grad, shift_grad], 1))


def backward_pass(saved, cotangent, weights, channel_f):
    w_five, w_six, w_seven, w_proj, bias_proj = weights
    unfold_five, pre_five, unfold_six, pre_six, unfold_seven, pre_seven, act_seven, normed = saved
    channels = pre_five.shape[1]
    grad_bias = jnp.sum(cotangent.astype(f32), 0)
    grad_proj = contract_rows(normed, cotangent)
    normed_grad = contract_cols(cotangent, w_proj)
    unused_out, pullback = jax.vjp(finish, act_seven.astype(f32), channel_f[:, 9], channel_f[:, 10])
    act_grad, gain_grad, shift_grad = pullback(normed_grad)
    grad_seven, unfold_grad, stats_seven = back_section(
        pre_seven, (channel_f[:, 6], channel_f[:, 7], channel_f[:, 8]), act_grad, unfold_seven, w_seven
    )
    act_grad = unfold_grad.reshape(-1, channels)
    grad_six, unfold_grad, stats_six = back_section(
        pre_six, (channel_f[:, 3], channel_f[:, 4], channel_f[:, 5]), act_grad, unfold_six, w_six
    )
    act_grad = unfold_grad.reshape(-1, channels)
    grad_five, back_five, stats_five = back_section(
        pre_five, (channel_f[:, 0], channel_f[:, 1], channel_f[:, 2]), act_grad, unfold_five, w_five
    )
    grad_channel = jnp.concatenate(
        [stats_five, stats_six, stats_seven, gain_grad[:, None], shift_grad[:, None]], 1
    )
    return (back_five, (grad_five, grad_six, grad_seven, grad_channel, grad_proj, grad_bias))


def assemble(back_five, carried):
    channels = back_five.shape[1] // 3
    third_back = back_five[:, 2 * channels :]
    shifted = jnp.concatenate([carried, third_back[:-1]], 0)
    first_half = back_five[:, :channels] + shifted
    joined = jnp.concatenate([first_half, back_five[:, channels : 2 * channels]], 1)
    return joined.reshape(-1, channels).astype(bf16)


def swap_cores(value):
    return lax.ppermute(value, "core", [(0, 1), (1, 0)])


def gather(shard):
    rows = shard.shape[0]
    core = lax.axis_index("core")
    half = jnp.where(core == 0, shard[:, :HALF], shard[:, HALF:])
    line = lax.all_to_all(jnp.broadcast_to(half[None], (4, rows, HALF)), "zh", 0, 0, tiled=True)
    plane = lax.all_to_all(
        jnp.broadcast_to(line[None], (16, 4, rows, HALF)), ("x", "y"), 0, 0, tiled=True
    )
    mine = plane.reshape(4, 4, 4, rows, HALF).transpose(0, 2, 1, 3, 4).reshape(64, rows, HALF)
    other = swap_cores(mine)
    return jnp.where(core == 0, mine, other), jnp.where(core == 0, other, mine)


def reduce(low, high):
    rows = low.shape[1]
    core = lax.axis_index("core")
    mine = jnp.where(core == 0, low, high)
    other = swap_cores(jnp.where(core == 0, high, low))
    total = (mine.astype(f32) + other.astype(f32)).astype(bf16)
    total = total.reshape(4, 4, 4, rows, HALF).transpose(0, 2, 1, 3, 4).reshape(16, 4, rows, HALF)
    plane = lax.all_to_all(total, ("x", "y"), 0, 0, tiled=True)
    total = jnp.sum(plane.astype(f32), 0).astype(bf16)
    line = jnp.broadcast_to(total[:, None], (4, 4, rows, HALF)).reshape(16, rows, HALF)
    line = lax.all_to_all(line, ("zh", "zl", "core"), 0, 0, tiled=True)
    total = jnp.sum(line.reshape(8, 2, rows, HALF).astype(f32), 0)
    return jnp.concatenate([total[0], total[1]], 1)


def proj_blocks(value, lead):
    value = jnp.pad(value, [(0, 0)] * (value.ndim - 1) + [(0, 128)])
    value = value.reshape(lead + (8, 2, 4, HALF))
    value = jnp.moveaxis(value, (-4, -3, -2, -1), (-3, -2, -4, -1))
    return value.reshape(lead + (32, 512))


def proj_rows(low, high):
    lead = low.shape[:-2]
    parts = [jnp.swapaxes(h.reshape(lead + (4, 8, HALF)), -3, -2).reshape(lead + (8, 1024)) for h in (low, high)]
    return jnp.concatenate(parts, -1)[..., :1920]


def shards(features, w_five, w_six, w_seven, channel_params, w_proj, proj_bias, out_cotangent):
    small = jnp.zeros((8, 512), bf16)
    small = small.at[:, :11].set(channel_params).at[0, HALF : HALF + 30].set(proj_bias)
    low_a, high_a = gather(jnp.concatenate([w_five, small], 0))
    low_b, high_b = gather(jnp.concatenate([w_six, w_seven, proj_blocks(w_proj, ())], 0))
    whole = lambda low, high, a, b: jnp.concatenate(
        [low[:, a:b].reshape(-1, HALF), high[:, a:b].reshape(-1, HALF)], 1
    )
    weights = (
        whole(low_a, high_a, 0, 24),
        whole(low_b, high_b, 0, 16),
        whole(low_b, high_b, 16, 32),
        proj_rows(low_b[:, 32:], high_b[:, 32:]).reshape(512, 1920),
        high_a[:, 24, :30].reshape(-1),
    )
    channel_f = low_a[:, 24:, :11].reshape(512, 11).astype(f32)
    inputs = features[0]
    next_row = lax.ppermute(inputs[:1], ("zl", "core"), [(1, 0), (2, 1), (3, 2)])
    projected, saved = forward_pass(inputs, next_row, weights, channel_f)
    back_five, grads = backward_pass(saved, out_cotangent[0], weights, channel_f)
    carried = lax.ppermute(back_five[-1:, 1024:], ("zl", "core"), [(0, 1), (1, 2), (2, 3)])
    input_grad = assemble(back_five, carried)
    grad_five, grad_six, grad_seven, grad_channel, grad_proj, grad_bias = grads
    grad_small = jnp.zeros((64, 8, 512), bf16)
    grad_small = grad_small.at[:, :, :11].set(grad_channel.reshape(64, 8, 11).astype(bf16))
    grad_small = grad_small.at[:, 0, HALF : HALF + 30].set(grad_bias.reshape(64, 30).astype(bf16))
    pack_b = jnp.concatenate(
        [
            grad_six.reshape(64, 16, 512).astype(bf16),
            grad_seven.reshape(64, 16, 512).astype(bf16),
            proj_blocks(grad_proj.reshape(64, 8, 1920).astype(bf16), (64,)),
        ],
        1,
    )
    pack_a = jnp.concatenate([grad_five.reshape(64, 24, 512).astype(bf16), grad_small], 1)
    sum_b = reduce(pack_b[:, :, :HALF], pack_b[:, :, HALF:])
    sum_a = reduce(pack_a[:, :, :HALF], pack_a[:, :, HALF:])
    return (
        projected[None],
        input_grad[None],
        sum_a[:24],
        sum_b[:16],
        sum_b[16:32],
        sum_a[24:, :11],
        proj_rows(sum_b[32:, :HALF], sum_b[32:, HALF:]),
        sum_a[24, HALF : HALF + 30],
    )


def solution(mesh):
    fine = Mesh(mesh.devices.reshape(4, 4, 4, 2, 2), ("x", "zh", "y", "zl", "core"))
    dp, seq = ("x", "zh", "y"), ("zl", "core")
    placed = (
        P(dp, seq, None),
        P(dp, None),
        P(dp, None),
        P(dp, None),
        P(dp, None),
        P(dp, None),
        P(dp),
        P(dp, seq, None),
    )
    return jax.shard_map(
        shards,
        mesh=fine,
        in_specs=placed,
        out_specs=(
            P(dp, seq, None),
            P(dp, seq, None),
            P(dp, None),
            P(dp, None),
            P(dp, None),
            P(dp, None),
            P(dp, None),
            P(dp),
        ),
        check_vma=False,
    )
```

```python
import jax
import jax.numpy as jnp
from jax import lax
from jax.experimental import pallas as pl
from jax.experimental.pallas import tpu as pltpu
from jax.sharding import Mesh, PartitionSpec as P

epsilon = 1e-05
f32 = jnp.float32
bf16 = jnp.bfloat16
CH = 512
WIDTH = 1920
HALF = 256
STEP = 32


def dot(left, right, contract=(1, 0)):
    return lax.dot_general(
        left, right, (((contract[0],), (contract[1],)), ((), ())), preferred_element_type=f32
    )


def call(body, outs, scratch=(), flops=0, moved=0):
    return pl.pallas_call(
        body,
        out_shape=[jax.ShapeDtypeStruct(shape, kind) for shape, kind in outs],
        scratch_shapes=[pltpu.VMEM(shape, kind) for shape, kind in scratch],
        compiler_params=pltpu.CompilerParams(vmem_limit_bytes=40 * 2**20),
        cost_estimate=pl.CostEstimate(flops=flops, bytes_accessed=moved, transcendentals=0),
    )


def scalar_call(body, arrays, outs, scratch, flops, moved):
    whole = pl.BlockSpec(memory_space=pltpu.VMEM)
    return pl.pallas_call(
        body,
        out_shape=[jax.ShapeDtypeStruct(shape, kind) for shape, kind in outs],
        in_specs=[pl.BlockSpec(memory_space=pltpu.SMEM)] + [whole] * arrays,
        scratch_shapes=[pltpu.VMEM(shape, kind) for shape, kind in scratch],
        compiler_params=pltpu.CompilerParams(vmem_limit_bytes=40 * 2**20),
        cost_estimate=pl.CostEstimate(flops=flops, bytes_accessed=moved, transcendentals=0),
    )


def place(index):
    return (index // 16) * 16 + (index % 4) * 4 + (index // 4) % 4


def rows(index, size):
    return pl.ds(pl.multiple_of(index * size, size), size)


def by_core(core_ref, body):
    @pl.when(core_ref[0] == 0)
    def _():
        body(0, HALF)

    @pl.when(core_ref[0] != 0)
    def _():
        body(HALF, 0)


def row_mean(values):
    return jnp.sum(values, -1, keepdims=True) * (1.0 / CH)


def standard(values):
    centred = values - row_mean(values)
    scale = lax.rsqrt(row_mean(centred * centred) + epsilon)
    return centred * scale, scale


def fold(values):
    return jnp.sum(values.reshape(-1, 8, values.shape[-1]), 0)


def block_forward(pre_ref, cp_ref, first, act_ref, unit_ref, slope_ref, scale_ref):
    offset, gain, shift = (cp_ref[first + i : first + i + 1] for i in range(3))

    def step(i, _):
        at = rows(i, STEP)
        unit, scale = standard(pre_ref[at, :] + offset)
        z = unit * gain + shift
        cdf = 0.5 + 0.5 * lax.erf(z * 0.7071067811865476)
        act_ref[at, :] = (z * cdf).astype(bf16)
        slope_ref[at, :] = cdf + z * (0.3989422804014327 * jnp.exp(-0.5 * z * z))
        unit_ref[at, :] = unit
        scale_ref[at, :] = jnp.broadcast_to(scale, (STEP, 128))
        return 0

    lax.fori_loop(0, pre_ref.shape[0] // STEP, step, 0)


def block_backward(grad_ref, cp_ref, first, unit_ref, slope_ref, scale_ref, out_ref):
    gain = cp_ref[first + 1 : first + 2]

    def step(i, sums):
        at = rows(i, STEP)
        unit = unit_ref[at, :]
        dz = grad_ref[at, :] * slope_ref[at, :]
        dunit = dz * gain
        du = scale_ref[at, :1] * (dunit - row_mean(dunit) - unit * row_mean(dunit * unit))
        out_ref[at, :] = du.astype(bf16)
        return (sums[0] + fold(du), sums[1] + fold(dz * unit), sums[2] + fold(dz))

    zero = jnp.zeros((8, CH), f32)
    return lax.fori_loop(0, grad_ref.shape[0] // STEP, step, (zero, zero, zero))


def total(values):
    return jnp.sum(values, 0, keepdims=True)


def spread(transposed):
    group = lax.broadcasted_iota(jnp.int32, (256, 256), 1 if transposed else 0)
    position = lax.broadcasted_iota(jnp.int32, (256, 256), 0 if transposed else 1)
    return (position == 8 * (group % 32) + group // 32).astype(bf16)


def split_kernel(x_ref, next_ref, even_ref, odd_ref, third_ref, first_ref):
    matrix = spread(False)
    for j in range(4):
        groups = dot(matrix, x_ref[256 * j : 256 * j + 256, :])
        first_ref[32 * j : 32 * j + 32, :] = groups[:32]
        groups = groups.astype(bf16)
        for r in range(4):
            at = slice(128 * r + 32 * j, 128 * r + 32 * j + 32)
            even_ref[at, :] = groups[64 * r : 64 * r + 32]
            odd_ref[at, :] = groups[64 * r + 32 : 64 * r + 64]
            if r > 0:
                third_ref[128 * r - 128 + 32 * j : 128 * r - 96 + 32 * j, :] = groups[64 * r : 64 * r + 32]
    later = pltpu.roll(first_ref[...], 127, 0)
    last = lax.broadcasted_iota(jnp.int32, (128, CH), 0) == 127
    third_ref[384:512, :] = jnp.where(last, next_ref[:1, :].astype(f32), later).astype(bf16)


def five_forward_kernel(
    core_ref, even_ref, odd_ref, third_ref, mine_ref, other_ref,
    act_ref, unit_ref, slope_ref, scale_ref, w_ref, cp_ref, wide_ref, small_ref, pre_ref,
):
    def body(mine_at, other_at):
        def step(i, _):
            to = place(i)
            for ref, at in ((mine_ref, mine_at), (other_ref, other_at)):
                block = ref[i].astype(f32)
                wide_ref[rows(to, 24), at : at + HALF] = block[:24]
                if at == 0:
                    small_ref[rows(to, 8), :] = block[24:, :128]
            return 0

        lax.fori_loop(0, 64, step, 0)

    by_core(core_ref, body)
    cp_ref[...] = small_ref[...].T[:16]

    def narrow(i, _):
        w_ref[rows(i, 128), :] = wide_ref[rows(i, 128), :].astype(bf16)
        return 0

    lax.fori_loop(0, 12, narrow, 0)

    def multiply(r, _):
        at = rows(r, 128)
        pre_ref[at, :] = (
            dot(even_ref[at, :], w_ref[:512, :]) + dot(odd_ref[at, :], w_ref[512:1024, :])
        ) + dot(third_ref[at, :], w_ref[1024:, :])
        return 0

    lax.fori_loop(0, 4, multiply, 0)
    block_forward(pre_ref, cp_ref, 0, act_ref, unit_ref, slope_ref, scale_ref)


def upper_kernel(
    core_ref, five_ref, mine_ref, other_ref, cp_ref, bias_ref, cot_ref,
    out_ref, grad_ref, sums_ref, give_ref, send_ref,
    w6_ref, w7_ref, wp_ref, wide_ref,
    pre6_ref, act6_ref, unit6_ref, slope6_ref, scale6_ref,
    pre7_ref, act7_ref, unit7_ref, slope7_ref, scale7_ref,
    g6_ref, g7_ref, gp_ref, d6_ref, d7_ref,
):
    def unpack(mine_at, other_at):
        def step(i, _):
            to = place(i)
            for ref, at in ((mine_ref, mine_at), (other_ref, other_at)):
                w6_ref[rows(to, 16), at : at + HALF] = ref[i, :16]
                w7_ref[rows(to, 16), at : at + HALF] = ref[i, 16:32]
                block = ref[i, 32:].astype(f32)
                for b in range(4):
                    wide_ref[rows(to, 8), 4 * at + HALF * b : 4 * at + HALF * (b + 1)] = block[8 * b : 8 * b + 8]
            return 0

        lax.fori_loop(0, 64, step, 0)

    by_core(core_ref, unpack)

    def narrow(i, _):
        wp_ref[rows(i, 64), :] = wide_ref[rows(i, 64), :WIDTH].astype(bf16)
        return 0

    lax.fori_loop(0, 8, narrow, 0)

    for s in range(2):
        pre6_ref[128 * s : 128 * s + 128, :] = dot(five_ref[256 * s : 256 * s + 128, :], w6_ref[:512, :]) + dot(
            five_ref[256 * s + 128 : 256 * s + 256, :], w6_ref[512:, :]
        )
    block_forward(pre6_ref, cp_ref, 3, act6_ref, unit6_ref, slope6_ref, scale6_ref)
    pre7_ref[...] = dot(act6_ref[:128, :], w7_ref[:512, :]) + dot(act6_ref[128:, :], w7_ref[512:, :])
    block_forward(pre7_ref, cp_ref, 6, act7_ref, unit7_ref, slope7_ref, scale7_ref)

    unit, scale = standard(act7_ref[...].astype(f32))
    normed = (unit * cp_ref[9:10] + cp_ref[10:11]).astype(bf16)
    flipped = normed.astype(f32).T.astype(bf16)
    normed_grad = jnp.zeros((128, CH), f32)
    for b in range(8):
        cols = slice(HALF * b, min(HALF * (b + 1), WIDTH))
        out_ref[:, cols] = (dot(normed, wp_ref[:, cols]) + bias_ref[:, cols]).astype(bf16)
        cot = cot_ref[:, cols]
        gp_ref[:, cols] = dot(flipped, cot)
        normed_grad = normed_grad + dot(cot, wp_ref[:, cols], (1, 1))
    gp_ref[:, WIDTH:] = jnp.zeros((CH, 8 * HALF - WIDTH), f32)

    dunit = normed_grad * cp_ref[9:10]
    sums_ref[9:10, :] = total(normed_grad * unit)
    sums_ref[10:11, :] = total(normed_grad)
    pre7_ref[...] = scale * (dunit - row_mean(dunit) - unit * row_mean(dunit * unit))

    for i, part in enumerate(block_backward(pre7_ref, cp_ref, 6, unit7_ref, slope7_ref, scale7_ref, d7_ref)):
        sums_ref[6 + i : 7 + i, :] = total(part)
    for s in range(2):
        half = slice(512 * s, 512 * s + 512)
        g7_ref[half, :] = dot(act6_ref[128 * s : 128 * s + 128, :], d7_ref[...], (0, 0))
        pre6_ref[128 * s : 128 * s + 128, :] = dot(d7_ref[...], w7_ref[half, :], (1, 1))
    for i, part in enumerate(block_backward(pre6_ref, cp_ref, 3, unit6_ref, slope6_ref, scale6_ref, d6_ref)):
        sums_ref[3 + i : 4 + i, :] = total(part)
    for r in range(2):
        half = slice(512 * r, 512 * r + 512)
        g6_ref[half, :] = dot(five_ref[128 * r : 128 * r + 128, :], d6_ref[:128, :], (0, 0)) + dot(
            five_ref[256 + 128 * r : 384 + 128 * r, :], d6_ref[128:, :], (0, 0)
        )
        for s in range(2):
            at = 256 * s + 128 * r
            grad_ref[at : at + 128, :] = dot(d6_ref[128 * s : 128 * s + 128, :], w6_ref[half, :], (1, 1))
    for i in (0, 1, 2, 11, 12, 13, 14, 15):
        sums_ref[i : i + 1, :] = jnp.zeros((1, CH), f32)

    def pack(mine_at, other_at):
        def step(i, _):
            to = place(i)
            for ref, at in ((give_ref, mine_at), (send_ref, other_at)):
                ref[i, :16, :] = g6_ref[rows(to, 16), at : at + HALF].astype(bf16)
                ref[i, 16:32, :] = g7_ref[rows(to, 16), at : at + HALF].astype(bf16)
                block = gp_ref[rows(to, 8), 4 * at : 4 * at + 4 * HALF]
                parts = [block[:, HALF * b : HALF * (b + 1)] for b in range(4)]
                ref[i, 32:, :] = jnp.concatenate(parts, 0).astype(bf16)
            return 0

        lax.fori_loop(0, 64, step, 0)

    by_core(core_ref, pack)


def five_backward_kernel(
    core_ref, grad_ref, even_ref, odd_ref, third_ref, unit_ref, slope_ref, scale_ref, w_ref, cp_ref, sums_ref, gb_ref,
    give_ref, send_ref, d_ref, edge_ref, g_ref, small_ref,
):
    parts = block_backward(grad_ref, cp_ref, 0, unit_ref, slope_ref, scale_ref, d_ref)
    for i, part in enumerate(parts):
        small_ref[i : i + 1, :] = total(part)
    small_ref[3:11, :] = sums_ref[3:11, :]
    small_ref[11:, :] = jnp.zeros((117, CH), f32)
    columns = small_ref[...].T
    edge_ref[...] = dot(d_ref[496:512, :], w_ref[1024:, :], (1, 1))[8:]
    for k, ref in enumerate((even_ref, odd_ref, third_ref)):
        g_ref[512 * k : 512 * k + 512, :] = dot(ref[...], d_ref[...], (0, 0))
    for i in range(4):
        small_ref[:, 128 * i : 128 * i + 128] = columns[128 * i : 128 * i + 128, :]

    def pack(mine_at, other_at):
        for x in range(4):

            def step(i, _, x=x):
                at_shard = 16 * x + i
                to = place(at_shard)
                for ref, at in ((give_ref, mine_at), (send_ref, other_at)):
                    if at == 0:
                        low = small_ref[rows(to - 16 * x, 8), 128 * x : 128 * x + 128]
                        tail = jnp.concatenate([low, gb_ref[rows(to, 8), :]], 1)
                    else:
                        tail = jnp.zeros((8, HALF), f32)
                    block = jnp.concatenate([g_ref[rows(to, 24), at : at + HALF], tail], 0)
                    ref[at_shard] = block.astype(bf16)
                return 0

            lax.fori_loop(0, 16, step, 0)

    by_core(core_ref, pack)


def input_kernel(d_ref, w_ref, carried_ref, out_ref, even_ref, odd_ref, third_ref):
    def multiply(r, _):
        at = rows(r, 128)
        d = d_ref[at, :]
        even_ref[at, :] = dot(d, w_ref[:512, :], (1, 1))
        odd_ref[at, :] = dot(d, w_ref[512:1024, :], (1, 1))
        third_ref[at, :] = dot(d, w_ref[1024:, :], (1, 1))
        return 0

    lax.fori_loop(0, 4, multiply, 0)
    earlier = pltpu.roll(third_ref[384:512, :], 1, 0)
    first = lax.broadcasted_iota(jnp.int32, (128, CH), 0) == 0
    even_ref[:128, :] += jnp.where(first, carried_ref[...], earlier)
    even_ref[128:, :] += third_ref[:384, :]
    matrix = spread(True)
    for j in range(4):
        parts = []
        for r in range(4):
            at = slice(128 * r + 32 * j, 128 * r + 32 * j + 32)
            parts += [even_ref[at, :].astype(bf16), odd_ref[at, :].astype(bf16)]
        out_ref[256 * j : 256 * j + 256, :] = dot(matrix, jnp.concatenate(parts, 0)).astype(bf16)


def swap_cores(value):
    return lax.ppermute(value, "core", [(0, 1), (1, 0)])


def gather(shard, core):
    count = shard.shape[0]
    half = jnp.where(core == 0, shard[:, :HALF], shard[:, HALF:])
    line = lax.all_to_all(jnp.broadcast_to(half[None], (4, count, HALF)), "zh", 0, 0, tiled=True)
    plane = lax.all_to_all(
        jnp.broadcast_to(line[None], (16, 4, count, HALF)), ("x", "y"), 0, 0, tiled=True
    )
    mine = plane.reshape(64, count, HALF)
    return mine, swap_cores(mine)


def reduce(give, send):
    count = give.shape[1]
    summed = (give.astype(f32) + swap_cores(send).astype(f32)).astype(bf16)
    plane = lax.all_to_all(summed.reshape(16, 4, count, HALF), ("x", "y"), 0, 0, tiled=True)
    summed = jnp.sum(plane.astype(f32), 0).astype(bf16)
    line = jnp.broadcast_to(summed[:, None], (4, 4, count, HALF)).reshape(16, count, HALF)
    line = lax.all_to_all(line, ("zh", "zl", "core"), 0, 0, tiled=True)
    return jnp.sum(line.reshape(8, 2, count, HALF).astype(f32), 0)


def proj_blocks(value):
    value = jnp.pad(value, [(0, 0), (0, 8 * HALF - WIDTH)]).reshape(8, 2, 4, HALF)
    return value.transpose(2, 0, 1, 3).reshape(32, 512)


def proj_rows(halves):
    return halves.reshape(2, 4, 8, HALF).transpose(2, 0, 1, 3).reshape(8, 8 * HALF)[:, :WIDTH]


def shards(features, w_five, w_six, w_seven, channel_params, w_proj, proj_bias, out_cotangent):
    core = lax.axis_index("core")
    core_at = core.astype(jnp.int32).reshape(1)
    inputs, cotangent = features[0], out_cotangent[0]

    small = jnp.concatenate(
        [
            jnp.pad(channel_params, [(0, 0), (0, 117)]),
            jnp.pad(proj_bias[None], [(0, 7), (0, 98)]),
            jnp.zeros((8, HALF), bf16),
        ],
        1,
    )
    mine_a, other_a = gather(jnp.concatenate([w_five, small], 0), core)
    mine_b, other_b = gather(jnp.concatenate([w_six, w_seven, proj_blocks(w_proj)], 0), core)
    next_row = lax.ppermute(inputs[:8], ("zl", "core"), [(1, 0), (2, 1), (3, 2)])

    square = (512, CH)
    even, odd, third, _ = call(
        split_kernel, [(square, bf16)] * 3 + [((128, CH), f32)], flops=2**28, moved=3 * 2**20
    )(inputs, next_row)
    grad_bias = jnp.sum(cotangent.astype(f32), 0).reshape(64, 1, 30)
    grad_bias = jnp.pad(grad_bias, [(0, 0), (0, 7), (0, 98)]).reshape(512, 128)

    low_a = jnp.where(core == 0, mine_a[:, 24, 128:158], other_a[:, 24, 128:158])
    bias = low_a.reshape(4, 4, 4, 30).transpose(0, 2, 1, 3).reshape(1, WIDTH).astype(f32)

    act_five, unit_five, slope_five, scale_five, w5, cp = scalar_call(
        five_forward_kernel,
        5,
        [(square, bf16), (square, f32), (square, f32), ((512, 128), f32), ((1536, CH), bf16), ((16, CH), f32)],
        [((1536, CH), f32), ((512, 128), f32), (square, f32)],
        flops=2**30,
        moved=8 * 2**20,
    )(core_at, even, odd, third, mine_a, other_a)

    half_rows = lambda n: [((n, CH), f32), ((n, CH), bf16), ((n, CH), f32), ((n, CH), f32), ((n, 128), f32)]
    projected, act_grad, sums, give_b, send_b = scalar_call(
        upper_kernel,
        6,
        [((128, WIDTH), bf16), (square, f32), ((16, CH), f32), ((64, 64, HALF), bf16), ((64, 64, HALF), bf16)],
        [((1024, CH), bf16), ((1024, CH), bf16), ((CH, WIDTH), bf16), ((CH, 8 * HALF), f32)]
        + half_rows(256)
        + half_rows(128)
        + [((1024, CH), f32), ((1024, CH), f32), ((CH, 8 * HALF), f32), ((256, CH), bf16), ((128, CH), bf16)],
        flops=2**31,
        moved=12 * 2**20,
    )(core_at, act_five, mine_b, other_b, cp, bias, cotangent)
    sum_b = reduce(give_b, send_b)

    give_a, send_a, d_five, edge = scalar_call(
        five_backward_kernel,
        11,
        [((64, 32, HALF), bf16), ((64, 32, HALF), bf16), (square, bf16), ((8, CH), f32)],
        [((1536, CH), f32), ((128, CH), f32)],
        flops=2**30,
        moved=8 * 2**20,
    )(core_at, act_grad, even, odd, third, unit_five, slope_five, scale_five, w5, cp, sums, grad_bias)
    sum_a = reduce(give_a, send_a)

    carried = lax.ppermute(edge[7:8], ("zl", "core"), [(0, 1), (1, 2), (2, 3)])
    (input_grad,) = call(
        input_kernel, [((1024, CH), bf16)], [(square, f32)] * 3, flops=2**30, moved=4 * 2**20
    )(d_five, w5, carried)

    joined = lambda halves: jnp.concatenate([halves[0], halves[1]], 1)
    return (
        projected[None],
        input_grad[None],
        joined(sum_a[:, :24]),
        joined(sum_b[:, :16]),
        joined(sum_b[:, 16:32]),
        sum_a[0, 24:, :11],
        proj_rows(sum_b[:, 32:]),
        sum_a[0, 24, 128:158],
    )


def solution(mesh):
    fine = Mesh(mesh.devices.reshape(4, 4, 4, 2, 2), ("x", "zh", "y", "zl", "core"))
    dp, seq = ("x", "zh", "y"), ("zl", "core")
    placed = (
        P(dp, seq, None),
        P(dp, None),
        P(dp, None),
        P(dp, None),
        P(dp, None),
        P(dp, None),
        P(dp),
        P(dp, seq, None),
    )
    return jax.shard_map(
        shards,
        mesh=fine,
        in_specs=placed,
        out_specs=(
            P(dp, seq, None),
            P(dp, seq, None),
            P(dp, None),
            P(dp, None),
            P(dp, None),
            P(dp, None),
            P(dp, None),
            P(dp),
        ),
        check_vma=False,
    )
```

```python
import jax
import jax.numpy as jnp
from jax import lax
from jax.experimental import pallas as pl
from jax.experimental.pallas import tpu as pltpu
from jax.sharding import Mesh, PartitionSpec as P

epsilon = 1e-05
f32 = jnp.float32
bf16 = jnp.bfloat16
CH = 512
WIDTH = 1920
HALF = 256
STEP = 32
ALL_VMEM = 2**26 - 2**18


def dot(left, right, contract=(1, 0)):
    return lax.dot_general(
        left, right, (((contract[0],), (contract[1],)), ((), ())), preferred_element_type=f32
    )


def staged(body, operands, outs, scratch, flops, moved):
    count, made = len(operands) - 1, len(outs)

    def kernel(place_ref, *refs):
        refs = list(refs)
        groups = []
        for size in (count, made, count, made):
            groups.append(refs[:size])
            refs = refs[size:]
        from_hbm, to_hbm, ins, results = groups
        in_sems, out_sems, *rest = refs
        loads = [pltpu.make_async_copy(a, b, in_sems.at[i]) for i, (a, b) in enumerate(zip(from_hbm, ins))]
        stores = [pltpu.make_async_copy(a, b, out_sems.at[i]) for i, (a, b) in enumerate(zip(results, to_hbm))]
        for load in loads:
            load.start()
        waited, sent = set(), set()

        def need(*which):
            for ref in which:
                index = next(i for i, own in enumerate(ins) if own is ref)
                if index not in waited:
                    waited.add(index)
                    loads[index].wait()

        def give(*which):
            for ref in which:
                index = next(i for i, own in enumerate(results) if own is ref)
                if index not in sent:
                    sent.add(index)
                    stores[index].start()

        body(place_ref, ins, results, rest, need, give)
        need(*ins)
        give(*results)
        for store in stores:
            store.wait()

    hbm = pl.BlockSpec(memory_space=pltpu.HBM)
    return pl.pallas_call(
        kernel,
        out_shape=[jax.ShapeDtypeStruct(shape, kind) for shape, kind in outs],
        in_specs=[pl.BlockSpec(memory_space=pltpu.SMEM)] + [hbm] * count,
        out_specs=[hbm] * made,
        scratch_shapes=[pltpu.VMEM(array.shape, array.dtype) for array in operands[1:]]
        + [pltpu.VMEM(shape, kind) for shape, kind in outs]
        + [pltpu.SemaphoreType.DMA((count,)), pltpu.SemaphoreType.DMA((made,))]
        + [pltpu.VMEM(shape, kind) for shape, kind in scratch],
        compiler_params=pltpu.CompilerParams(vmem_limit_bytes=ALL_VMEM),
        cost_estimate=pl.CostEstimate(flops=flops, bytes_accessed=moved, transcendentals=0),
    )(*operands)


def place(index):
    return (index // 16) * 16 + (index % 4) * 4 + (index // 4) % 4


def rows(index, size):
    return pl.ds(pl.multiple_of(index * size, size), size)


def by_core(core_ref, body):
    @pl.when(core_ref[0] == 0)
    def _():
        body(0, HALF)

    @pl.when(core_ref[0] != 0)
    def _():
        body(HALF, 0)


def row_mean(values):
    return jnp.sum(values, -1, keepdims=True) * (1.0 / CH)


def standard(values):
    centred = values - row_mean(values)
    scale = lax.rsqrt(row_mean(centred * centred) + epsilon)
    return centred * scale, scale


def fold(values):
    return jnp.sum(values.reshape(-1, 8, values.shape[-1]), 0)


def block_forward(pre_ref, cp_ref, first, act_ref, unit_ref, slope_ref, scale_ref):
    offset, gain, shift = (cp_ref[first + i : first + i + 1] for i in range(3))

    def step(i, _):
        at = rows(i, STEP)
        unit, scale = standard(pre_ref[at, :] + offset)
        z = unit * gain + shift
        cdf = 0.5 + 0.5 * lax.erf(z * 0.7071067811865476)
        act_ref[at, :] = (z * cdf).astype(bf16)
        slope_ref[at, :] = cdf + z * (0.3989422804014327 * jnp.exp(-0.5 * z * z))
        unit_ref[at, :] = unit
        scale_ref[at, :] = jnp.broadcast_to(scale, (STEP, 128))
        return 0

    lax.fori_loop(0, pre_ref.shape[0] // STEP, step, 0, unroll=2)


def block_backward(grad_ref, cp_ref, first, unit_ref, slope_ref, scale_ref, out_ref):
    gain = cp_ref[first + 1 : first + 2]

    def step(i, sums):
        at = rows(i, STEP)
        unit = unit_ref[at, :]
        dz = grad_ref[at, :] * slope_ref[at, :]
        dunit = dz * gain
        du = scale_ref[at, :1] * (dunit - row_mean(dunit) - unit * row_mean(dunit * unit))
        out_ref[at, :] = du.astype(bf16)
        return (sums[0] + fold(du), sums[1] + fold(dz * unit), sums[2] + fold(dz))

    zero = jnp.zeros((8, CH), f32)
    return lax.fori_loop(0, grad_ref.shape[0] // STEP, step, (zero, zero, zero), unroll=2)


def total(values):
    return jnp.sum(values, 0, keepdims=True)


def spread(transposed):
    group = lax.broadcasted_iota(jnp.int32, (256, 256), 1 if transposed else 0)
    position = lax.broadcasted_iota(jnp.int32, (256, 256), 0 if transposed else 1)
    return (position == 8 * (group % 32) + group // 32).astype(bf16)


def pack_kernel(place_ref, ins, outs, scratch, need, give):
    w5_ref, w6_ref, w7_ref, wp_ref, cp_ref, bias_ref = ins
    (out_ref,) = outs
    (small_ref,) = scratch
    need(*ins)
    small_ref[...] = jnp.zeros((8, HALF), f32)
    small_ref[:, :11] = cp_ref[...].astype(f32)
    small_ref[:1, 128:158] = bias_ref[...].astype(f32)

    def body(at, _):
        tail = small_ref[...] if at == 0 else jnp.zeros((8, HALF), f32)
        first = jnp.concatenate([w5_ref[:, at : at + HALF].astype(f32), tail], 0).astype(bf16)
        parts = []
        for b in range(4):
            start = 4 * at + HALF * b
            part = wp_ref[:, start : min(start + HALF, WIDTH)].astype(f32)
            if start + HALF > WIDTH:
                part = jnp.concatenate([part, jnp.zeros((8, start + HALF - WIDTH), f32)], 1)
            parts.append(part)
        last = jnp.concatenate(parts, 0).astype(bf16)
        for k in range(4):
            out_ref[k, :32, :] = first
            out_ref[k, 32:48, :] = w6_ref[:, at : at + HALF]
            out_ref[k, 48:64, :] = w7_ref[:, at : at + HALF]
            out_ref[k, 64:, :] = last

    by_core(place_ref, body)


def split_kernel(place_ref, ins, outs, scratch, need, give):
    x_ref, next_ref, line_ref = ins
    even_ref, odd_ref, third_ref, spread_c_ref = outs
    (first_ref,) = scratch
    need(*ins)
    for k in range(16):
        spread_c_ref[k] = line_ref[:, 64:]
    give(spread_c_ref)
    matrix = spread(False)
    for j in range(4):
        groups = dot(matrix, x_ref[256 * j : 256 * j + 256, :])
        first_ref[32 * j : 32 * j + 32, :] = groups[:32]
        groups = groups.astype(bf16)
        for r in range(4):
            at = slice(128 * r + 32 * j, 128 * r + 32 * j + 32)
            even_ref[at, :] = groups[64 * r : 64 * r + 32]
            odd_ref[at, :] = groups[64 * r + 32 : 64 * r + 64]
            if r > 0:
                third_ref[128 * r - 128 + 32 * j : 128 * r - 96 + 32 * j, :] = groups[64 * r : 64 * r + 32]
    later = pltpu.roll(first_ref[...], 127, 0)
    last = lax.broadcasted_iota(jnp.int32, (128, CH), 0) == 127
    third_ref[384:512, :] = jnp.where(last, next_ref[:1, :].astype(f32), later).astype(bf16)


def forward_kernel(core_ref, ins, outs, scratch, need, give):
    mine_ref, other_ref, even_ref, odd_ref, third_ref, cot_ref = ins
    (
        cp_ref, w5_ref, five_ref, unit5_ref, slope5_ref, scale5_ref,
        w6_ref, w7_ref, act6_ref, unit6_ref, slope6_ref, scale6_ref, unit7_ref, slope7_ref, scale7_ref,
        normed_ref, unit_ref, scale_ref, give_ref, send_ref,
    ) = outs
    wide_ref, small_ref, pre5_ref, pre6_ref, pre7_ref, act7_ref, gp_ref = scratch
    need(mine_ref, other_ref)

    def unpack(mine_at, other_at):
        def step(i, _):
            to = place(i)
            for ref, at in ((mine_ref, mine_at), (other_ref, other_at)):
                block = ref[i, :32].astype(f32)
                wide_ref[rows(to, 24), at : at + HALF] = block[:24]
                if at == 0:
                    small_ref[rows(to, 8), :] = block[24:, :128]
                w6_ref[rows(to, 16), at : at + HALF] = ref[i, 32:48]
                w7_ref[rows(to, 16), at : at + HALF] = ref[i, 48:]
            return 0

        lax.fori_loop(0, 64, step, 0, unroll=4)

    by_core(core_ref, unpack)
    cp_ref[...] = small_ref[...].T[:16]

    def narrow(i, _):
        w5_ref[rows(i, 128), :] = wide_ref[rows(i, 128), :].astype(bf16)
        return 0

    lax.fori_loop(0, 12, narrow, 0)
    give(cp_ref, w5_ref, w6_ref, w7_ref)
    need(even_ref, odd_ref, third_ref)

    def multiply(r, _):
        at = rows(r, 128)
        pre5_ref[at, :] = (
            dot(even_ref[at, :], w5_ref[:512, :]) + dot(odd_ref[at, :], w5_ref[512:1024, :])
        ) + dot(third_ref[at, :], w5_ref[1024:, :])
        return 0

    lax.fori_loop(0, 4, multiply, 0)
    block_forward(pre5_ref, cp_ref, 0, five_ref, unit5_ref, slope5_ref, scale5_ref)
    give(five_ref, unit5_ref, slope5_ref, scale5_ref)
    for s in range(2):
        pre6_ref[128 * s : 128 * s + 128, :] = dot(five_ref[256 * s : 256 * s + 128, :], w6_ref[:512, :]) + dot(
            five_ref[256 * s + 128 : 256 * s + 256, :], w6_ref[512:, :]
        )
    block_forward(pre6_ref, cp_ref, 3, act6_ref, unit6_ref, slope6_ref, scale6_ref)
    pre7_ref[...] = dot(act6_ref[:128, :], w7_ref[:512, :]) + dot(act6_ref[128:, :], w7_ref[512:, :])
    block_forward(pre7_ref, cp_ref, 6, act7_ref, unit7_ref, slope7_ref, scale7_ref)

    unit, scale = standard(act7_ref[...].astype(f32))
    normed = (unit * cp_ref[9:10] + cp_ref[10:11]).astype(bf16)
    unit_ref[...] = unit
    scale_ref[...] = jnp.broadcast_to(scale, (128, 128))
    normed_ref[...] = normed
    flipped = normed.astype(f32).T.astype(bf16)
    give(act6_ref, unit6_ref, slope6_ref, scale6_ref, unit7_ref, slope7_ref, scale7_ref)
    need(cot_ref)
    for b in range(8):
        cols = slice(HALF * b, min(HALF * (b + 1), WIDTH))
        gp_ref[:, cols] = dot(flipped, cot_ref[:, cols])
    gp_ref[:, WIDTH:] = jnp.zeros((CH, 8 * HALF - WIDTH), f32)

    def pack(mine_at, other_at):
        def step(i, _):
            to = place(i)
            for ref, at in ((give_ref, mine_at), (send_ref, other_at)):
                block = gp_ref[rows(to, 8), 4 * at : 4 * at + 4 * HALF]
                parts = [block[:, HALF * b : HALF * (b + 1)] for b in range(4)]
                ref[i] = jnp.concatenate(parts, 0).astype(bf16)
            return 0

        lax.fori_loop(0, 64, step, 0, unroll=4)

    by_core(core_ref, pack)


def backward_kernel(core_ref, ins, outs, scratch, need, give):
    (
        mine_ref, other_ref, cp_ref, bias_ref, cot_ref, normed_ref, unit_ref, scale_ref,
        unit7_ref, slope7_ref, scale7_ref, w7_ref, act6_ref, unit6_ref, slope6_ref, scale6_ref, w6_ref, five_ref,
        unit5_ref, slope5_ref, scale5_ref, w5_ref, even_ref, odd_ref, third_ref, gb_ref,
    ) = ins
    out_ref, edge_ref, d5_ref, give_ref, send_ref = outs
    wp_ref, wide_ref, pre5_ref, pre6_ref, pre7_ref, g5_ref, g6_ref, g7_ref, d6_ref, d7_ref, small_ref, sums_ref = scratch
    need(mine_ref, other_ref)

    def unpack(mine_at, other_at):
        def step(i, _):
            to = place(i)
            for ref, at in ((mine_ref, mine_at), (other_ref, other_at)):
                block = ref[i].astype(f32)
                for b in range(4):
                    wide_ref[rows(to, 8), 4 * at + HALF * b : 4 * at + HALF * (b + 1)] = block[8 * b : 8 * b + 8]
            return 0

        lax.fori_loop(0, 64, step, 0, unroll=4)

    by_core(core_ref, unpack)

    def narrow(i, _):
        wp_ref[rows(i, 64), :] = wide_ref[rows(i, 64), :WIDTH].astype(bf16)
        return 0

    lax.fori_loop(0, 8, narrow, 0)
    need(cp_ref, bias_ref, cot_ref, normed_ref)

    normed_grad = jnp.zeros((128, CH), f32)
    for b in range(8):
        cols = slice(HALF * b, min(HALF * (b + 1), WIDTH))
        out_ref[:, cols] = (dot(normed_ref[...], wp_ref[:, cols]) + bias_ref[:, cols]).astype(bf16)
        normed_grad = normed_grad + dot(cot_ref[:, cols], wp_ref[:, cols], (1, 1))

    need(unit_ref, scale_ref, unit7_ref, slope7_ref, scale7_ref)
    give(out_ref)
    unit = unit_ref[...]
    dunit = normed_grad * cp_ref[9:10]
    sums_ref[...] = jnp.zeros((128, CH), f32)
    sums_ref[9:10, :] = total(normed_grad * unit)
    sums_ref[10:11, :] = total(normed_grad)
    pre7_ref[...] = scale_ref[:, :1] * (dunit - row_mean(dunit) - unit * row_mean(dunit * unit))

    for i, part in enumerate(block_backward(pre7_ref, cp_ref, 6, unit7_ref, slope7_ref, scale7_ref, d7_ref)):
        sums_ref[6 + i : 7 + i, :] = total(part)
    need(w7_ref, act6_ref)
    for s in range(2):
        half = slice(512 * s, 512 * s + 512)
        pre6_ref[128 * s : 128 * s + 128, :] = dot(d7_ref[...], w7_ref[half, :], (1, 1))
        g7_ref[half, :] = dot(act6_ref[128 * s : 128 * s + 128, :], d7_ref[...], (0, 0))
    need(unit6_ref, slope6_ref, scale6_ref)
    for i, part in enumerate(block_backward(pre6_ref, cp_ref, 3, unit6_ref, slope6_ref, scale6_ref, d6_ref)):
        sums_ref[3 + i : 4 + i, :] = total(part)
    need(w6_ref, five_ref)
    for r in range(2):
        half = slice(512 * r, 512 * r + 512)
        for s in range(2):
            at = 256 * s + 128 * r
            pre5_ref[at : at + 128, :] = dot(d6_ref[128 * s : 128 * s + 128, :], w6_ref[half, :], (1, 1))
        g6_ref[half, :] = dot(five_ref[128 * r : 128 * r + 128, :], d6_ref[:128, :], (0, 0)) + dot(
            five_ref[256 + 128 * r : 384 + 128 * r, :], d6_ref[128:, :], (0, 0)
        )
    need(unit5_ref, slope5_ref, scale5_ref)
    for i, part in enumerate(block_backward(pre5_ref, cp_ref, 0, unit5_ref, slope5_ref, scale5_ref, d5_ref)):
        sums_ref[i : i + 1, :] = total(part)
    need(*ins)
    give(d5_ref)
    edge_ref[...] = dot(d5_ref[496:512, :], w5_ref[1024:, :], (1, 1))[8:]
    for k, ref in enumerate((even_ref, odd_ref, third_ref)):
        g5_ref[512 * k : 512 * k + 512, :] = dot(ref[...], d5_ref[...], (0, 0))
    small_ref[...] = sums_ref[...].T

    def pack(mine_at, other_at):
        def step(i, _):
            to = place(i)
            for ref, at in ((give_ref, mine_at), (send_ref, other_at)):
                if at == 0:
                    tail = jnp.concatenate([small_ref[rows(to, 8), :], gb_ref[rows(to, 8), :]], 1)
                else:
                    tail = jnp.zeros((8, HALF), f32)
                block = jnp.concatenate([g5_ref[rows(to, 24), at : at + HALF], tail], 0)
                ref[i, :32, :] = block.astype(bf16)
                ref[i, 32:48, :] = g6_ref[rows(to, 16), at : at + HALF].astype(bf16)
                ref[i, 48:, :] = g7_ref[rows(to, 16), at : at + HALF].astype(bf16)
            return 0

        lax.fori_loop(0, 64, step, 0, unroll=4)

    by_core(core_ref, pack)


def input_kernel(place_ref, ins, outs, scratch, need, give):
    d_ref, w_ref, carried_ref = ins
    (out_ref,) = outs
    even_ref, odd_ref, third_ref = scratch
    need(*ins)

    def multiply(r, _):
        at = rows(r, 128)
        d = d_ref[at, :]
        even_ref[at, :] = dot(d, w_ref[:512, :], (1, 1))
        odd_ref[at, :] = dot(d, w_ref[512:1024, :], (1, 1))
        third_ref[at, :] = dot(d, w_ref[1024:, :], (1, 1))
        return 0

    lax.fori_loop(0, 4, multiply, 0)
    earlier = pltpu.roll(third_ref[384:512, :], 1, 0)
    first = lax.broadcasted_iota(jnp.int32, (128, CH), 0) == 0
    even_ref[:128, :] += jnp.where(first, carried_ref[...], earlier)
    even_ref[128:, :] += third_ref[:384, :]
    matrix = spread(True)
    for j in range(4):
        parts = []
        for r in range(4):
            at = slice(128 * r + 32 * j, 128 * r + 32 * j + 32)
            parts += [even_ref[at, :].astype(bf16), odd_ref[at, :].astype(bf16)]
        out_ref[256 * j : 256 * j + 256, :] = dot(matrix, jnp.concatenate(parts, 0)).astype(bf16)


def swap_cores(value):
    return lax.ppermute(value, "core", [(0, 1), (1, 0)])


def together(*values):
    return lax.optimization_barrier(values)


def around(value, axis, size, back):
    return lax.ppermute(value, axis, [(i, (i + back) % size) for i in range(size)])


def across_plane(value, *meanwhile):
    return together(lax.all_to_all(value, ("x", "y"), 0, 0, tiled=True), *meanwhile)


def sum_cores(give, send):
    return (give.astype(f32) + swap_cores(send).astype(f32)).astype(bf16)


def sum_plane(plane):
    return jnp.sum(plane.astype(f32), 0).astype(bf16)


def sum_line(value):
    count = value.shape[1]
    line = jnp.broadcast_to(value[:, None], (4, 4, count, HALF)).reshape(16, count, HALF)
    line = lax.all_to_all(line, ("zh", "zl", "core"), 0, 0, tiled=True)
    return jnp.sum(line.reshape(8, 2, count, HALF).astype(f32), 0)


def sum_line_by_permutes(value, core):
    zh = lax.axis_index("zh")
    pick = lambda k: lax.dynamic_index_in_dim(value, (zh + k) % 4, 0, False)
    parts = [pick(0)] + [around(pick(k), "zh", 4, k) for k in range(1, 4)]
    summed = sum(part.astype(f32) for part in parts)
    summed = summed + lax.ppermute(summed, "zl", [(0, 1), (1, 0)])
    other = swap_cores(summed)
    return jnp.stack([jnp.where(core == 0, summed, other), jnp.where(core == 0, other, summed)])


def proj_rows(halves):
    return halves.reshape(2, 4, 8, HALF).transpose(2, 0, 1, 3).reshape(8, 8 * HALF)[:, :WIDTH]


def shards(features, w_five, w_six, w_seven, channel_params, w_proj, proj_bias, out_cotangent):
    core = lax.axis_index("core")
    place_at = core.astype(jnp.int32).reshape(1)
    inputs, cotangent = features[0], out_cotangent[0]
    square, flat, stack = (512, CH), (512, 128), (64, 32, HALF)

    (packed,) = staged(
        pack_kernel,
        (place_at, w_five, w_six, w_seven, w_proj, channel_params, proj_bias.reshape(1, 30)),
        [((4, 96, HALF), bf16)],
        [((8, HALF), f32)],
        flops=0,
        moved=2**18,
    )
    line = lax.all_to_all(packed, "zh", 0, 0, tiled=True)
    spread_ab = jnp.broadcast_to(line[None, :, :64], (16, 4, 64, HALF))

    line, first_rows, late_cotangent = together(line, inputs[:16], cotangent)
    next_row = lax.ppermute(first_rows, ("zl", "core"), [(1, 0), (2, 1), (3, 2)])
    even, odd, third, spread_c = staged(
        split_kernel,
        (place_at, inputs, next_row, line),
        [(square, bf16)] * 3 + [((16, 4, 32, HALF), bf16)],
        [((128, CH), f32)],
        flops=2**28,
        moved=3 * 2**20,
    )
    grad_bias = jnp.sum(late_cotangent.astype(f32), 0).reshape(64, 1, 30)
    grad_bias = jnp.pad(grad_bias, [(0, 0), (0, 7), (0, 98)]).reshape(512, 128)

    mine_ab, spread_c, even, odd, third, grad_bias = across_plane(spread_ab, spread_c, even, odd, third, grad_bias)
    mine_ab = mine_ab.reshape(64, 64, HALF)
    other_ab = swap_cores(mine_ab)
    bias = jnp.where(core == 0, mine_ab[:, 24, 128:158], other_ab[:, 24, 128:158])
    bias = bias.reshape(4, 4, 4, 30).transpose(0, 2, 1, 3).reshape(1, WIDTH).astype(f32)

    saved = lambda n: [((n, CH), f32), ((n, CH), f32), ((n, 128), f32)]
    pair = lambda n: [((64, n, HALF), bf16)] * 2
    w_shapes = [((1536, CH), bf16), ((1024, CH), bf16), ((1024, CH), bf16)]
    cp, w5, act_five, *saved_five, w6, w7, act_six, u6, s6, r6, u7, s7, r7, normed, unit, scale, give_c, send_c = staged(
        forward_kernel,
        (place_at, mine_ab, other_ab, even, odd, third, cotangent),
        [((16, CH), f32), w_shapes[0], (square, bf16)]
        + saved(512)
        + w_shapes[1:]
        + [((256, CH), bf16)]
        + saved(256)
        + saved(128)
        + [((128, CH), bf16), ((128, CH), f32), ((128, 128), f32)]
        + pair(32),
        [((1536, CH), f32), (flat, f32), (square, f32), ((256, CH), f32), ((128, CH), f32), ((128, CH), bf16)]
        + [((CH, 8 * HALF), f32)],
        flops=2**31,
        moved=16 * 2**20,
    )

    mine_c, give_c, send_c = across_plane(spread_c, give_c, send_c)
    mine_c = mine_c.reshape(stack)
    other_c = swap_cores(mine_c)
    mine_c, cores_c = together(mine_c, sum_cores(give_c, send_c))
    projected, edge, d_five, give_ab, send_ab = staged(
        backward_kernel,
        (place_at, mine_c, other_c, cp, bias, cotangent, normed, unit, scale, u7, s7, r7, w7, act_six)
        + (u6, s6, r6, w6, act_five, *saved_five, w5, even, odd, third, grad_bias),
        [((128, WIDTH), bf16), ((8, CH), f32), (square, bf16)] + pair(64),
        [((CH, WIDTH), bf16), ((CH, 8 * HALF), f32), (square, f32), ((256, CH), f32), ((128, CH), f32)]
        + [((1536, CH), f32), ((1024, CH), f32), ((1024, CH), f32), ((256, CH), bf16), ((128, CH), bf16)]
        + [(flat, f32), ((128, CH), f32)],
        flops=2**31,
        moved=16 * 2**20,
    )

    plane_c, give_ab, send_ab = across_plane(cores_c.reshape(16, 4, 32, HALF), give_ab, send_ab)
    cores_ab, plane_c, d_five = together(sum_cores(give_ab, send_ab), plane_c, d_five)
    carried = lax.ppermute(edge[7:8], ("zl", "core"), [(0, 1), (1, 2), (2, 3)])
    (input_grad,) = staged(
        input_kernel,
        (place_at, d_five, w5, carried),
        [((1024, CH), bf16)],
        [(square, f32)] * 3,
        flops=2**30,
        moved=4 * 2**20,
    )
    sum_c = sum_line_by_permutes(sum_plane(plane_c), core)
    plane_ab, sum_c, input_grad = across_plane(cores_ab.reshape(16, 4, 64, HALF), sum_c, input_grad)
    sum_ab = sum_line(sum_plane(plane_ab))

    joined = lambda halves: jnp.concatenate([halves[0], halves[1]], 1)
    return (
        projected[None],
        input_grad[None],
        joined(sum_ab[:, :24]),
        joined(sum_ab[:, 32:48]),
        joined(sum_ab[:, 48:]),
        sum_ab[0, 24:32, :11],
        proj_rows(sum_c),
        sum_ab[0, 24, 128:158],
    )


def solution(mesh):
    fine = Mesh(mesh.devices.reshape(4, 4, 4, 2, 2), ("x", "zh", "y", "zl", "core"))
    dp, seq = ("x", "zh", "y"), ("zl", "core")
    placed = (
        P(dp, seq, None),
        P(dp, None),
        P(dp, None),
        P(dp, None),
        P(dp, None),
        P(dp, None),
        P(dp),
        P(dp, seq, None),
    )
    return jax.shard_map(
        shards,
        mesh=fine,
        in_specs=placed,
        out_specs=(
            P(dp, seq, None),
            P(dp, seq, None),
            P(dp, None),
            P(dp, None),
            P(dp, None),
            P(dp, None),
            P(dp, None),
            P(dp),
        ),
        check_vma=False,
    )
```

```python
import jax
import jax.numpy as jnp
from jax import lax
from jax.experimental import pallas as pl
from jax.experimental.pallas import tpu as pltpu
from jax.sharding import Mesh, PartitionSpec as P

epsilon = 1e-05
f32 = jnp.float32
bf16 = jnp.bfloat16
CH = 512
WIDTH = 1920
HALF = 256
STEP = 32
ALL_VMEM = 2**26 - 2**18


def dot(left, right, contract=(1, 0)):
    return lax.dot_general(
        left, right, (((contract[0],), (contract[1],)), ((), ())), preferred_element_type=f32
    )


def staged(body, operands, outs, scratch, flops, moved):
    count, made = len(operands) - 1, len(outs)

    def kernel(place_ref, *refs):
        refs = list(refs)
        groups = []
        for size in (count, made, count, made):
            groups.append(refs[:size])
            refs = refs[size:]
        from_hbm, to_hbm, ins, results = groups
        in_sems, out_sems, *rest = refs
        loads = [pltpu.make_async_copy(a, b, in_sems.at[i]) for i, (a, b) in enumerate(zip(from_hbm, ins))]
        stores = [pltpu.make_async_copy(a, b, out_sems.at[i]) for i, (a, b) in enumerate(zip(results, to_hbm))]
        for load in loads:
            load.start()
        waited, sent = set(), set()

        def need(*which):
            for ref in which:
                index = next(i for i, own in enumerate(ins) if own is ref)
                if index not in waited:
                    waited.add(index)
                    loads[index].wait()

        def give(*which):
            for ref in which:
                index = next(i for i, own in enumerate(results) if own is ref)
                if index not in sent:
                    sent.add(index)
                    stores[index].start()

        body(place_ref, ins, results, rest, need, give)
        need(*ins)
        give(*results)
        for store in stores:
            store.wait()

    hbm = pl.BlockSpec(memory_space=pltpu.HBM)
    return pl.pallas_call(
        kernel,
        out_shape=[jax.ShapeDtypeStruct(shape, kind) for shape, kind in outs],
        in_specs=[pl.BlockSpec(memory_space=pltpu.SMEM)] + [hbm] * count,
        out_specs=[hbm] * made,
        scratch_shapes=[pltpu.VMEM(array.shape, array.dtype) for array in operands[1:]]
        + [pltpu.VMEM(shape, kind) for shape, kind in outs]
        + [pltpu.SemaphoreType.DMA((count,)), pltpu.SemaphoreType.DMA((made,))]
        + [pltpu.VMEM(shape, kind) for shape, kind in scratch],
        compiler_params=pltpu.CompilerParams(vmem_limit_bytes=ALL_VMEM),
        cost_estimate=pl.CostEstimate(flops=flops, bytes_accessed=moved, transcendentals=0),
    )(*operands)


def place(index):
    return (index // 16) * 16 + (index % 4) * 4 + (index // 4) % 4


def rows(index, size):
    return pl.ds(pl.multiple_of(index * size, size), size)


def by_core(core_ref, body):
    @pl.when(core_ref[0] == 0)
    def _():
        body(0, HALF)

    @pl.when(core_ref[0] != 0)
    def _():
        body(HALF, 0)


def row_mean(values):
    return jnp.sum(values, -1, keepdims=True) * (1.0 / CH)


def standard(values):
    centred = values - row_mean(values)
    scale = lax.rsqrt(row_mean(centred * centred) + epsilon)
    return centred * scale, scale


def fold(values):
    return jnp.sum(values.reshape(-1, 8, values.shape[-1]), 0)


def block_forward(pre_ref, cp_ref, first, act_ref, unit_ref, slope_ref, scale_ref):
    offset, gain, shift = (cp_ref[first + i : first + i + 1] for i in range(3))

    def step(i, _):
        at = rows(i, STEP)
        unit, scale = standard(pre_ref[at, :] + offset)
        z = unit * gain + shift
        cdf = 0.5 + 0.5 * lax.erf(z * 0.7071067811865476)
        act_ref[at, :] = (z * cdf).astype(bf16)
        slope_ref[at, :] = cdf + z * (0.3989422804014327 * jnp.exp(-0.5 * z * z))
        unit_ref[at, :] = unit
        scale_ref[at, :] = jnp.broadcast_to(scale, (STEP, 128))
        return 0

    lax.fori_loop(0, pre_ref.shape[0] // STEP, step, 0, unroll=2)


def block_backward(grad_ref, cp_ref, first, unit_ref, slope_ref, scale_ref, out_ref):
    gain = cp_ref[first + 1 : first + 2]

    def step(i, sums):
        at = rows(i, STEP)
        unit = unit_ref[at, :]
        dz = grad_ref[at, :] * slope_ref[at, :]
        dunit = dz * gain
        du = scale_ref[at, :1] * (dunit - row_mean(dunit) - unit * row_mean(dunit * unit))
        out_ref[at, :] = du.astype(bf16)
        return (sums[0] + fold(du), sums[1] + fold(dz * unit), sums[2] + fold(dz))

    zero = jnp.zeros((8, CH), f32)
    return lax.fori_loop(0, grad_ref.shape[0] // STEP, step, (zero, zero, zero), unroll=2)


def total(values):
    return jnp.sum(values, 0, keepdims=True)


def spread(transposed):
    group = lax.broadcasted_iota(jnp.int32, (256, 256), 1 if transposed else 0)
    position = lax.broadcasted_iota(jnp.int32, (256, 256), 0 if transposed else 1)
    return (position == 8 * (group % 32) + group // 32).astype(bf16)


def pack_kernel(place_ref, ins, outs, scratch, need, give):
    w5_ref, w6_ref, w7_ref, wp_ref, cp_ref, bias_ref = ins
    (out_ref,) = outs
    (small_ref,) = scratch
    need(*ins)
    small_ref[...] = jnp.zeros((8, HALF), f32)
    small_ref[:, :11] = cp_ref[...].astype(f32)
    small_ref[:1, 128:158] = bias_ref[...].astype(f32)

    def body(at, _):
        tail = small_ref[...] if at == 0 else jnp.zeros((8, HALF), f32)
        first = jnp.concatenate([w5_ref[:, at : at + HALF].astype(f32), tail], 0).astype(bf16)
        parts = []
        for b in range(4):
            start = 4 * at + HALF * b
            part = wp_ref[:, start : min(start + HALF, WIDTH)].astype(f32)
            if start + HALF > WIDTH:
                part = jnp.concatenate([part, jnp.zeros((8, start + HALF - WIDTH), f32)], 1)
            parts.append(part)
        last = jnp.concatenate(parts, 0).astype(bf16)
        for k in range(4):
            out_ref[k, :32, :] = first
            out_ref[k, 32:48, :] = w6_ref[:, at : at + HALF]
            out_ref[k, 48:64, :] = w7_ref[:, at : at + HALF]
            out_ref[k, 64:, :] = last

    by_core(place_ref, body)


def split_kernel(place_ref, ins, outs, scratch, need, give):
    x_ref, next_ref, line_ref = ins
    even_ref, odd_ref, third_ref, spread_c_ref = outs
    (first_ref,) = scratch
    need(*ins)
    for k in range(16):
        spread_c_ref[k] = line_ref[:, 64:]
    give(spread_c_ref)
    matrix = spread(False)
    for j in range(4):
        groups = dot(matrix, x_ref[256 * j : 256 * j + 256, :])
        first_ref[32 * j : 32 * j + 32, :] = groups[:32]
        groups = groups.astype(bf16)
        for r in range(4):
            at = slice(128 * r + 32 * j, 128 * r + 32 * j + 32)
            even_ref[at, :] = groups[64 * r : 64 * r + 32]
            odd_ref[at, :] = groups[64 * r + 32 : 64 * r + 64]
            if r > 0:
                third_ref[128 * r - 128 + 32 * j : 128 * r - 96 + 32 * j, :] = groups[64 * r : 64 * r + 32]
    later = pltpu.roll(first_ref[...], 127, 0)
    last = lax.broadcasted_iota(jnp.int32, (128, CH), 0) == 127
    third_ref[384:512, :] = jnp.where(last, next_ref[:1, :].astype(f32), later).astype(bf16)


def forward_kernel(core_ref, ins, outs, scratch, need, give):
    mine_ref, other_ref, even_ref, odd_ref, third_ref, cot_ref = ins
    (
        cp_ref, w5_ref, five_ref, unit5_ref, slope5_ref, scale5_ref,
        w6_ref, w7_ref, act6_ref, unit6_ref, slope6_ref, scale6_ref, unit7_ref, slope7_ref, scale7_ref,
        normed_ref, unit_ref, scale_ref, give_ref, send_ref,
    ) = outs
    wide_ref, small_ref, pre5_ref, pre6_ref, pre7_ref, act7_ref, gp_ref = scratch
    need(mine_ref, other_ref)

    def unpack(mine_at, other_at):
        def step(i, _):
            to = place(i)
            for ref, at in ((mine_ref, mine_at), (other_ref, other_at)):
                block = ref[i, :32].astype(f32)
                wide_ref[rows(to, 24), at : at + HALF] = block[:24]
                if at == 0:
                    small_ref[rows(to, 8), :] = block[24:, :128]
                w6_ref[rows(to, 16), at : at + HALF] = ref[i, 32:48]
                w7_ref[rows(to, 16), at : at + HALF] = ref[i, 48:]
            return 0

        lax.fori_loop(0, 64, step, 0, unroll=4)

    by_core(core_ref, unpack)
    cp_ref[...] = small_ref[...].T[:16]

    def narrow(i, _):
        w5_ref[rows(i, 128), :] = wide_ref[rows(i, 128), :].astype(bf16)
        return 0

    lax.fori_loop(0, 12, narrow, 0)
    give(cp_ref, w5_ref, w6_ref, w7_ref)
    need(even_ref, odd_ref, third_ref)

    def multiply(r, _):
        at = rows(r, 128)
        pre5_ref[at, :] = (
            dot(even_ref[at, :], w5_ref[:512, :]) + dot(odd_ref[at, :], w5_ref[512:1024, :])
        ) + dot(third_ref[at, :], w5_ref[1024:, :])
        return 0

    lax.fori_loop(0, 4, multiply, 0)
    block_forward(pre5_ref, cp_ref, 0, five_ref, unit5_ref, slope5_ref, scale5_ref)
    give(five_ref, unit5_ref, slope5_ref, scale5_ref)
    for s in range(2):
        pre6_ref[128 * s : 128 * s + 128, :] = dot(five_ref[256 * s : 256 * s + 128, :], w6_ref[:512, :]) + dot(
            five_ref[256 * s + 128 : 256 * s + 256, :], w6_ref[512:, :]
        )
    block_forward(pre6_ref, cp_ref, 3, act6_ref, unit6_ref, slope6_ref, scale6_ref)
    pre7_ref[...] = dot(act6_ref[:128, :], w7_ref[:512, :]) + dot(act6_ref[128:, :], w7_ref[512:, :])
    block_forward(pre7_ref, cp_ref, 6, act7_ref, unit7_ref, slope7_ref, scale7_ref)

    unit, scale = standard(act7_ref[...].astype(f32))
    normed = (unit * cp_ref[9:10] + cp_ref[10:11]).astype(bf16)
    unit_ref[...] = unit
    scale_ref[...] = jnp.broadcast_to(scale, (128, 128))
    normed_ref[...] = normed
    flipped = normed.astype(f32).T.astype(bf16)
    give(act6_ref, unit6_ref, slope6_ref, scale6_ref, unit7_ref, slope7_ref, scale7_ref)
    need(cot_ref)
    for b in range(8):
        cols = slice(HALF * b, min(HALF * (b + 1), WIDTH))
        gp_ref[:, cols] = dot(flipped, cot_ref[:, cols])
    gp_ref[:, WIDTH:] = jnp.zeros((CH, 8 * HALF - WIDTH), f32)

    def pack(mine_at, other_at):
        def step(i, _):
            to = place(i)
            for ref, at in ((give_ref, mine_at), (send_ref, other_at)):
                block = gp_ref[rows(to, 8), 4 * at : 4 * at + 4 * HALF]
                parts = [block[:, HALF * b : HALF * (b + 1)] for b in range(4)]
                ref[i] = jnp.concatenate(parts, 0).astype(bf16)
            return 0

        lax.fori_loop(0, 64, step, 0, unroll=4)

    by_core(core_ref, pack)


def backward_kernel(core_ref, ins, outs, scratch, need, give):
    (
        mine_ref, other_ref, cp_ref, bias_ref, cot_ref, normed_ref, unit_ref, scale_ref,
        unit7_ref, slope7_ref, scale7_ref, w7_ref, act6_ref, unit6_ref, slope6_ref, scale6_ref, w6_ref, five_ref,
        unit5_ref, slope5_ref, scale5_ref, w5_ref, even_ref, odd_ref, third_ref, gb_ref,
    ) = ins
    out_ref, edge_ref, d5_ref, give_ref, send_ref = outs
    wp_ref, wide_ref, pre5_ref, pre6_ref, pre7_ref, g5_ref, g6_ref, g7_ref, d6_ref, d7_ref, small_ref, sums_ref = scratch
    need(mine_ref, other_ref)

    def unpack(mine_at, other_at):
        def step(i, _):
            to = place(i)
            for ref, at in ((mine_ref, mine_at), (other_ref, other_at)):
                block = ref[i].astype(f32)
                for b in range(4):
                    wide_ref[rows(to, 8), 4 * at + HALF * b : 4 * at + HALF * (b + 1)] = block[8 * b : 8 * b + 8]
            return 0

        lax.fori_loop(0, 64, step, 0, unroll=4)

    by_core(core_ref, unpack)

    def narrow(i, _):
        wp_ref[rows(i, 64), :] = wide_ref[rows(i, 64), :WIDTH].astype(bf16)
        return 0

    lax.fori_loop(0, 8, narrow, 0)
    need(cp_ref, bias_ref, cot_ref, normed_ref)

    normed_grad = jnp.zeros((128, CH), f32)
    for b in range(8):
        cols = slice(HALF * b, min(HALF * (b + 1), WIDTH))
        out_ref[:, cols] = (dot(normed_ref[...], wp_ref[:, cols]) + bias_ref[:, cols]).astype(bf16)
        normed_grad = normed_grad + dot(cot_ref[:, cols], wp_ref[:, cols], (1, 1))

    need(unit_ref, scale_ref, unit7_ref, slope7_ref, scale7_ref)
    give(out_ref)
    unit = unit_ref[...]
    dunit = normed_grad * cp_ref[9:10]
    sums_ref[...] = jnp.zeros((128, CH), f32)
    sums_ref[9:10, :] = total(normed_grad * unit)
    sums_ref[10:11, :] = total(normed_grad)
    pre7_ref[...] = scale_ref[:, :1] * (dunit - row_mean(dunit) - unit * row_mean(dunit * unit))

    for i, part in enumerate(block_backward(pre7_ref, cp_ref, 6, unit7_ref, slope7_ref, scale7_ref, d7_ref)):
        sums_ref[6 + i : 7 + i, :] = total(part)
    need(w7_ref, act6_ref)
    for s in range(2):
        half = slice(512 * s, 512 * s + 512)
        pre6_ref[128 * s : 128 * s + 128, :] = dot(d7_ref[...], w7_ref[half, :], (1, 1))
        g7_ref[half, :] = dot(act6_ref[128 * s : 128 * s + 128, :], d7_ref[...], (0, 0))
    need(unit6_ref, slope6_ref, scale6_ref)
    for i, part in enumerate(block_backward(pre6_ref, cp_ref, 3, unit6_ref, slope6_ref, scale6_ref, d6_ref)):
        sums_ref[3 + i : 4 + i, :] = total(part)
    need(w6_ref, five_ref)
    for r in range(2):
        half = slice(512 * r, 512 * r + 512)
        for s in range(2):
            at = 256 * s + 128 * r
            pre5_ref[at : at + 128, :] = dot(d6_ref[128 * s : 128 * s + 128, :], w6_ref[half, :], (1, 1))
        g6_ref[half, :] = dot(five_ref[128 * r : 128 * r + 128, :], d6_ref[:128, :], (0, 0)) + dot(
            five_ref[256 + 128 * r : 384 + 128 * r, :], d6_ref[128:, :], (0, 0)
        )
    need(unit5_ref, slope5_ref, scale5_ref)
    for i, part in enumerate(block_backward(pre5_ref, cp_ref, 0, unit5_ref, slope5_ref, scale5_ref, d5_ref)):
        sums_ref[i : i + 1, :] = total(part)
    need(*ins)
    give(d5_ref)
    edge_ref[...] = dot(d5_ref[496:512, :], w5_ref[1024:, :], (1, 1))[8:]
    for k, ref in enumerate((even_ref, odd_ref, third_ref)):
        g5_ref[512 * k : 512 * k + 512, :] = dot(ref[...], d5_ref[...], (0, 0))
    small_ref[...] = sums_ref[...].T

    def pack(mine_at, other_at):
        def step(i, _):
            to = place(i)
            for ref, at in ((give_ref, mine_at), (send_ref, other_at)):
                if at == 0:
                    tail = jnp.concatenate([small_ref[rows(to, 8), :], gb_ref[rows(to, 8), :]], 1)
                else:
                    tail = jnp.zeros((8, HALF), f32)
                block = jnp.concatenate([g5_ref[rows(to, 24), at : at + HALF], tail], 0)
                ref[i, :32, :] = block.astype(bf16)
                ref[i, 32:48, :] = g6_ref[rows(to, 16), at : at + HALF].astype(bf16)
                ref[i, 48:, :] = g7_ref[rows(to, 16), at : at + HALF].astype(bf16)
            return 0

        lax.fori_loop(0, 64, step, 0, unroll=4)

    by_core(core_ref, pack)


def input_kernel(place_ref, ins, outs, scratch, need, give):
    d_ref, w_ref, carried_ref = ins
    (out_ref,) = outs
    even_ref, odd_ref, third_ref = scratch
    need(*ins)

    def multiply(r, _):
        at = rows(r, 128)
        d = d_ref[at, :]
        even_ref[at, :] = dot(d, w_ref[:512, :], (1, 1))
        odd_ref[at, :] = dot(d, w_ref[512:1024, :], (1, 1))
        third_ref[at, :] = dot(d, w_ref[1024:, :], (1, 1))
        return 0

    lax.fori_loop(0, 4, multiply, 0)
    earlier = pltpu.roll(third_ref[384:512, :], 1, 0)
    first = lax.broadcasted_iota(jnp.int32, (128, CH), 0) == 0
    even_ref[:128, :] += jnp.where(first, carried_ref[...], earlier)
    even_ref[128:, :] += third_ref[:384, :]
    matrix = spread(True)
    for j in range(4):
        parts = []
        for r in range(4):
            at = slice(128 * r + 32 * j, 128 * r + 32 * j + 32)
            parts += [even_ref[at, :].astype(bf16), odd_ref[at, :].astype(bf16)]
        out_ref[256 * j : 256 * j + 256, :] = dot(matrix, jnp.concatenate(parts, 0)).astype(bf16)


def finish_kernel(core_ref, ins, outs, scratch, need, give):
    mine_ref, other_ref = ins
    g5_ref, g6_ref, g7_ref, channel_ref, bias_ref = outs
    need(*ins)

    def body(mine_at, other_at):
        for ref, at in ((mine_ref, mine_at), (other_ref, other_at)):
            g5_ref[:, at : at + HALF] = ref[:24, :]
            g6_ref[:, at : at + HALF] = ref[32:48, :]
            g7_ref[:, at : at + HALF] = ref[48:, :]
            if at == 0:
                channel_ref[...] = ref[24:32, :11]
                bias_ref[...] = ref[24:25, 128:158]

    by_core(core_ref, body)


def swap_cores(value):
    return lax.ppermute(value, "core", [(0, 1), (1, 0)])


def together(*values):
    return lax.optimization_barrier(values)


def around(value, axis, size, back):
    return lax.ppermute(value, axis, [(i, (i + back) % size) for i in range(size)])


def across_plane(value, *meanwhile):
    return together(lax.all_to_all(value, ("x", "y"), 0, 0, tiled=True), *meanwhile)


def add_kernel(a_ref, b_ref, out_ref, a, b, both, a_sems, b_sems, out_sems):
    size = a_ref.shape[0] // 4
    parts = [pl.ds(size * k, size) for k in range(4)]
    loads = []
    for k, part in enumerate(parts):
        loads.append(pltpu.make_async_copy(a_ref.at[part], a.at[part], a_sems.at[k]))
        loads.append(pltpu.make_async_copy(b_ref.at[part], b.at[part], b_sems.at[k]))
    stores = [pltpu.make_async_copy(both.at[part], out_ref.at[part], out_sems.at[k]) for k, part in enumerate(parts)]
    for load in loads:
        load.start()
    for k, store in enumerate(stores):
        loads[2 * k].wait()
        loads[2 * k + 1].wait()

        def step(i, _, k=k):
            at = size * k + i
            both[at] = (a[at].astype(f32) + b[at].astype(f32)).astype(bf16)
            return 0

        lax.fori_loop(0, size, step, 0, unroll=4)
        store.start()
    for store in stores:
        store.wait()


def sum_cores(give, send):
    hbm = pl.BlockSpec(memory_space=pltpu.HBM)
    return pl.pallas_call(
        add_kernel,
        out_shape=jax.ShapeDtypeStruct(give.shape, bf16),
        in_specs=[hbm, hbm],
        out_specs=hbm,
        scratch_shapes=[pltpu.VMEM(give.shape, bf16)] * 3 + [pltpu.SemaphoreType.DMA((4,))] * 3,
        compiler_params=pltpu.CompilerParams(vmem_limit_bytes=ALL_VMEM),
        cost_estimate=pl.CostEstimate(flops=2**20, bytes_accessed=6 * 2**20, transcendentals=0),
    )(give, swap_cores(send))


def sum_plane(plane):
    return jnp.sum(plane.astype(f32), 0).astype(bf16)


def both_halves(summed, core):
    other = swap_cores(summed)
    return jnp.stack([jnp.where(core == 0, summed, other), jnp.where(core == 0, other, summed)])


def sum_line(value):
    count = value.shape[1]
    line = jnp.broadcast_to(value[:, None], (4, 2, count, HALF)).reshape(8, count, HALF)
    line = lax.all_to_all(line, ("zh", "zl"), 0, 0, tiled=True)
    return jnp.sum(line.astype(f32), 0)


def sum_line_by_permutes(value, core):
    zh = lax.axis_index("zh")
    pick = lambda k: lax.dynamic_index_in_dim(value, (zh + k) % 4, 0, False)
    parts = [pick(0)] + [around(pick(k), "zh", 4, k) for k in range(1, 4)]
    summed = sum(part.astype(f32) for part in parts)
    summed = summed + lax.ppermute(summed, "zl", [(0, 1), (1, 0)])
    return both_halves(summed, core)


def proj_rows(halves):
    return halves.reshape(2, 4, 8, HALF).transpose(2, 0, 1, 3).reshape(8, 8 * HALF)[:, :WIDTH]


def shards(features, w_five, w_six, w_seven, channel_params, w_proj, proj_bias, out_cotangent):
    core = lax.axis_index("core")
    place_at = core.astype(jnp.int32).reshape(1)
    inputs, cotangent = features[0], out_cotangent[0]
    square, flat, stack = (512, CH), (512, 128), (64, 32, HALF)

    (packed,) = staged(
        pack_kernel,
        (place_at, w_five, w_six, w_seven, w_proj, channel_params, proj_bias.reshape(1, 30)),
        [((4, 96, HALF), bf16)],
        [((8, HALF), f32)],
        flops=0,
        moved=2**18,
    )
    line = lax.all_to_all(packed, "zh", 0, 0, tiled=True)
    spread_ab = jnp.broadcast_to(line[None, :, :64], (16, 4, 64, HALF))

    line, first_rows, late_cotangent = together(line, inputs[:16], cotangent)
    next_row = lax.ppermute(first_rows, ("zl", "core"), [(1, 0), (2, 1), (3, 2)])
    even, odd, third, spread_c = staged(
        split_kernel,
        (place_at, inputs, next_row, line),
        [(square, bf16)] * 3 + [((16, 4, 32, HALF), bf16)],
        [((128, CH), f32)],
        flops=2**28,
        moved=3 * 2**20,
    )
    grad_bias = jnp.sum(late_cotangent.astype(f32), 0).reshape(64, 1, 30)
    grad_bias = jnp.pad(grad_bias, [(0, 0), (0, 7), (0, 98)]).reshape(512, 128)

    mine_ab, spread_c, even, odd, third, grad_bias = across_plane(spread_ab, spread_c, even, odd, third, grad_bias)
    mine_ab = mine_ab.reshape(64, 64, HALF)
    other_ab = swap_cores(mine_ab)
    bias = jnp.where(core == 0, mine_ab[:, 24, 128:158], other_ab[:, 24, 128:158])
    bias = bias.reshape(4, 4, 4, 30).transpose(0, 2, 1, 3).reshape(1, WIDTH).astype(f32)

    saved = lambda n: [((n, CH), f32), ((n, CH), f32), ((n, 128), f32)]
    pair = lambda n: [((64, n, HALF), bf16)] * 2
    w_shapes = [((1536, CH), bf16), ((1024, CH), bf16), ((1024, CH), bf16)]
    cp, w5, act_five, *saved_five, w6, w7, act_six, u6, s6, r6, u7, s7, r7, normed, unit, scale, give_c, send_c = staged(
        forward_kernel,
        (place_at, mine_ab, other_ab, even, odd, third, cotangent),
        [((16, CH), f32), w_shapes[0], (square, bf16)]
        + saved(512)
        + w_shapes[1:]
        + [((256, CH), bf16)]
        + saved(256)
        + saved(128)
        + [((128, CH), bf16), ((128, CH), f32), ((128, 128), f32)]
        + pair(32),
        [((1536, CH), f32), (flat, f32), (square, f32), ((256, CH), f32), ((128, CH), f32), ((128, CH), bf16)]
        + [((CH, 8 * HALF), f32)],
        flops=2**31,
        moved=16 * 2**20,
    )

    (mine_c,) = across_plane(spread_c)
    mine_c = mine_c.reshape(stack)
    other_c = swap_cores(mine_c)
    mine_c, cores_c = together(mine_c, sum_cores(give_c, send_c))
    projected, edge, d_five, give_ab, send_ab = staged(
        backward_kernel,
        (place_at, mine_c, other_c, cp, bias, cotangent, normed, unit, scale, u7, s7, r7, w7, act_six)
        + (u6, s6, r6, w6, act_five, *saved_five, w5, even, odd, third, grad_bias),
        [((128, WIDTH), bf16), ((8, CH), f32), (square, bf16)] + pair(64),
        [((CH, WIDTH), bf16), ((CH, 8 * HALF), f32), (square, f32), ((256, CH), f32), ((128, CH), f32)]
        + [((1536, CH), f32), ((1024, CH), f32), ((1024, CH), f32), ((256, CH), bf16), ((128, CH), bf16)]
        + [(flat, f32), ((128, CH), f32)],
        flops=2**31,
        moved=16 * 2**20,
    )

    plane_c, give_ab, send_ab = across_plane(cores_c.reshape(16, 4, 32, HALF), give_ab, send_ab)
    cores_ab, plane_c, d_five = together(sum_cores(give_ab, send_ab), plane_c, d_five)
    carried = lax.ppermute(edge[7:8], ("zl", "core"), [(0, 1), (1, 2), (2, 3)])
    (input_grad,) = staged(
        input_kernel,
        (place_at, d_five, w5, carried),
        [((1024, CH), bf16)],
        [(square, f32)] * 3,
        flops=2**30,
        moved=4 * 2**20,
    )
    sum_c = sum_line_by_permutes(sum_plane(plane_c), core)
    grad_proj = proj_rows(sum_c)
    plane_ab, grad_proj, input_grad = across_plane(cores_ab.reshape(16, 4, 64, HALF), grad_proj, input_grad)
    sum_ab = sum_line(sum_plane(plane_ab))
    grad_five, grad_six, grad_seven, grad_channel, grad_bias = staged(
        finish_kernel,
        (place_at, sum_ab, swap_cores(sum_ab)),
        [((24, CH), f32), ((16, CH), f32), ((16, CH), f32), ((8, 11), f32), ((1, 30), f32)],
        [],
        flops=0,
        moved=2**18,
    )

    return (
        projected[None],
        input_grad[None],
        grad_five,
        grad_six,
        grad_seven,
        grad_channel,
        grad_proj,
        grad_bias.reshape(30),
    )


def solution(mesh):
    fine = Mesh(mesh.devices.reshape(4, 4, 4, 2, 2), ("x", "zh", "y", "zl", "core"))
    dp, seq = ("x", "zh", "y"), ("zl", "core")
    placed = (
        P(dp, seq, None),
        P(dp, None),
        P(dp, None),
        P(dp, None),
        P(dp, None),
        P(dp, None),
        P(dp),
        P(dp, seq, None),
    )
    return jax.shard_map(
        shards,
        mesh=fine,
        in_specs=placed,
        out_specs=(
            P(dp, seq, None),
            P(dp, seq, None),
            P(dp, None),
            P(dp, None),
            P(dp, None),
            P(dp, None),
            P(dp, None),
            P(dp),
        ),
        check_vma=False,
    )
```

```python
import jax
import jax.numpy as jnp
from jax import lax
from jax.experimental import pallas as pl
from jax.experimental.pallas import tpu as pltpu
from jax.sharding import Mesh, PartitionSpec as P

epsilon = 1e-05
f32 = jnp.float32
bf16 = jnp.bfloat16
CH = 512
WIDTH = 1920
HALF = 256
STEP = 64
ALL_VMEM = 2**26 - 2**18


def dot(left, right, contract=(1, 0)):
    return lax.dot_general(
        left, right, (((contract[0],), (contract[1],)), ((), ())), preferred_element_type=f32
    )


def staged(body, operands, outs, scratch, flops, moved):
    count, made = len(operands) - 1, len(outs)

    def kernel(place_ref, *refs):
        refs = list(refs)
        groups = []
        for size in (count, made, count, made):
            groups.append(refs[:size])
            refs = refs[size:]
        from_hbm, to_hbm, ins, results = groups
        in_sems, out_sems, *rest = refs
        loads = [pltpu.make_async_copy(a, b, in_sems.at[i]) for i, (a, b) in enumerate(zip(from_hbm, ins))]
        stores = [pltpu.make_async_copy(a, b, out_sems.at[i]) for i, (a, b) in enumerate(zip(results, to_hbm))]
        for load in loads:
            load.start()
        waited, sent = set(), set()

        def need(*which):
            for ref in which:
                index = next(i for i, own in enumerate(ins) if own is ref)
                if index not in waited:
                    waited.add(index)
                    loads[index].wait()

        def give(*which):
            for ref in which:
                index = next(i for i, own in enumerate(results) if own is ref)
                if index not in sent:
                    sent.add(index)
                    stores[index].start()

        body(place_ref, ins, results, rest, need, give)
        need(*ins)
        give(*results)
        for store in stores:
            store.wait()

    hbm = pl.BlockSpec(memory_space=pltpu.HBM)
    return pl.pallas_call(
        kernel,
        out_shape=[jax.ShapeDtypeStruct(shape, kind) for shape, kind in outs],
        in_specs=[pl.BlockSpec(memory_space=pltpu.SMEM)] + [hbm] * count,
        out_specs=[hbm] * made,
        scratch_shapes=[pltpu.VMEM(array.shape, array.dtype) for array in operands[1:]]
        + [pltpu.VMEM(shape, kind) for shape, kind in outs]
        + [pltpu.SemaphoreType.DMA((count,)), pltpu.SemaphoreType.DMA((made,))]
        + [pltpu.VMEM(shape, kind) for shape, kind in scratch],
        compiler_params=pltpu.CompilerParams(vmem_limit_bytes=ALL_VMEM),
        cost_estimate=pl.CostEstimate(flops=flops, bytes_accessed=moved, transcendentals=0),
    )(*operands)


def place(index):
    return (index // 16) * 16 + (index % 4) * 4 + (index // 4) % 4


def rows(index, size):
    return pl.ds(pl.multiple_of(index * size, size), size)


def by_core(core_ref, body):
    @pl.when(core_ref[0] == 0)
    def _():
        body(0, HALF)

    @pl.when(core_ref[0] != 0)
    def _():
        body(HALF, 0)


def row_mean(values):
    return jnp.sum(values, -1, keepdims=True) * (1.0 / CH)


def standard(values):
    centred = values - row_mean(values)
    scale = lax.rsqrt(row_mean(centred * centred) + epsilon)
    return centred * scale, scale


def fold(values):
    return jnp.sum(values.reshape(-1, 8, values.shape[-1]), 0)


def block_forward(pre_ref, cp_ref, first, act_ref, unit_ref, slope_ref, scale_ref):
    offset, gain, shift = (cp_ref[first + i : first + i + 1] for i in range(3))

    def step(i, _):
        at = rows(i, STEP)
        unit, scale = standard(pre_ref[at, :] + offset)
        z = unit * gain + shift
        cdf = 0.5 + 0.5 * lax.erf(z * 0.7071067811865476)
        act_ref[at, :] = (z * cdf).astype(bf16)
        slope_ref[at, :] = cdf + z * (0.3989422804014327 * jnp.exp(-0.5 * z * z))
        unit_ref[at, :] = unit
        scale_ref[at, :] = jnp.broadcast_to(scale, (STEP, 128))
        return 0

    lax.fori_loop(0, pre_ref.shape[0] // STEP, step, 0, unroll=2)


def block_backward(grad_ref, cp_ref, first, unit_ref, slope_ref, scale_ref, out_ref):
    gain = cp_ref[first + 1 : first + 2]

    def step(i, sums):
        at = rows(i, STEP)
        unit = unit_ref[at, :]
        dz = grad_ref[at, :] * slope_ref[at, :]
        dunit = dz * gain
        du = scale_ref[at, :1] * (dunit - row_mean(dunit) - unit * row_mean(dunit * unit))
        out_ref[at, :] = du.astype(bf16)
        return (sums[0] + fold(du), sums[1] + fold(dz * unit), sums[2] + fold(dz))

    zero = jnp.zeros((8, CH), f32)
    return lax.fori_loop(0, grad_ref.shape[0] // STEP, step, (zero, zero, zero), unroll=2)


def total(values):
    return jnp.sum(values, 0, keepdims=True)


def spread(transposed):
    group = lax.broadcasted_iota(jnp.int32, (256, 256), 1 if transposed else 0)
    position = lax.broadcasted_iota(jnp.int32, (256, 256), 0 if transposed else 1)
    return (position == 8 * (group % 32) + group // 32).astype(bf16)


def pack_kernel(place_ref, ins, outs, scratch, need, give):
    w5_ref, w6_ref, w7_ref, wp_ref, cp_ref, bias_ref = ins
    (out_ref,) = outs
    (small_ref,) = scratch
    need(*ins)
    small_ref[...] = jnp.zeros((8, HALF), f32)
    small_ref[:, :11] = cp_ref[...].astype(f32)
    small_ref[:1, 128:158] = bias_ref[...].astype(f32)

    def body(at, _):
        tail = small_ref[...] if at == 0 else jnp.zeros((8, HALF), f32)
        first = jnp.concatenate([w5_ref[:, at : at + HALF].astype(f32), tail], 0).astype(bf16)
        parts = []
        for b in range(4):
            start = 4 * at + HALF * b
            part = wp_ref[:, start : min(start + HALF, WIDTH)].astype(f32)
            if start + HALF > WIDTH:
                part = jnp.concatenate([part, jnp.zeros((8, start + HALF - WIDTH), f32)], 1)
            parts.append(part)
        last = jnp.concatenate(parts, 0).astype(bf16)
        for k in range(4):
            out_ref[k, :32, :] = first
            out_ref[k, 32:48, :] = w6_ref[:, at : at + HALF]
            out_ref[k, 48:64, :] = w7_ref[:, at : at + HALF]
            out_ref[k, 64:, :] = last

    by_core(place_ref, body)


def split_kernel(place_ref, ins, outs, scratch, need, give):
    x_ref, next_ref, line_ref = ins
    unfold_ref, spread_c_ref = outs
    (first_ref,) = scratch
    need(*ins)
    for k in range(16):
        spread_c_ref[k] = line_ref[:, 64:]
    give(spread_c_ref)
    matrix = spread(False)
    for j in range(4):
        groups = dot(matrix, x_ref[256 * j : 256 * j + 256, :])
        first_ref[32 * j : 32 * j + 32, :] = groups[:32]
        groups = groups.astype(bf16)
        for r in range(4):
            at = slice(128 * r + 32 * j, 128 * r + 32 * j + 32)
            unfold_ref[0, at, :] = groups[64 * r : 64 * r + 32]
            unfold_ref[1, at, :] = groups[64 * r + 32 : 64 * r + 64]
            if r > 0:
                unfold_ref[2, 128 * r - 128 + 32 * j : 128 * r - 96 + 32 * j, :] = groups[64 * r : 64 * r + 32]
    later = pltpu.roll(first_ref[...], 127, 0)
    last = lax.broadcasted_iota(jnp.int32, (128, CH), 0) == 127
    unfold_ref[2, 384:512, :] = jnp.where(last, next_ref[:1, :].astype(f32), later).astype(bf16)


def forward_kernel(core_ref, ins, outs, scratch, need, give):
    mine_ref, other_ref, unfold_ref, unfold_other_ref, cot_ref, cot_other_ref = ins
    (
        cp_ref, w5_ref, five_ref, unit5_ref, slope5_ref, scale5_ref,
        w6_ref, w7_ref, act6_ref, unit6_ref, slope6_ref, scale6_ref, unit7_ref, slope7_ref, scale7_ref,
        normed_ref, unit_ref, scale_ref, give_ref,
    ) = outs
    wide_ref, small_ref, pre5_ref, pre6_ref, pre7_ref, act7_ref, gp_ref = scratch
    need(mine_ref, other_ref)

    def unpack(mine_at, other_at):
        def step(i, _):
            to = place(i)
            for ref, at in ((mine_ref, mine_at), (other_ref, other_at)):
                block = ref[i, :32].astype(f32)
                wide_ref[rows(to, 24), at : at + HALF] = block[:24]
                if at == 0:
                    small_ref[rows(to, 8), :] = block[24:, :128]
                w6_ref[rows(to, 16), at : at + HALF] = ref[i, 32:48]
                w7_ref[rows(to, 16), at : at + HALF] = ref[i, 48:]
            return 0

        lax.fori_loop(0, 64, step, 0, unroll=4)

    by_core(core_ref, unpack)
    cp_ref[...] = small_ref[...].T[:16]

    def narrow(i, _):
        w5_ref[rows(i, 128), :] = wide_ref[rows(i, 128), :].astype(bf16)
        return 0

    lax.fori_loop(0, 12, narrow, 0)
    give(cp_ref, w5_ref, w6_ref, w7_ref)
    need(unfold_ref, unfold_other_ref)

    for b, ref in enumerate((unfold_ref, unfold_other_ref)):

        def multiply(r, _, b=b, ref=ref):
            at = rows(r, 128)
            pre5_ref[rows(r + 4 * b, 128), :] = (
                dot(ref[0, at, :], w5_ref[:512, :]) + dot(ref[1, at, :], w5_ref[512:1024, :])
            ) + dot(ref[2, at, :], w5_ref[1024:, :])
            return 0

        lax.fori_loop(0, 4, multiply, 0)
    block_forward(pre5_ref, cp_ref, 0, five_ref, unit5_ref, slope5_ref, scale5_ref)
    give(five_ref, unit5_ref, slope5_ref, scale5_ref)
    for s in range(4):
        pre6_ref[128 * s : 128 * s + 128, :] = dot(five_ref[256 * s : 256 * s + 128, :], w6_ref[:512, :]) + dot(
            five_ref[256 * s + 128 : 256 * s + 256, :], w6_ref[512:, :]
        )
    block_forward(pre6_ref, cp_ref, 3, act6_ref, unit6_ref, slope6_ref, scale6_ref)
    give(act6_ref, unit6_ref, slope6_ref, scale6_ref)
    for b in range(2):
        pre7_ref[128 * b : 128 * b + 128, :] = dot(act6_ref[256 * b : 256 * b + 128, :], w7_ref[:512, :]) + dot(
            act6_ref[256 * b + 128 : 256 * b + 256, :], w7_ref[512:, :]
        )
    block_forward(pre7_ref, cp_ref, 6, act7_ref, unit7_ref, slope7_ref, scale7_ref)
    give(unit7_ref, slope7_ref, scale7_ref)

    unit, scale = standard(act7_ref[...].astype(f32))
    normed = (unit * cp_ref[9:10] + cp_ref[10:11]).astype(bf16)
    unit_ref[...] = unit
    scale_ref[...] = jnp.broadcast_to(scale, (256, 128))
    normed_ref[...] = normed
    give(unit_ref, scale_ref, normed_ref)
    flipped = normed.astype(f32).T.astype(bf16)
    need(cot_ref, cot_other_ref)

    def multiply_proj(mine_at, other_at):
        for b in range(4):
            start = 4 * mine_at + HALF * b
            cols = slice(start, min(start + HALF, WIDTH))
            both = jnp.concatenate([cot_ref[:, cols], cot_other_ref[:, cols]], 0)
            gp_ref[:, HALF * b : HALF * b + both.shape[1]] = dot(flipped, both)
            if both.shape[1] < HALF:
                gp_ref[:, HALF * b + both.shape[1] : HALF * (b + 1)] = jnp.zeros((CH, HALF - both.shape[1]), f32)

    by_core(core_ref, multiply_proj)

    def pack(i, _):
        block = gp_ref[rows(place(i), 8), :]
        parts = [block[:, HALF * b : HALF * (b + 1)] for b in range(4)]
        give_ref[i] = jnp.concatenate(parts, 0).astype(bf16)
        return 0

    lax.fori_loop(0, 64, pack, 0, unroll=4)


def backward_kernel(core_ref, ins, outs, scratch, need, give):
    (
        mine_ref, other_ref, cp_ref, bias_ref, cot_ref, cot_other_ref, normed_ref, unit_ref, scale_ref,
        unit7_ref, slope7_ref, scale7_ref, w7_ref, act6_ref, unit6_ref, slope6_ref, scale6_ref, w6_ref, five_ref,
        unit5_ref, slope5_ref, scale5_ref, w5_ref, unfold_ref, unfold_other_ref, gb_ref,
    ) = ins
    out_ref, edge_ref, d5_ref, give_ref = outs
    (
        wp_ref, wide_ref, pre5_ref, pre6_ref, pre7_ref, g5_ref, g6_ref, g7_ref, d6_ref, d7_ref, half_ref, small_ref, sums_ref,
    ) = scratch
    need(mine_ref, other_ref)

    def unpack(mine_at, other_at):
        def step(i, _):
            to = place(i)
            for ref, at in ((mine_ref, mine_at), (other_ref, other_at)):
                block = ref[i].astype(f32)
                for b in range(4):
                    wide_ref[rows(to, 8), 4 * at + HALF * b : 4 * at + HALF * (b + 1)] = block[8 * b : 8 * b + 8]
            return 0

        lax.fori_loop(0, 64, step, 0, unroll=4)

    by_core(core_ref, unpack)

    def narrow(i, _):
        wp_ref[rows(i, 64), :] = wide_ref[rows(i, 64), :WIDTH].astype(bf16)
        return 0

    lax.fori_loop(0, 8, narrow, 0)
    need(cp_ref, bias_ref, cot_ref, cot_other_ref, normed_ref)

    def keep(ref):
        size = ref.shape[0]

        def body(mine_at, other_at):
            half_ref[:size, :] = ref[:, mine_at : mine_at + HALF]

        by_core(core_ref, body)

    normed_grad = jnp.zeros((256, CH), f32)
    for b in range(8):
        cols = slice(HALF * b, min(HALF * (b + 1), WIDTH))
        out_ref[:, cols] = (dot(normed_ref[:128, :], wp_ref[:, cols]) + bias_ref[:, cols]).astype(bf16)
        both = jnp.concatenate([cot_ref[:, cols], cot_other_ref[:, cols]], 0)
        normed_grad = normed_grad + dot(both, wp_ref[:, cols], (1, 1))

    need(unit_ref, scale_ref, unit7_ref, slope7_ref, scale7_ref)
    give(out_ref)
    unit = unit_ref[...]
    dunit = normed_grad * cp_ref[9:10]
    sums_ref[...] = jnp.zeros((128, CH), f32)
    sums_ref[9:10, :] = total(normed_grad * unit)
    sums_ref[10:11, :] = total(normed_grad)
    pre7_ref[...] = scale_ref[:, :1] * (dunit - row_mean(dunit) - unit * row_mean(dunit * unit))

    for i, part in enumerate(block_backward(pre7_ref, cp_ref, 6, unit7_ref, slope7_ref, scale7_ref, d7_ref)):
        sums_ref[6 + i : 7 + i, :] = total(part)
    need(w7_ref, act6_ref)
    keep(d7_ref)
    for s in range(2):
        half = slice(512 * s, 512 * s + 512)
        left = [act6_ref[256 * b + 128 * s : 256 * b + 128 * s + 128, :] for b in range(2)]
        g7_ref[half, :] = dot(jnp.concatenate(left, 0), half_ref[:256, :], (0, 0))
        for b in range(2):
            at = 256 * b + 128 * s
            pre6_ref[at : at + 128, :] = dot(d7_ref[128 * b : 128 * b + 128, :], w7_ref[half, :], (1, 1))
    need(unit6_ref, slope6_ref, scale6_ref)
    for i, part in enumerate(block_backward(pre6_ref, cp_ref, 3, unit6_ref, slope6_ref, scale6_ref, d6_ref)):
        sums_ref[3 + i : 4 + i, :] = total(part)
    need(w6_ref, five_ref)
    keep(d6_ref)
    for r in range(2):
        half = slice(512 * r, 512 * r + 512)
        left = [five_ref[256 * s + 128 * r : 256 * s + 128 * r + 128, :] for s in range(4)]
        g6_ref[half, :] = dot(jnp.concatenate(left, 0), half_ref[:512, :], (0, 0))
        for s in range(4):
            at = 256 * s + 128 * r
            pre5_ref[at : at + 128, :] = dot(d6_ref[128 * s : 128 * s + 128, :], w6_ref[half, :], (1, 1))
    need(unit5_ref, slope5_ref, scale5_ref)
    for i, part in enumerate(block_backward(pre5_ref, cp_ref, 0, unit5_ref, slope5_ref, scale5_ref, d5_ref)):
        sums_ref[i : i + 1, :] = total(part)
    need(*ins)
    give(d5_ref)
    edge_ref[...] = dot(d5_ref[496:512, :], w5_ref[1024:, :], (1, 1))[8:]
    keep(d5_ref)
    for k in range(3):
        g5_ref[512 * k : 512 * k + 512, :] = dot(unfold_ref[k], half_ref[:512, :], (0, 0)) + dot(
            unfold_other_ref[k], half_ref[512:, :], (0, 0)
        )
    small_ref[...] = sums_ref[...].T

    def pack(mine_at, other_at):
        def step(i, _):
            to = place(i)
            if mine_at == 0:
                tail = jnp.concatenate([small_ref[rows(to, 8), :], gb_ref[rows(to, 8), :]], 1)
            else:
                tail = jnp.zeros((8, HALF), f32)
            give_ref[i, :32, :] = jnp.concatenate([g5_ref[rows(to, 24), :], tail], 0).astype(bf16)
            give_ref[i, 32:48, :] = g6_ref[rows(to, 16), :].astype(bf16)
            give_ref[i, 48:, :] = g7_ref[rows(to, 16), :].astype(bf16)
            return 0

        lax.fori_loop(0, 64, step, 0, unroll=4)

    by_core(core_ref, pack)


def input_kernel(place_ref, ins, outs, scratch, need, give):
    d_ref, w_ref, carried_ref = ins
    (out_ref,) = outs
    even_ref, odd_ref, third_ref = scratch
    need(*ins)

    def multiply(r, _):
        at = rows(r, 128)
        d = d_ref[at, :]
        even_ref[at, :] = dot(d, w_ref[:512, :], (1, 1))
        odd_ref[at, :] = dot(d, w_ref[512:1024, :], (1, 1))
        third_ref[at, :] = dot(d, w_ref[1024:, :], (1, 1))
        return 0

    lax.fori_loop(0, 4, multiply, 0)
    earlier = pltpu.roll(third_ref[384:512, :], 1, 0)
    first = lax.broadcasted_iota(jnp.int32, (128, CH), 0) == 0
    even_ref[:128, :] += jnp.where(first, carried_ref[...], earlier)
    even_ref[128:, :] += third_ref[:384, :]
    matrix = spread(True)
    for j in range(4):
        parts = []
        for r in range(4):
            at = slice(128 * r + 32 * j, 128 * r + 32 * j + 32)
            parts += [even_ref[at, :].astype(bf16), odd_ref[at, :].astype(bf16)]
        out_ref[256 * j : 256 * j + 256, :] = dot(matrix, jnp.concatenate(parts, 0)).astype(bf16)


def finish_kernel(core_ref, ins, outs, scratch, need, give):
    mine_ref, other_ref = ins
    g5_ref, g6_ref, g7_ref, channel_ref, bias_ref = outs
    need(*ins)

    def body(mine_at, other_at):
        for ref, at in ((mine_ref, mine_at), (other_ref, other_at)):
            g5_ref[:, at : at + HALF] = ref[:24, :]
            g6_ref[:, at : at + HALF] = ref[32:48, :]
            g7_ref[:, at : at + HALF] = ref[48:, :]
            if at == 0:
                channel_ref[...] = ref[24:32, :11]
                bias_ref[...] = ref[24:25, 128:158]

    by_core(core_ref, body)


def swap_cores(value):
    return lax.ppermute(value, "core", [(0, 1), (1, 0)])


def together(*values):
    return lax.optimization_barrier(values)


def around(value, axis, size, back):
    return lax.ppermute(value, axis, [(i, (i + back) % size) for i in range(size)])


def across_plane(value, *meanwhile):
    return together(lax.all_to_all(value, ("x", "y"), 0, 0, tiled=True), *meanwhile)


def sum_plane(plane):
    return jnp.sum(plane.astype(f32), 0).astype(bf16)


def both_halves(summed, core):
    other = swap_cores(summed)
    return jnp.stack([jnp.where(core == 0, summed, other), jnp.where(core == 0, other, summed)])


def sum_line(value):
    count = value.shape[1]
    line = jnp.broadcast_to(value[:, None], (4, 2, count, HALF)).reshape(8, count, HALF)
    line = lax.all_to_all(line, ("zh", "zl"), 0, 0, tiled=True)
    return jnp.sum(line.astype(f32), 0)


def sum_line_by_permutes(value, core):
    zh = lax.axis_index("zh")
    pick = lambda k: lax.dynamic_index_in_dim(value, (zh + k) % 4, 0, False)
    parts = [pick(0)] + [around(pick(k), "zh", 4, k) for k in range(1, 4)]
    summed = sum(part.astype(f32) for part in parts)
    summed = summed + lax.ppermute(summed, "zl", [(0, 1), (1, 0)])
    return both_halves(summed, core)


def proj_rows(halves):
    return halves.reshape(2, 4, 8, HALF).transpose(2, 0, 1, 3).reshape(8, 8 * HALF)[:, :WIDTH]


def shards(features, w_five, w_six, w_seven, channel_params, w_proj, proj_bias, out_cotangent):
    core = lax.axis_index("core")
    place_at = core.astype(jnp.int32).reshape(1)
    inputs, cotangent = features[0], out_cotangent[0]
    square, flat, stack = (512, CH), (512, 128), (64, 32, HALF)

    (packed,) = staged(
        pack_kernel,
        (place_at, w_five, w_six, w_seven, w_proj, channel_params, proj_bias.reshape(1, 30)),
        [((4, 96, HALF), bf16)],
        [((8, HALF), f32)],
        flops=0,
        moved=2**18,
    )
    line = lax.all_to_all(packed, "zh", 0, 0, tiled=True)
    spread_ab = jnp.broadcast_to(line[None, :, :64], (16, 4, 64, HALF))

    line, first_rows, late_cotangent = together(line, inputs[:16], cotangent)
    next_row = lax.ppermute(first_rows, ("zl", "core"), [(1, 0), (2, 1), (3, 2)])
    unfold, spread_c = staged(
        split_kernel,
        (place_at, inputs, next_row, line),
        [((3, 512, CH), bf16), ((16, 4, 32, HALF), bf16)],
        [((128, CH), f32)],
        flops=2**28,
        moved=3 * 2**20,
    )
    unfold_other = swap_cores(unfold)
    cot_other = swap_cores(late_cotangent)
    grad_bias = (jnp.sum(late_cotangent.astype(f32), 0) + jnp.sum(cot_other.astype(f32), 0)).reshape(64, 1, 30)
    grad_bias = jnp.pad(grad_bias, [(0, 0), (0, 7), (0, 98)]).reshape(512, 128)

    mine_ab, spread_c, unfold, unfold_other, cot_other, grad_bias = across_plane(
        spread_ab, spread_c, unfold, unfold_other, cot_other, grad_bias
    )
    mine_ab = mine_ab.reshape(64, 64, HALF)
    other_ab = swap_cores(mine_ab)
    bias = jnp.where(core == 0, mine_ab[:, 24, 128:158], other_ab[:, 24, 128:158])
    bias = bias.reshape(4, 4, 4, 30).transpose(0, 2, 1, 3).reshape(1, WIDTH).astype(f32)

    saved = lambda n: [((n, CH), f32), ((n, CH), f32), ((n, 128), f32)]
    w_shapes = [((1536, CH), bf16), ((1024, CH), bf16), ((1024, CH), bf16)]
    cp, w5, act_five, *saved_five, w6, w7, act_six, u6, s6, r6, u7, s7, r7, normed, unit, scale, give_c = staged(
        forward_kernel,
        (place_at, mine_ab, other_ab, unfold, unfold_other, cotangent, cot_other),
        [((16, CH), f32), w_shapes[0], ((1024, CH), bf16)]
        + saved(1024)
        + w_shapes[1:]
        + [(square, bf16)]
        + saved(512)
        + saved(256)
        + [((256, CH), bf16), ((256, CH), f32), ((256, 128), f32)]
        + [(stack, bf16)],
        [((1536, CH), f32), (flat, f32), ((1024, CH), f32), (square, f32), ((256, CH), f32), ((256, CH), bf16)]
        + [((CH, 4 * HALF), f32)],
        flops=2**31,
        moved=16 * 2**20,
    )

    mine_c, give_c = across_plane(spread_c, give_c)
    mine_c = mine_c.reshape(stack)
    other_c = swap_cores(mine_c)
    projected, edge, d_five, give_ab = staged(
        backward_kernel,
        (place_at, mine_c, other_c, cp, bias, cotangent, cot_other, normed, unit, scale, u7, s7, r7, w7, act_six)
        + (u6, s6, r6, w6, act_five, *saved_five, w5, unfold, unfold_other, grad_bias),
        [((128, WIDTH), bf16), ((8, CH), f32), ((1024, CH), bf16), ((64, 64, HALF), bf16)],
        [((CH, WIDTH), bf16), ((CH, 8 * HALF), f32), ((1024, CH), f32), (square, f32), ((256, CH), f32)]
        + [((1536, HALF), f32), ((1024, HALF), f32), ((1024, HALF), f32), (square, bf16), ((256, CH), bf16)]
        + [((1024, HALF), bf16), (flat, f32), ((128, CH), f32)],
        flops=2**31,
        moved=16 * 2**20,
    )

    plane_c, give_ab = across_plane(give_c.reshape(16, 4, 32, HALF), give_ab)
    give_ab, plane_c, d_five = together(give_ab, plane_c, d_five)
    carried = lax.ppermute(edge[7:8], ("zl", "core"), [(0, 1), (1, 2), (2, 3)])
    (input_grad,) = staged(
        input_kernel,
        (place_at, d_five, w5, carried),
        [((1024, CH), bf16)],
        [(square, f32)] * 3,
        flops=2**30,
        moved=4 * 2**20,
    )
    sum_c = sum_line_by_permutes(sum_plane(plane_c), core)
    grad_proj = proj_rows(sum_c)
    plane_ab, grad_proj, input_grad = across_plane(give_ab.reshape(16, 4, 64, HALF), grad_proj, input_grad)
    sum_ab = sum_line(sum_plane(plane_ab))
    grad_five, grad_six, grad_seven, grad_channel, grad_bias = staged(
        finish_kernel,
        (place_at, sum_ab, swap_cores(sum_ab)),
        [((24, CH), f32), ((16, CH), f32), ((16, CH), f32), ((8, 11), f32), ((1, 30), f32)],
        [],
        flops=0,
        moved=2**18,
    )

    return (
        projected[None],
        input_grad[None],
        grad_five,
        grad_six,
        grad_seven,
        grad_channel,
        grad_proj,
        grad_bias.reshape(30),
    )


def solution(mesh):
    fine = Mesh(mesh.devices.reshape(4, 4, 4, 2, 2), ("x", "zh", "y", "zl", "core"))
    dp, seq = ("x", "zh", "y"), ("zl", "core")
    placed = (
        P(dp, seq, None),
        P(dp, None),
        P(dp, None),
        P(dp, None),
        P(dp, None),
        P(dp, None),
        P(dp),
        P(dp, seq, None),
    )
    return jax.shard_map(
        shards,
        mesh=fine,
        in_specs=placed,
        out_specs=(
            P(dp, seq, None),
            P(dp, seq, None),
            P(dp, None),
            P(dp, None),
            P(dp, None),
            P(dp, None),
            P(dp, None),
            P(dp),
        ),
        check_vma=False,
    )
```

```python
import jax
import jax.numpy as jnp
from jax import lax
from jax.experimental import pallas as pl
from jax.experimental.pallas import tpu as pltpu
from jax.sharding import Mesh, PartitionSpec as P

epsilon = 1e-05
f32 = jnp.float32
bf16 = jnp.bfloat16
CH = 512
WIDTH = 1920
HALF = 256
STEP = 64
SEAT = 64
BLOCK = 240
ALL_VMEM = 2**26 - 2**18


def dot(left, right, contract=(1, 0)):
    return lax.dot_general(
        left, right, (((contract[0],), (contract[1],)), ((), ())), preferred_element_type=f32
    )


def staged(body, operands, outs, scratch, flops, moved):
    count, made = len(operands) - 1, len(outs)

    def kernel(place_ref, *refs):
        refs = list(refs)
        groups = []
        for size in (count, made, count, made):
            groups.append(refs[:size])
            refs = refs[size:]
        from_hbm, to_hbm, ins, results = groups
        in_sems, out_sems, *rest = refs
        loads = [pltpu.make_async_copy(a, b, in_sems.at[i]) for i, (a, b) in enumerate(zip(from_hbm, ins))]
        stores = [pltpu.make_async_copy(a, b, out_sems.at[i]) for i, (a, b) in enumerate(zip(results, to_hbm))]
        for load in loads:
            load.start()
        waited, sent = set(), set()

        def need(*which):
            for ref in which:
                index = next(i for i, own in enumerate(ins) if own is ref)
                if index not in waited:
                    waited.add(index)
                    loads[index].wait()

        def give(*which):
            for ref in which:
                index = next(i for i, own in enumerate(results) if own is ref)
                if index not in sent:
                    sent.add(index)
                    stores[index].start()

        body(place_ref, ins, results, rest, need, give)
        need(*ins)
        give(*results)
        for store in stores:
            store.wait()

    hbm = pl.BlockSpec(memory_space=pltpu.HBM)
    return pl.pallas_call(
        kernel,
        out_shape=[jax.ShapeDtypeStruct(shape, kind) for shape, kind in outs],
        in_specs=[pl.BlockSpec(memory_space=pltpu.SMEM)] + [hbm] * count,
        out_specs=[hbm] * made,
        scratch_shapes=[pltpu.VMEM(array.shape, array.dtype) for array in operands[1:]]
        + [pltpu.VMEM(shape, kind) for shape, kind in outs]
        + [pltpu.SemaphoreType.DMA((count,)), pltpu.SemaphoreType.DMA((made,))]
        + [pltpu.VMEM(shape, kind) for shape, kind in scratch],
        compiler_params=pltpu.CompilerParams(vmem_limit_bytes=ALL_VMEM),
        cost_estimate=pl.CostEstimate(flops=flops, bytes_accessed=moved, transcendentals=0),
    )(*operands)


def place(index):
    return (index // 16) * 16 + (index % 4) * 4 + (index // 4) % 4


def seated(values, seat):
    return pltpu.roll(values, SEAT * seat, 1) if seat else values


def unseated(values, seat):
    return pltpu.roll(values, HALF - SEAT * seat, 1) if seat else values


def shard_of(plane, seat):
    return (plane // 4) * 16 + seat * 4 + plane % 4


def rows(index, size):
    return pl.ds(pl.multiple_of(index * size, size), size)


def by_core(core_ref, body):
    @pl.when(core_ref[0] == 0)
    def _():
        body(0, HALF)

    @pl.when(core_ref[0] != 0)
    def _():
        body(HALF, 0)


def row_mean(values):
    return jnp.sum(values, -1, keepdims=True) * (1.0 / CH)


def standard(values):
    centred = values - row_mean(values)
    scale = lax.rsqrt(row_mean(centred * centred) + epsilon)
    return centred * scale, scale


def fold(values):
    return jnp.sum(values.reshape(-1, 8, values.shape[-1]), 0)


def block_forward(pre_ref, cp_ref, first, act_ref, unit_ref, slope_ref, scale_ref):
    offset, gain, shift = (cp_ref[first + i : first + i + 1] for i in range(3))

    def step(i, _):
        at = rows(i, STEP)
        unit, scale = standard(pre_ref[at, :] + offset)
        z = unit * gain + shift
        cdf = 0.5 + 0.5 * lax.erf(z * 0.7071067811865476)
        act_ref[at, :] = (z * cdf).astype(bf16)
        slope_ref[at, :] = cdf + z * (0.3989422804014327 * jnp.exp(-0.5 * z * z))
        unit_ref[at, :] = unit
        scale_ref[at, :] = jnp.broadcast_to(scale, (STEP, 128))
        return 0

    lax.fori_loop(0, pre_ref.shape[0] // STEP, step, 0, unroll=2)


def block_backward(grad_ref, cp_ref, first, unit_ref, slope_ref, scale_ref, out_ref):
    gain = cp_ref[first + 1 : first + 2]

    def step(i, sums):
        at = rows(i, STEP)
        unit = unit_ref[at, :]
        dz = grad_ref[at, :] * slope_ref[at, :]
        dunit = dz * gain
        du = scale_ref[at, :1] * (dunit - row_mean(dunit) - unit * row_mean(dunit * unit))
        out_ref[at, :] = du.astype(bf16)
        return (sums[0] + fold(du), sums[1] + fold(dz * unit), sums[2] + fold(dz))

    zero = jnp.zeros((8, CH), f32)
    return lax.fori_loop(0, grad_ref.shape[0] // STEP, step, (zero, zero, zero), unroll=2)


def total(values):
    return jnp.sum(values, 0, keepdims=True)


def spread(transposed):
    group = lax.broadcasted_iota(jnp.int32, (256, 256), 1 if transposed else 0)
    position = lax.broadcasted_iota(jnp.int32, (256, 256), 0 if transposed else 1)
    return (position == 8 * (group % 32) + group // 32).astype(bf16)


def pack_kernel(place_ref, ins, outs, scratch, need, give):
    w5_ref, w6_ref, w7_ref, wp_ref, cp_ref, bias_ref = ins
    (out_ref,) = outs
    (small_ref,) = scratch
    need(*ins)
    small_ref[...] = jnp.zeros((8, HALF), f32)
    small_ref[:, :11] = cp_ref[...].astype(f32)
    small_ref[:1, 16:46] = bias_ref[...].astype(f32)

    def body(at, _):
        tail = small_ref[...] if at == 0 else jnp.zeros((8, HALF), f32)
        first = jnp.concatenate([w5_ref[:, at : at + HALF].astype(f32), tail], 0).astype(bf16)
        parts = []
        for b in range(4):
            start = 4 * at + HALF * b
            part = wp_ref[:, start : min(start + HALF, WIDTH)].astype(f32)
            if start + HALF > WIDTH:
                part = jnp.concatenate([part, jnp.zeros((8, start + HALF - WIDTH), f32)], 1)
            parts.append(part)
        last = jnp.concatenate(parts, 0).astype(bf16)
        for k in range(4):
            out_ref[k, :32, :] = first
            out_ref[k, 32:48, :] = w6_ref[:, at : at + HALF]
            out_ref[k, 48:64, :] = w7_ref[:, at : at + HALF]
            out_ref[k, 64:, :] = last

    by_core(place_ref, body)


def split_kernel(place_ref, ins, outs, scratch, need, give):
    x_ref, next_ref, line_ref = ins
    unfold_ref, spread_c_ref = outs
    (first_ref,) = scratch
    need(*ins)
    for k in range(16):
        spread_c_ref[k] = line_ref[:, 64:]
    give(spread_c_ref)
    matrix = spread(False)
    for j in range(4):
        groups = dot(matrix, x_ref[256 * j : 256 * j + 256, :])
        first_ref[32 * j : 32 * j + 32, :] = groups[:32]
        groups = groups.astype(bf16)
        for r in range(4):
            at = slice(128 * r + 32 * j, 128 * r + 32 * j + 32)
            unfold_ref[0, at, :] = groups[64 * r : 64 * r + 32]
            unfold_ref[1, at, :] = groups[64 * r + 32 : 64 * r + 64]
            if r > 0:
                unfold_ref[2, 128 * r - 128 + 32 * j : 128 * r - 96 + 32 * j, :] = groups[64 * r : 64 * r + 32]
    later = pltpu.roll(first_ref[...], 127, 0)
    last = lax.broadcasted_iota(jnp.int32, (128, CH), 0) == 127
    unfold_ref[2, 384:512, :] = jnp.where(last, next_ref[:1, :].astype(f32), later).astype(bf16)


def forward_kernel(core_ref, ins, outs, scratch, need, give):
    mine_ref, other_ref, unfold_ref, unfold_other_ref, cot_ref, cot_other_ref = ins
    (
        cp_ref, w5_ref, five_ref, unit5_ref, slope5_ref, scale5_ref,
        w6_ref, w7_ref, act6_ref, unit6_ref, slope6_ref, scale6_ref, unit7_ref, slope7_ref, scale7_ref,
        normed_ref, unit_ref, scale_ref, give_ref,
    ) = outs
    wide_ref, small_ref, pre5_ref, pre6_ref, pre7_ref, act7_ref, gp_ref = scratch
    need(mine_ref, other_ref)

    def unpack(mine_at, other_at):
        def step(i, _):
            for ref, at in ((mine_ref, mine_at), (other_ref, other_at)):
                block = ref[i, :112].astype(f32)
                for seat in range(4):
                    to = shard_of(i, seat)
                    low = 112 + 32 * seat
                    wide_ref[rows(to, 24), at : at + HALF] = block[24 * seat : 24 * seat + 24]
                    if at == 0:
                        small_ref[rows(to, 8), :] = unseated(block[96:104], seat)[:, :128]
                    w6_ref[rows(to, 16), at : at + HALF] = ref[i, low : low + 16]
                    w7_ref[rows(to, 16), at : at + HALF] = ref[i, low + 16 : low + 32]
            return 0

        lax.fori_loop(0, 16, step, 0)

    by_core(core_ref, unpack)
    cp_ref[...] = small_ref[...].T[:16]

    def narrow(i, _):
        w5_ref[rows(i, 128), :] = wide_ref[rows(i, 128), :].astype(bf16)
        return 0

    lax.fori_loop(0, 12, narrow, 0)
    give(cp_ref, w5_ref, w6_ref, w7_ref)
    need(unfold_ref, unfold_other_ref)

    for b, ref in enumerate((unfold_ref, unfold_other_ref)):

        def multiply(r, _, b=b, ref=ref):
            at = rows(r, 128)
            pre5_ref[rows(r + 4 * b, 128), :] = (
                dot(ref[0, at, :], w5_ref[:512, :]) + dot(ref[1, at, :], w5_ref[512:1024, :])
            ) + dot(ref[2, at, :], w5_ref[1024:, :])
            return 0

        lax.fori_loop(0, 4, multiply, 0)
    block_forward(pre5_ref, cp_ref, 0, five_ref, unit5_ref, slope5_ref, scale5_ref)
    give(five_ref, unit5_ref, slope5_ref, scale5_ref)
    for s in range(4):
        pre6_ref[128 * s : 128 * s + 128, :] = dot(five_ref[256 * s : 256 * s + 128, :], w6_ref[:512, :]) + dot(
            five_ref[256 * s + 128 : 256 * s + 256, :], w6_ref[512:, :]
        )
    block_forward(pre6_ref, cp_ref, 3, act6_ref, unit6_ref, slope6_ref, scale6_ref)
    give(act6_ref, unit6_ref, slope6_ref, scale6_ref)
    for b in range(2):
        pre7_ref[128 * b : 128 * b + 128, :] = dot(act6_ref[256 * b : 256 * b + 128, :], w7_ref[:512, :]) + dot(
            act6_ref[256 * b + 128 : 256 * b + 256, :], w7_ref[512:, :]
        )
    block_forward(pre7_ref, cp_ref, 6, act7_ref, unit7_ref, slope7_ref, scale7_ref)
    give(unit7_ref, slope7_ref, scale7_ref)

    unit, scale = standard(act7_ref[...].astype(f32))
    normed = (unit * cp_ref[9:10] + cp_ref[10:11]).astype(bf16)
    unit_ref[...] = unit
    scale_ref[...] = jnp.broadcast_to(scale, (256, 128))
    normed_ref[...] = normed
    give(unit_ref, scale_ref, normed_ref)
    flipped = normed.astype(f32).T.astype(bf16)
    need(cot_ref, cot_other_ref)

    def multiply_proj(mine_at, other_at):
        for b in range(4):
            start = 4 * mine_at + HALF * b
            cols = slice(start, min(start + HALF, WIDTH))
            both = jnp.concatenate([cot_ref[:, cols], cot_other_ref[:, cols]], 0)
            gp_ref[:, HALF * b : HALF * b + both.shape[1]] = dot(flipped, both)
            if both.shape[1] < HALF:
                gp_ref[:, HALF * b + both.shape[1] : HALF * (b + 1)] = jnp.zeros((CH, HALF - both.shape[1]), f32)

    by_core(core_ref, multiply_proj)

    def pack(i, _):
        block = gp_ref[rows(place(i), 8), :]
        parts = [block[:, HALF * b : HALF * (b + 1)] for b in range(4)]
        give_ref[i] = jnp.concatenate(parts, 0).astype(bf16)
        return 0

    lax.fori_loop(0, 64, pack, 0, unroll=4)


def backward_kernel(core_ref, ins, outs, scratch, need, give):
    (
        mine_ref, other_ref, cp_ref, bias_ref, cot_ref, cot_other_ref, normed_ref, unit_ref, scale_ref,
        unit7_ref, slope7_ref, scale7_ref, w7_ref, act6_ref, unit6_ref, slope6_ref, scale6_ref, w6_ref, five_ref,
        unit5_ref, slope5_ref, scale5_ref, w5_ref, unfold_ref, unfold_other_ref, gb_ref,
    ) = ins
    out_ref, edge_ref, d5_ref, give_ref = outs
    (
        wp_ref, wide_ref, pre5_ref, pre6_ref, pre7_ref, g5_ref, g6_ref, g7_ref, d6_ref, d7_ref, half_ref, small_ref, sums_ref,
    ) = scratch
    need(mine_ref, other_ref)

    def unpack(mine_at, other_at):
        def step(i, _):
            to = place(i)
            for ref, at in ((mine_ref, mine_at), (other_ref, other_at)):
                block = ref[i].astype(f32)
                for b in range(4):
                    wide_ref[rows(to, 8), 4 * at + HALF * b : 4 * at + HALF * (b + 1)] = block[8 * b : 8 * b + 8]
            return 0

        lax.fori_loop(0, 64, step, 0, unroll=4)

    by_core(core_ref, unpack)

    def narrow(i, _):
        wp_ref[rows(i, 64), :] = wide_ref[rows(i, 64), :WIDTH].astype(bf16)
        return 0

    lax.fori_loop(0, 8, narrow, 0)
    need(cp_ref, bias_ref, cot_ref, cot_other_ref, normed_ref)

    def keep(ref):
        size = ref.shape[0]

        def body(mine_at, other_at):
            half_ref[:size, :] = ref[:, mine_at : mine_at + HALF]

        by_core(core_ref, body)

    normed_grad = jnp.zeros((256, CH), f32)
    for b in range(8):
        cols = slice(HALF * b, min(HALF * (b + 1), WIDTH))
        out_ref[:, cols] = (dot(normed_ref[:128, :], wp_ref[:, cols]) + bias_ref[:, cols]).astype(bf16)
        both = jnp.concatenate([cot_ref[:, cols], cot_other_ref[:, cols]], 0)
        normed_grad = normed_grad + dot(both, wp_ref[:, cols], (1, 1))

    need(unit_ref, scale_ref, unit7_ref, slope7_ref, scale7_ref)
    give(out_ref)
    unit = unit_ref[...]
    dunit = normed_grad * cp_ref[9:10]
    sums_ref[...] = jnp.zeros((128, CH), f32)
    sums_ref[9:10, :] = total(normed_grad * unit)
    sums_ref[10:11, :] = total(normed_grad)
    pre7_ref[...] = scale_ref[:, :1] * (dunit - row_mean(dunit) - unit * row_mean(dunit * unit))

    for i, part in enumerate(block_backward(pre7_ref, cp_ref, 6, unit7_ref, slope7_ref, scale7_ref, d7_ref)):
        sums_ref[6 + i : 7 + i, :] = total(part)
    need(w7_ref, act6_ref)
    keep(d7_ref)
    for s in range(2):
        half = slice(512 * s, 512 * s + 512)
        left = [act6_ref[256 * b + 128 * s : 256 * b + 128 * s + 128, :] for b in range(2)]
        g7_ref[half, :] = dot(jnp.concatenate(left, 0), half_ref[:256, :], (0, 0))
        for b in range(2):
            at = 256 * b + 128 * s
            pre6_ref[at : at + 128, :] = dot(d7_ref[128 * b : 128 * b + 128, :], w7_ref[half, :], (1, 1))
    need(unit6_ref, slope6_ref, scale6_ref)
    for i, part in enumerate(block_backward(pre6_ref, cp_ref, 3, unit6_ref, slope6_ref, scale6_ref, d6_ref)):
        sums_ref[3 + i : 4 + i, :] = total(part)
    need(w6_ref, five_ref)
    keep(d6_ref)
    for r in range(2):
        half = slice(512 * r, 512 * r + 512)
        left = [five_ref[256 * s + 128 * r : 256 * s + 128 * r + 128, :] for s in range(4)]
        g6_ref[half, :] = dot(jnp.concatenate(left, 0), half_ref[:512, :], (0, 0))
        for s in range(4):
            at = 256 * s + 128 * r
            pre5_ref[at : at + 128, :] = dot(d6_ref[128 * s : 128 * s + 128, :], w6_ref[half, :], (1, 1))
    need(unit5_ref, slope5_ref, scale5_ref)
    for i, part in enumerate(block_backward(pre5_ref, cp_ref, 0, unit5_ref, slope5_ref, scale5_ref, d5_ref)):
        sums_ref[i : i + 1, :] = total(part)
    need(*ins)
    give(d5_ref)
    edge_ref[...] = dot(d5_ref[496:512, :], w5_ref[1024:, :], (1, 1))[8:]
    keep(d5_ref)
    for k in range(3):
        g5_ref[512 * k : 512 * k + 512, :] = dot(unfold_ref[k], half_ref[:512, :], (0, 0)) + dot(
            unfold_other_ref[k], half_ref[512:, :], (0, 0)
        )
    small_ref[...] = sums_ref[...].T

    def pack(mine_at, other_at):
        def step(i, _):
            parts, tail = [], jnp.zeros((8, HALF), f32)
            for seat in range(4):
                to = shard_of(i, seat)
                low = 112 + 32 * seat
                parts.append(g5_ref[rows(to, 24), :])
                if mine_at == 0:
                    own = small_ref[rows(to, 8), :] + gb_ref[rows(to, 8), :]
                    tail = tail + seated(jnp.concatenate([own, jnp.zeros((8, HALF - 128), f32)], 1), seat)
                give_ref[i, low : low + 16, :] = g6_ref[rows(to, 16), :].astype(bf16)
                give_ref[i, low + 16 : low + 32, :] = g7_ref[rows(to, 16), :].astype(bf16)
            parts += [tail, jnp.zeros((8, HALF), f32)]
            give_ref[i, :112, :] = jnp.concatenate(parts, 0).astype(bf16)
            return 0

        lax.fori_loop(0, 16, step, 0)

    by_core(core_ref, pack)


def input_kernel(place_ref, ins, outs, scratch, need, give):
    d_ref, w_ref, carried_ref = ins
    (out_ref,) = outs
    even_ref, odd_ref, third_ref = scratch
    need(*ins)

    def multiply(r, _):
        at = rows(r, 128)
        d = d_ref[at, :]
        even_ref[at, :] = dot(d, w_ref[:512, :], (1, 1))
        odd_ref[at, :] = dot(d, w_ref[512:1024, :], (1, 1))
        third_ref[at, :] = dot(d, w_ref[1024:, :], (1, 1))
        return 0

    lax.fori_loop(0, 4, multiply, 0)
    earlier = pltpu.roll(third_ref[384:512, :], 1, 0)
    first = lax.broadcasted_iota(jnp.int32, (128, CH), 0) == 0
    even_ref[:128, :] += jnp.where(first, carried_ref[...], earlier)
    even_ref[128:, :] += third_ref[:384, :]
    matrix = spread(True)
    for j in range(4):
        parts = []
        for r in range(4):
            at = slice(128 * r + 32 * j, 128 * r + 32 * j + 32)
            parts += [even_ref[at, :].astype(bf16), odd_ref[at, :].astype(bf16)]
        out_ref[256 * j : 256 * j + 256, :] = dot(matrix, jnp.concatenate(parts, 0)).astype(bf16)


def finish_kernel(place_ref, zh_ref, mine_ref, other_ref, *refs):
    to_hbm, outs, sems = refs[:5], refs[5:10], refs[10]
    g5_ref, g6_ref, g7_ref, channel_ref, bias_ref = outs

    def body(mine_at, other_at):
        for ref, at in ((mine_ref, mine_at), (other_ref, other_at)):
            g5_ref[:, at : at + HALF] = ref[:24, :]
            g6_ref[:, at : at + HALF] = ref[32:48, :]
            g7_ref[:, at : at + HALF] = ref[48:, :]
            if at == 0:
                small = sum(jnp.where(zh_ref[0] == seat, unseated(ref[24:32, :], seat), 0.0) for seat in range(4))
                channel_ref[...] = small[:, :11]
                bias_ref[...] = small[:1, 16:46]

    by_core(place_ref, body)
    stores = [pltpu.make_async_copy(a, b, sems.at[i]) for i, (a, b) in enumerate(zip(outs, to_hbm))]
    for store in stores:
        store.start()
    for store in stores:
        store.wait()


def finish(place_at, zh_at, mine, other):
    shapes = [(24, CH), (16, CH), (16, CH), (8, 11), (1, 30)]
    vmem = pl.BlockSpec(memory_space=pltpu.VMEM)
    return pl.pallas_call(
        finish_kernel,
        out_shape=[jax.ShapeDtypeStruct(shape, f32) for shape in shapes],
        in_specs=[pl.BlockSpec(memory_space=pltpu.SMEM)] * 2 + [vmem, vmem],
        out_specs=[pl.BlockSpec(memory_space=pltpu.HBM)] * 5,
        scratch_shapes=[pltpu.VMEM(shape, f32) for shape in shapes] + [pltpu.SemaphoreType.DMA((5,))],
        compiler_params=pltpu.CompilerParams(vmem_limit_bytes=2**23),
        cost_estimate=pl.CostEstimate(flops=0, bytes_accessed=2**18, transcendentals=0),
    )(place_at, zh_at, mine, other)


def copies_kernel(line, out_ref, block, out_sems):
    small = sum(seated(line[seat, 16:32, :].astype(f32)[8:], seat) for seat in range(4))
    parts = [line[seat, :32, :].astype(f32)[:24] for seat in range(4)] + [small, jnp.zeros((8, HALF), f32)]
    block[:112, :] = jnp.concatenate(parts, 0).astype(bf16)
    for seat in range(4):
        block[112 + 32 * seat : 144 + 32 * seat, :] = line[seat, 32:64, :]
    stores = [pltpu.make_async_copy(block, out_ref.at[k], out_sems.at[k]) for k in range(16)]
    for store in stores:
        store.start()
    for store in stores:
        store.wait()


def copies(line):
    return pl.pallas_call(
        copies_kernel,
        out_shape=jax.ShapeDtypeStruct((16, BLOCK, HALF), bf16),
        in_specs=[pl.BlockSpec(memory_space=pltpu.VMEM)],
        out_specs=pl.BlockSpec(memory_space=pltpu.HBM),
        scratch_shapes=[pltpu.VMEM((BLOCK, HALF), bf16), pltpu.SemaphoreType.DMA((16,))],
        compiler_params=pltpu.CompilerParams(vmem_limit_bytes=2**23),
        cost_estimate=pl.CostEstimate(flops=0, bytes_accessed=2**21, transcendentals=0),
    )(line)


def swap_cores(value):
    return lax.ppermute(value, "core", [(0, 1), (1, 0)])


def together(*values):
    return lax.optimization_barrier(values)


def around(value, axis, size, back):
    return lax.ppermute(value, axis, [(i, (i + back) % size) for i in range(size)])


def across_plane(value, *meanwhile):
    return together(lax.all_to_all(value, ("x", "y"), 0, 0, tiled=True), *meanwhile)


def sum_plane(plane):
    return jnp.sum(plane.astype(f32), 0).astype(bf16)


def both_halves(summed, core):
    other = swap_cores(summed)
    return jnp.stack([jnp.where(core == 0, summed, other), jnp.where(core == 0, other, summed)])


def by_shard(value):
    parts = [[value[24 * z : 24 * z + 24], value[96:104], value[112 + 32 * z : 144 + 32 * z]] for z in range(4)]
    return jnp.concatenate(sum(parts, []), 0).reshape(4, 64, HALF)


def sum_line(value):
    count = value.shape[1]
    line = jnp.broadcast_to(value[:, None], (4, 2, count, HALF)).reshape(8, count, HALF)
    line = lax.all_to_all(line, ("zh", "zl"), 0, 0, tiled=True)
    return jnp.sum(line.astype(f32), 0)


def sum_line_by_permutes(value, core):
    zh = lax.axis_index("zh")
    pick = lambda k: lax.dynamic_index_in_dim(value, (zh + k) % 4, 0, False)
    parts = [pick(0)] + [around(pick(k), "zh", 4, k) for k in range(1, 4)]
    summed = sum(part.astype(f32) for part in parts)
    summed = summed + lax.ppermute(summed, "zl", [(0, 1), (1, 0)])
    return both_halves(summed, core)


def proj_rows(halves):
    return halves.reshape(2, 4, 8, HALF).transpose(2, 0, 1, 3).reshape(8, 8 * HALF)[:, :WIDTH]


def shards(features, w_five, w_six, w_seven, channel_params, w_proj, proj_bias, out_cotangent):
    core = lax.axis_index("core")
    place_at = core.astype(jnp.int32).reshape(1)
    zh_at = lax.axis_index("zh").astype(jnp.int32).reshape(1)
    inputs, cotangent = features[0], out_cotangent[0]
    square, flat, stack = (512, CH), (512, 128), (64, 32, HALF)

    (packed,) = staged(
        pack_kernel,
        (place_at, w_five, w_six, w_seven, w_proj, channel_params, proj_bias.reshape(1, 30)),
        [((4, 96, HALF), bf16)],
        [((8, HALF), f32)],
        flops=0,
        moved=2**18,
    )
    line = lax.all_to_all(packed, "zh", 0, 0, tiled=True)
    spread_ab = copies(line)

    line, first_rows, late_cotangent = together(line, inputs[:16], cotangent)
    next_row = lax.ppermute(first_rows, ("zl", "core"), [(1, 0), (2, 1), (3, 2)])
    unfold, spread_c = staged(
        split_kernel,
        (place_at, inputs, next_row, line),
        [((3, 512, CH), bf16), ((16, 4, 32, HALF), bf16)],
        [((128, CH), f32)],
        flops=2**28,
        moved=3 * 2**20,
    )
    unfold_other = swap_cores(unfold)
    cot_other = swap_cores(late_cotangent)
    grad_bias = (jnp.sum(late_cotangent.astype(f32), 0) + jnp.sum(cot_other.astype(f32), 0)).reshape(64, 1, 30)
    grad_bias = jnp.pad(grad_bias, [(0, 0), (0, 7), (16, 82)]).reshape(512, 128)

    mine_ab, spread_c, unfold, unfold_other, cot_other, grad_bias = across_plane(
        spread_ab, spread_c, unfold, unfold_other, cot_other, grad_bias
    )
    other_ab = swap_cores(mine_ab)
    bias = jnp.where(core == 0, mine_ab[:, 96, :], other_ab[:, 96, :])
    bias = bias.reshape(4, 4, 4, SEAT)[..., 16:46].transpose(0, 2, 1, 3).reshape(1, WIDTH).astype(f32)

    saved = lambda n: [((n, CH), f32), ((n, CH), f32), ((n, 128), f32)]
    w_shapes = [((1536, CH), bf16), ((1024, CH), bf16), ((1024, CH), bf16)]
    cp, w5, act_five, *saved_five, w6, w7, act_six, u6, s6, r6, u7, s7, r7, normed, unit, scale, give_c = staged(
        forward_kernel,
        (place_at, mine_ab, other_ab, unfold, unfold_other, cotangent, cot_other),
        [((16, CH), f32), w_shapes[0], ((1024, CH), bf16)]
        + saved(1024)
        + w_shapes[1:]
        + [(square, bf16)]
        + saved(512)
        + saved(256)
        + [((256, CH), bf16), ((256, CH), f32), ((256, 128), f32)]
        + [(stack, bf16)],
        [((1536, CH), f32), (flat, f32), ((1024, CH), f32), (square, f32), ((256, CH), f32), ((256, CH), bf16)]
        + [((CH, 4 * HALF), f32)],
        flops=2**31,
        moved=16 * 2**20,
    )

    mine_c, give_c = across_plane(spread_c, give_c)
    mine_c = mine_c.reshape(stack)
    other_c = swap_cores(mine_c)
    projected, edge, d_five, give_ab = staged(
        backward_kernel,
        (place_at, mine_c, other_c, cp, bias, cotangent, cot_other, normed, unit, scale, u7, s7, r7, w7, act_six)
        + (u6, s6, r6, w6, act_five, *saved_five, w5, unfold, unfold_other, grad_bias),
        [((128, WIDTH), bf16), ((8, CH), f32), ((1024, CH), bf16), ((16, BLOCK, HALF), bf16)],
        [((CH, WIDTH), bf16), ((CH, 8 * HALF), f32), ((1024, CH), f32), (square, f32), ((256, CH), f32)]
        + [((1536, HALF), f32), ((1024, HALF), f32), ((1024, HALF), f32), (square, bf16), ((256, CH), bf16)]
        + [((1024, HALF), bf16), (flat, f32), ((128, CH), f32)],
        flops=2**31,
        moved=16 * 2**20,
    )

    plane_c, give_ab = across_plane(give_c.reshape(16, 4, 32, HALF), give_ab)
    give_ab, plane_c, d_five = together(give_ab, plane_c, d_five)
    carried = lax.ppermute(edge[7:8], ("zl", "core"), [(0, 1), (1, 2), (2, 3)])
    (input_grad,) = staged(
        input_kernel,
        (place_at, d_five, w5, carried),
        [((1024, CH), bf16)],
        [(square, f32)] * 3,
        flops=2**30,
        moved=4 * 2**20,
    )
    sum_c = sum_line_by_permutes(sum_plane(plane_c), core)
    grad_proj = proj_rows(sum_c)
    plane_ab, grad_proj, input_grad = across_plane(give_ab, grad_proj, input_grad)
    sum_ab = sum_line(by_shard(sum_plane(plane_ab)))
    grad_five, grad_six, grad_seven, grad_channel, grad_bias = finish(place_at, zh_at, sum_ab, swap_cores(sum_ab))
    return (
        projected[None],
        input_grad[None],
        grad_five,
        grad_six,
        grad_seven,
        grad_channel,
        grad_proj,
        grad_bias.reshape(30),
    )


def solution(mesh):
    fine = Mesh(mesh.devices.reshape(4, 4, 4, 2, 2), ("x", "zh", "y", "zl", "core"))
    dp, seq = ("x", "zh", "y"), ("zl", "core")
    placed = (
        P(dp, seq, None),
        P(dp, None),
        P(dp, None),
        P(dp, None),
        P(dp, None),
        P(dp, None),
        P(dp),
        P(dp, seq, None),
    )
    return jax.shard_map(
        shards,
        mesh=fine,
        in_specs=placed,
        out_specs=(
            P(dp, seq, None),
            P(dp, seq, None),
            P(dp, None),
            P(dp, None),
            P(dp, None),
            P(dp, None),
            P(dp, None),
            P(dp),
        ),
        check_vma=False,
    )
```

```python
import jax
import jax.numpy as jnp
from jax import lax
from jax.experimental import pallas as pl
from jax.experimental.pallas import tpu as pltpu
from jax.sharding import Mesh, PartitionSpec as P

epsilon = 1e-05
f32 = jnp.float32
bf16 = jnp.bfloat16
CH = 512
WIDTH = 1920
HALF = 256
STEP = 128
SEAT = 64
BLOCK = 240
ALL_VMEM = 2**26 - 2**18


def dot(left, right, contract=(1, 0)):
    return lax.dot_general(
        left, right, (((contract[0],), (contract[1],)), ((), ())), preferred_element_type=f32
    )


def staged(body, operands, outs, scratch, flops, moved):
    count, made = len(operands) - 1, len(outs)

    def kernel(place_ref, *refs):
        refs = list(refs)
        groups = []
        for size in (count, made, count, made):
            groups.append(refs[:size])
            refs = refs[size:]
        from_hbm, to_hbm, ins, results = groups
        in_sems, out_sems, *rest = refs
        loads = [pltpu.make_async_copy(a, b, in_sems.at[i]) for i, (a, b) in enumerate(zip(from_hbm, ins))]
        stores = [pltpu.make_async_copy(a, b, out_sems.at[i]) for i, (a, b) in enumerate(zip(results, to_hbm))]
        for load in loads:
            load.start()
        waited, sent = set(), set()

        def need(*which):
            for ref in which:
                index = next(i for i, own in enumerate(ins) if own is ref)
                if index not in waited:
                    waited.add(index)
                    loads[index].wait()

        def give(*which):
            for ref in which:
                index = next(i for i, own in enumerate(results) if own is ref)
                if index not in sent:
                    sent.add(index)
                    stores[index].start()

        body(place_ref, ins, results, rest, need, give)
        need(*ins)
        give(*results)
        for store in stores:
            store.wait()

    hbm = pl.BlockSpec(memory_space=pltpu.HBM)
    return pl.pallas_call(
        kernel,
        out_shape=[jax.ShapeDtypeStruct(shape, kind) for shape, kind in outs],
        in_specs=[pl.BlockSpec(memory_space=pltpu.SMEM)] + [hbm] * count,
        out_specs=[hbm] * made,
        scratch_shapes=[pltpu.VMEM(array.shape, array.dtype) for array in operands[1:]]
        + [pltpu.VMEM(shape, kind) for shape, kind in outs]
        + [pltpu.SemaphoreType.DMA((count,)), pltpu.SemaphoreType.DMA((made,))]
        + [pltpu.VMEM(shape, kind) for shape, kind in scratch],
        compiler_params=pltpu.CompilerParams(vmem_limit_bytes=ALL_VMEM),
        cost_estimate=pl.CostEstimate(flops=flops, bytes_accessed=moved, transcendentals=0),
    )(*operands)


def place(index):
    return (index // 16) * 16 + (index % 4) * 4 + (index // 4) % 4


def seated(values, seat):
    return pltpu.roll(values, SEAT * seat, 1) if seat else values


def unseated(values, seat):
    return pltpu.roll(values, HALF - SEAT * seat, 1) if seat else values


def shard_of(plane, seat):
    return (plane // 4) * 16 + seat * 4 + plane % 4


def rows(index, size):
    return pl.ds(pl.multiple_of(index * size, size), size)


def by_core(core_ref, body):
    @pl.when(core_ref[0] == 0)
    def _():
        body(0, HALF)

    @pl.when(core_ref[0] != 0)
    def _():
        body(HALF, 0)


def row_mean(values):
    return jnp.sum(values, -1, keepdims=True) * (1.0 / CH)


def standard(values):
    centred = values - row_mean(values)
    scale = lax.rsqrt(row_mean(centred * centred) + epsilon)
    return centred * scale, scale


def fold(values):
    return jnp.sum(values.reshape(-1, 8, values.shape[-1]), 0)


def block_forward(pre_ref, cp_ref, first, act_ref, unit_ref, slope_ref, scale_ref):
    offset, gain, shift = (cp_ref[first + i : first + i + 1] for i in range(3))

    def step(i, _):
        at = rows(i, STEP)
        unit, scale = standard(pre_ref[at, :] + offset)
        z = unit * gain + shift
        cdf = 0.5 + 0.5 * lax.erf(z * 0.7071067811865476)
        act_ref[at, :] = (z * cdf).astype(bf16)
        slope_ref[at, :] = cdf + z * (0.3989422804014327 * jnp.exp(-0.5 * z * z))
        unit_ref[at, :] = unit
        scale_ref[at, :] = jnp.broadcast_to(scale, (STEP, 128))
        return 0

    lax.fori_loop(0, pre_ref.shape[0] // STEP, step, 0, unroll=2)


def block_backward(grad_ref, cp_ref, first, unit_ref, slope_ref, scale_ref, out_ref):
    gain = cp_ref[first + 1 : first + 2]

    def step(i, sums):
        at = rows(i, STEP)
        unit = unit_ref[at, :]
        dz = grad_ref[at, :] * slope_ref[at, :]
        dunit = dz * gain
        du = scale_ref[at, :1] * (dunit - row_mean(dunit) - unit * row_mean(dunit * unit))
        out_ref[at, :] = du.astype(bf16)
        return (sums[0] + fold(du), sums[1] + fold(dz * unit), sums[2] + fold(dz))

    zero = jnp.zeros((8, CH), f32)
    return lax.fori_loop(0, grad_ref.shape[0] // STEP, step, (zero, zero, zero), unroll=2)


def total(values):
    return jnp.sum(values, 0, keepdims=True)


def spread(transposed):
    group = lax.broadcasted_iota(jnp.int32, (256, 256), 1 if transposed else 0)
    position = lax.broadcasted_iota(jnp.int32, (256, 256), 0 if transposed else 1)
    return (position == 8 * (group % 32) + group // 32).astype(bf16)


def pack_kernel(place_ref, ins, outs, scratch, need, give):
    w5_ref, w6_ref, w7_ref, wp_ref, cp_ref, bias_ref = ins
    (out_ref,) = outs
    (small_ref,) = scratch
    need(*ins)
    small_ref[...] = jnp.zeros((8, HALF), f32)
    small_ref[:, :11] = cp_ref[...].astype(f32)
    small_ref[:1, 16:46] = bias_ref[...].astype(f32)

    def body(at, _):
        tail = small_ref[...] if at == 0 else jnp.zeros((8, HALF), f32)
        first = jnp.concatenate([w5_ref[:, at : at + HALF].astype(f32), tail], 0).astype(bf16)
        parts = []
        for b in range(4):
            start = 4 * at + HALF * b
            part = wp_ref[:, start : min(start + HALF, WIDTH)].astype(f32)
            if start + HALF > WIDTH:
                part = jnp.concatenate([part, jnp.zeros((8, start + HALF - WIDTH), f32)], 1)
            parts.append(part)
        last = jnp.concatenate(parts, 0).astype(bf16)
        for k in range(4):
            out_ref[k, :32, :] = first
            out_ref[k, 32:48, :] = w6_ref[:, at : at + HALF]
            out_ref[k, 48:64, :] = w7_ref[:, at : at + HALF]
            out_ref[k, 64:, :] = last

    by_core(place_ref, body)


def split_kernel(place_ref, ins, outs, scratch, need, give):
    x_ref, next_ref, line_ref = ins
    unfold_ref, spread_c_ref = outs
    (first_ref,) = scratch
    need(*ins)
    for k in range(16):
        spread_c_ref[k] = line_ref[:, 64:]
    give(spread_c_ref)
    matrix = spread(False)
    for j in range(4):
        groups = dot(matrix, x_ref[256 * j : 256 * j + 256, :])
        first_ref[32 * j : 32 * j + 32, :] = groups[:32]
        groups = groups.astype(bf16)
        for r in range(4):
            at = slice(128 * r + 32 * j, 128 * r + 32 * j + 32)
            unfold_ref[0, at, :] = groups[64 * r : 64 * r + 32]
            unfold_ref[1, at, :] = groups[64 * r + 32 : 64 * r + 64]
            if r > 0:
                unfold_ref[2, 128 * r - 128 + 32 * j : 128 * r - 96 + 32 * j, :] = groups[64 * r : 64 * r + 32]
    later = pltpu.roll(first_ref[...], 127, 0)
    last = lax.broadcasted_iota(jnp.int32, (128, CH), 0) == 127
    unfold_ref[2, 384:512, :] = jnp.where(last, next_ref[:1, :].astype(f32), later).astype(bf16)


def forward_kernel(core_ref, ins, outs, scratch, need, give):
    mine_ref, other_ref, unfold_ref, unfold_other_ref, cot_ref, cot_other_ref = ins
    (
        cp_ref, w5_ref, five_ref, unit5_ref, slope5_ref, scale5_ref,
        w6_ref, w7_ref, act6_ref, unit6_ref, slope6_ref, scale6_ref, unit7_ref, slope7_ref, scale7_ref,
        normed_ref, unit_ref, scale_ref, give_ref,
    ) = outs
    wide_ref, small_ref, pre5_ref, pre6_ref, pre7_ref, act7_ref, gp_ref = scratch
    need(mine_ref, other_ref)

    def unpack(mine_at, other_at):
        def step(i, _):
            for ref, at in ((mine_ref, mine_at), (other_ref, other_at)):
                block = ref[i, :112].astype(f32)
                for seat in range(4):
                    to = shard_of(i, seat)
                    low = 112 + 32 * seat
                    wide_ref[rows(to, 24), at : at + HALF] = block[24 * seat : 24 * seat + 24]
                    if at == 0:
                        small_ref[rows(to, 8), :] = unseated(block[96:104], seat)[:, :128]
                    w6_ref[rows(to, 16), at : at + HALF] = ref[i, low : low + 16]
                    w7_ref[rows(to, 16), at : at + HALF] = ref[i, low + 16 : low + 32]
            return 0

        lax.fori_loop(0, 16, step, 0)

    by_core(core_ref, unpack)
    cp_ref[...] = small_ref[...].T[:16]

    def narrow(i, _):
        w5_ref[rows(i, 128), :] = wide_ref[rows(i, 128), :].astype(bf16)
        return 0

    lax.fori_loop(0, 12, narrow, 0)
    give(cp_ref, w5_ref, w6_ref, w7_ref)
    need(unfold_ref, unfold_other_ref)

    for b, ref in enumerate((unfold_ref, unfold_other_ref)):

        def multiply(r, _, b=b, ref=ref):
            at = rows(r, 128)
            pre5_ref[rows(r + 4 * b, 128), :] = (
                dot(ref[0, at, :], w5_ref[:512, :]) + dot(ref[1, at, :], w5_ref[512:1024, :])
            ) + dot(ref[2, at, :], w5_ref[1024:, :])
            return 0

        lax.fori_loop(0, 4, multiply, 0)
    block_forward(pre5_ref, cp_ref, 0, five_ref, unit5_ref, slope5_ref, scale5_ref)
    give(five_ref, unit5_ref, slope5_ref, scale5_ref)
    for s in range(4):
        pre6_ref[128 * s : 128 * s + 128, :] = dot(five_ref[256 * s : 256 * s + 128, :], w6_ref[:512, :]) + dot(
            five_ref[256 * s + 128 : 256 * s + 256, :], w6_ref[512:, :]
        )
    block_forward(pre6_ref, cp_ref, 3, act6_ref, unit6_ref, slope6_ref, scale6_ref)
    give(act6_ref, unit6_ref, slope6_ref, scale6_ref)
    for b in range(2):
        pre7_ref[128 * b : 128 * b + 128, :] = dot(act6_ref[256 * b : 256 * b + 128, :], w7_ref[:512, :]) + dot(
            act6_ref[256 * b + 128 : 256 * b + 256, :], w7_ref[512:, :]
        )
    block_forward(pre7_ref, cp_ref, 6, act7_ref, unit7_ref, slope7_ref, scale7_ref)
    give(unit7_ref, slope7_ref, scale7_ref)

    unit, scale = standard(act7_ref[...].astype(f32))
    normed = (unit * cp_ref[9:10] + cp_ref[10:11]).astype(bf16)
    unit_ref[...] = unit
    scale_ref[...] = jnp.broadcast_to(scale, (256, 128))
    normed_ref[...] = normed
    give(unit_ref, scale_ref, normed_ref)
    flipped = normed.astype(f32).T.astype(bf16)
    need(cot_ref, cot_other_ref)

    def multiply_proj(mine_at, other_at):
        for b in range(4):
            start = 4 * mine_at + HALF * b
            cols = slice(start, min(start + HALF, WIDTH))
            both = jnp.concatenate([cot_ref[:, cols], cot_other_ref[:, cols]], 0)
            gp_ref[:, HALF * b : HALF * b + both.shape[1]] = dot(flipped, both)
            if both.shape[1] < HALF:
                gp_ref[:, HALF * b + both.shape[1] : HALF * (b + 1)] = jnp.zeros((CH, HALF - both.shape[1]), f32)

    by_core(core_ref, multiply_proj)

    def pack(i, _):
        block = gp_ref[rows(place(i), 8), :]
        parts = [block[:, HALF * b : HALF * (b + 1)] for b in range(4)]
        give_ref[i] = jnp.concatenate(parts, 0).astype(bf16)
        return 0

    lax.fori_loop(0, 64, pack, 0, unroll=4)


def backward_kernel(core_ref, ins, outs, scratch, need, give):
    (
        mine_ref, other_ref, cp_ref, bias_ref, cot_ref, cot_other_ref, normed_ref, unit_ref, scale_ref,
        unit7_ref, slope7_ref, scale7_ref, w7_ref, act6_ref, unit6_ref, slope6_ref, scale6_ref, w6_ref, five_ref,
        unit5_ref, slope5_ref, scale5_ref, w5_ref, unfold_ref, unfold_other_ref, gb_ref,
    ) = ins
    out_ref, edge_ref, d5_ref, give_ref = outs
    (
        wp_ref, wide_ref, pre5_ref, pre6_ref, pre7_ref, g5_ref, g6_ref, g7_ref, d6_ref, d7_ref, half_ref, small_ref, sums_ref,
    ) = scratch
    need(mine_ref, other_ref)

    def unpack(mine_at, other_at):
        def step(i, _):
            to = place(i)
            for ref, at in ((mine_ref, mine_at), (other_ref, other_at)):
                block = ref[i].astype(f32)
                for b in range(4):
                    wide_ref[rows(to, 8), 4 * at + HALF * b : 4 * at + HALF * (b + 1)] = block[8 * b : 8 * b + 8]
            return 0

        lax.fori_loop(0, 64, step, 0, unroll=4)

    by_core(core_ref, unpack)

    def narrow(i, _):
        wp_ref[rows(i, 64), :] = wide_ref[rows(i, 64), :WIDTH].astype(bf16)
        return 0

    lax.fori_loop(0, 8, narrow, 0)
    need(cp_ref, bias_ref, cot_ref, cot_other_ref, normed_ref)

    def keep(ref):
        size = ref.shape[0]

        def body(mine_at, other_at):
            half_ref[:size, :] = ref[:, mine_at : mine_at + HALF]

        by_core(core_ref, body)

    normed_grad = jnp.zeros((256, CH), f32)
    for b in range(8):
        cols = slice(HALF * b, min(HALF * (b + 1), WIDTH))
        out_ref[:, cols] = (dot(normed_ref[:128, :], wp_ref[:, cols]) + bias_ref[:, cols]).astype(bf16)
        both = jnp.concatenate([cot_ref[:, cols], cot_other_ref[:, cols]], 0)
        normed_grad = normed_grad + dot(both, wp_ref[:, cols], (1, 1))

    need(unit_ref, scale_ref, unit7_ref, slope7_ref, scale7_ref)
    give(out_ref)
    unit = unit_ref[...]
    dunit = normed_grad * cp_ref[9:10]
    sums_ref[...] = jnp.zeros((128, CH), f32)
    sums_ref[9:10, :] = total(normed_grad * unit)
    sums_ref[10:11, :] = total(normed_grad)
    pre7_ref[...] = scale_ref[:, :1] * (dunit - row_mean(dunit) - unit * row_mean(dunit * unit))

    for i, part in enumerate(block_backward(pre7_ref, cp_ref, 6, unit7_ref, slope7_ref, scale7_ref, d7_ref)):
        sums_ref[6 + i : 7 + i, :] = total(part)
    need(w7_ref, act6_ref)
    keep(d7_ref)
    for s in range(2):
        half = slice(512 * s, 512 * s + 512)
        left = [act6_ref[256 * b + 128 * s : 256 * b + 128 * s + 128, :] for b in range(2)]
        g7_ref[half, :] = dot(jnp.concatenate(left, 0), half_ref[:256, :], (0, 0))
        for b in range(2):
            at = 256 * b + 128 * s
            pre6_ref[at : at + 128, :] = dot(d7_ref[128 * b : 128 * b + 128, :], w7_ref[half, :], (1, 1))
    need(unit6_ref, slope6_ref, scale6_ref)
    for i, part in enumerate(block_backward(pre6_ref, cp_ref, 3, unit6_ref, slope6_ref, scale6_ref, d6_ref)):
        sums_ref[3 + i : 4 + i, :] = total(part)
    need(w6_ref, five_ref)
    keep(d6_ref)
    for r in range(2):
        half = slice(512 * r, 512 * r + 512)
        left = [five_ref[256 * s + 128 * r : 256 * s + 128 * r + 128, :] for s in range(4)]
        g6_ref[half, :] = dot(jnp.concatenate(left, 0), half_ref[:512, :], (0, 0))
        for s in range(4):
            at = 256 * s + 128 * r
            pre5_ref[at : at + 128, :] = dot(d6_ref[128 * s : 128 * s + 128, :], w6_ref[half, :], (1, 1))
    need(unit5_ref, slope5_ref, scale5_ref)
    for i, part in enumerate(block_backward(pre5_ref, cp_ref, 0, unit5_ref, slope5_ref, scale5_ref, d5_ref)):
        sums_ref[i : i + 1, :] = total(part)
    need(*ins)
    give(d5_ref)
    edge_ref[...] = dot(d5_ref[496:512, :], w5_ref[1024:, :], (1, 1))[8:]
    keep(d5_ref)
    for k in range(3):
        g5_ref[512 * k : 512 * k + 512, :] = dot(unfold_ref[k], half_ref[:512, :], (0, 0)) + dot(
            unfold_other_ref[k], half_ref[512:, :], (0, 0)
        )
    small_ref[...] = sums_ref[...].T

    def pack(mine_at, other_at):
        def step(i, _):
            parts, tail = [], jnp.zeros((8, HALF), f32)
            for seat in range(4):
                to = shard_of(i, seat)
                low = 112 + 32 * seat
                parts.append(g5_ref[rows(to, 24), :])
                if mine_at == 0:
                    own = small_ref[rows(to, 8), :] + gb_ref[rows(to, 8), :]
                    tail = tail + seated(jnp.concatenate([own, jnp.zeros((8, HALF - 128), f32)], 1), seat)
                give_ref[i, low : low + 16, :] = g6_ref[rows(to, 16), :].astype(bf16)
                give_ref[i, low + 16 : low + 32, :] = g7_ref[rows(to, 16), :].astype(bf16)
            parts += [tail, jnp.zeros((8, HALF), f32)]
            give_ref[i, :112, :] = jnp.concatenate(parts, 0).astype(bf16)
            return 0

        lax.fori_loop(0, 16, step, 0)

    by_core(core_ref, pack)


def input_kernel(place_ref, ins, outs, scratch, need, give):
    d_ref, w_ref, carried_ref = ins
    (out_ref,) = outs
    even_ref, odd_ref, third_ref = scratch
    need(*ins)

    def multiply(r, _):
        at = rows(r, 128)
        d = d_ref[at, :]
        even_ref[at, :] = dot(d, w_ref[:512, :], (1, 1))
        odd_ref[at, :] = dot(d, w_ref[512:1024, :], (1, 1))
        third_ref[at, :] = dot(d, w_ref[1024:, :], (1, 1))
        return 0

    lax.fori_loop(0, 4, multiply, 0)
    earlier = pltpu.roll(third_ref[384:512, :], 1, 0)
    first = lax.broadcasted_iota(jnp.int32, (128, CH), 0) == 0
    even_ref[:128, :] += jnp.where(first, carried_ref[...], earlier)
    even_ref[128:, :] += third_ref[:384, :]
    matrix = spread(True)
    for j in range(4):
        parts = []
        for r in range(4):
            at = slice(128 * r + 32 * j, 128 * r + 32 * j + 32)
            parts += [even_ref[at, :].astype(bf16), odd_ref[at, :].astype(bf16)]
        out_ref[256 * j : 256 * j + 256, :] = dot(matrix, jnp.concatenate(parts, 0)).astype(bf16)


def finish_kernel(place_ref, zh_ref, mine_ref, other_ref, *refs):
    to_hbm, outs, sems = refs[:5], refs[5:10], refs[10]
    g5_ref, g6_ref, g7_ref, channel_ref, bias_ref = outs

    def body(mine_at, other_at):
        for ref, at in ((mine_ref, mine_at), (other_ref, other_at)):
            g5_ref[:, at : at + HALF] = ref[:24, :]
            g6_ref[:, at : at + HALF] = ref[32:48, :]
            g7_ref[:, at : at + HALF] = ref[48:, :]
            if at == 0:
                small = sum(jnp.where(zh_ref[0] == seat, unseated(ref[24:32, :], seat), 0.0) for seat in range(4))
                channel_ref[...] = small[:, :11]
                bias_ref[...] = small[:1, 16:46]

    by_core(place_ref, body)
    stores = [pltpu.make_async_copy(a, b, sems.at[i]) for i, (a, b) in enumerate(zip(outs, to_hbm))]
    for store in stores:
        store.start()
    for store in stores:
        store.wait()


def finish(place_at, zh_at, mine, other):
    shapes = [(24, CH), (16, CH), (16, CH), (8, 11), (1, 30)]
    vmem = pl.BlockSpec(memory_space=pltpu.VMEM)
    return pl.pallas_call(
        finish_kernel,
        out_shape=[jax.ShapeDtypeStruct(shape, f32) for shape in shapes],
        in_specs=[pl.BlockSpec(memory_space=pltpu.SMEM)] * 2 + [vmem, vmem],
        out_specs=[pl.BlockSpec(memory_space=pltpu.HBM)] * 5,
        scratch_shapes=[pltpu.VMEM(shape, f32) for shape in shapes] + [pltpu.SemaphoreType.DMA((5,))],
        compiler_params=pltpu.CompilerParams(vmem_limit_bytes=2**23),
        cost_estimate=pl.CostEstimate(flops=0, bytes_accessed=2**18, transcendentals=0),
    )(place_at, zh_at, mine, other)


def copies_kernel(line, out_ref, block, out_sems):
    small = sum(seated(line[seat, 16:32, :].astype(f32)[8:], seat) for seat in range(4))
    parts = [line[seat, :32, :].astype(f32)[:24] for seat in range(4)] + [small, jnp.zeros((8, HALF), f32)]
    block[:112, :] = jnp.concatenate(parts, 0).astype(bf16)
    for seat in range(4):
        block[112 + 32 * seat : 144 + 32 * seat, :] = line[seat, 32:64, :]
    stores = [pltpu.make_async_copy(block, out_ref.at[k], out_sems.at[k]) for k in range(16)]
    for store in stores:
        store.start()
    for store in stores:
        store.wait()


def copies(line):
    return pl.pallas_call(
        copies_kernel,
        out_shape=jax.ShapeDtypeStruct((16, BLOCK, HALF), bf16),
        in_specs=[pl.BlockSpec(memory_space=pltpu.VMEM)],
        out_specs=pl.BlockSpec(memory_space=pltpu.HBM),
        scratch_shapes=[pltpu.VMEM((BLOCK, HALF), bf16), pltpu.SemaphoreType.DMA((16,))],
        compiler_params=pltpu.CompilerParams(vmem_limit_bytes=2**23),
        cost_estimate=pl.CostEstimate(flops=0, bytes_accessed=2**21, transcendentals=0),
    )(line)


def swap_cores(value):
    return lax.ppermute(value, "core", [(0, 1), (1, 0)])


def together(*values):
    return lax.optimization_barrier(values)


def around(value, axis, size, back):
    return lax.ppermute(value, axis, [(i, (i + back) % size) for i in range(size)])


def across_plane(value, *meanwhile):
    return together(lax.all_to_all(value, ("x", "y"), 0, 0, tiled=True), *meanwhile)


def sum_plane(plane):
    return jnp.sum(plane.astype(f32), 0).astype(bf16)


def both_halves(summed, core):
    other = swap_cores(summed)
    return jnp.stack([jnp.where(core == 0, summed, other), jnp.where(core == 0, other, summed)])


def by_shard(value):
    parts = [[value[24 * z : 24 * z + 24], value[96:104], value[112 + 32 * z : 144 + 32 * z]] for z in range(4)]
    return jnp.concatenate(sum(parts, []), 0).reshape(4, 64, HALF)


def sum_line(value, meanwhile):
    count = value.shape[1]
    line = jnp.broadcast_to(value[:, None], (4, 2, count, HALF)).reshape(8, count, HALF)
    line, meanwhile = together(lax.all_to_all(line, ("zh", "zl"), 0, 0, tiled=True), meanwhile)
    return jnp.sum(line.astype(f32), 0), meanwhile


def sum_line_by_permutes(value, core):
    zh = lax.axis_index("zh")
    pick = lambda k: lax.dynamic_index_in_dim(value, (zh + k) % 4, 0, False)
    parts = [pick(0)] + [around(pick(k), "zh", 4, k) for k in range(1, 4)]
    summed = sum(part.astype(f32) for part in parts)
    summed = summed + lax.ppermute(summed, "zl", [(0, 1), (1, 0)])
    return both_halves(summed, core)


def proj_rows(halves):
    return halves.reshape(2, 4, 8, HALF).transpose(2, 0, 1, 3).reshape(8, 8 * HALF)[:, :WIDTH]


def shards(features, w_five, w_six, w_seven, channel_params, w_proj, proj_bias, out_cotangent):
    core = lax.axis_index("core")
    place_at = core.astype(jnp.int32).reshape(1)
    zh_at = lax.axis_index("zh").astype(jnp.int32).reshape(1)
    inputs, cotangent = features[0], out_cotangent[0]
    square, flat, stack = (512, CH), (512, 128), (64, 32, HALF)

    (packed,) = staged(
        pack_kernel,
        (place_at, w_five, w_six, w_seven, w_proj, channel_params, proj_bias.reshape(1, 30)),
        [((4, 96, HALF), bf16)],
        [((8, HALF), f32)],
        flops=0,
        moved=2**18,
    )
    line = lax.all_to_all(packed, "zh", 0, 0, tiled=True)
    spread_ab = copies(line)

    line, first_rows, late_cotangent = together(line, inputs[:16], cotangent)
    next_row = lax.ppermute(first_rows, ("zl", "core"), [(1, 0), (2, 1), (3, 2)])
    unfold, spread_c = staged(
        split_kernel,
        (place_at, inputs, next_row, line),
        [((3, 512, CH), bf16), ((16, 4, 32, HALF), bf16)],
        [((128, CH), f32)],
        flops=2**28,
        moved=3 * 2**20,
    )
    unfold_other = swap_cores(unfold)
    cot_other = swap_cores(late_cotangent)
    grad_bias = (jnp.sum(late_cotangent.astype(f32), 0) + jnp.sum(cot_other.astype(f32), 0)).reshape(64, 1, 30)
    grad_bias = jnp.pad(grad_bias, [(0, 0), (0, 7), (16, 82)]).reshape(512, 128)

    mine_ab, spread_c, unfold, unfold_other, cot_other, grad_bias = across_plane(
        spread_ab, spread_c, unfold, unfold_other, cot_other, grad_bias
    )
    other_ab = swap_cores(mine_ab)
    bias = jnp.where(core == 0, mine_ab[:, 96, :], other_ab[:, 96, :])
    bias = bias.reshape(4, 4, 4, SEAT)[..., 16:46].transpose(0, 2, 1, 3).reshape(1, WIDTH).astype(f32)

    saved = lambda n: [((n, CH), f32), ((n, CH), f32), ((n, 128), f32)]
    w_shapes = [((1536, CH), bf16), ((1024, CH), bf16), ((1024, CH), bf16)]
    cp, w5, act_five, *saved_five, w6, w7, act_six, u6, s6, r6, u7, s7, r7, normed, unit, scale, give_c = staged(
        forward_kernel,
        (place_at, mine_ab, other_ab, unfold, unfold_other, cotangent, cot_other),
        [((16, CH), f32), w_shapes[0], ((1024, CH), bf16)]
        + saved(1024)
        + w_shapes[1:]
        + [(square, bf16)]
        + saved(512)
        + saved(256)
        + [((256, CH), bf16), ((256, CH), f32), ((256, 128), f32)]
        + [(stack, bf16)],
        [((1536, CH), f32), (flat, f32), ((1024, CH), f32), (square, f32), ((256, CH), f32), ((256, CH), bf16)]
        + [((CH, 4 * HALF), f32)],
        flops=2**31,
        moved=16 * 2**20,
    )

    mine_c, give_c = across_plane(spread_c, give_c)
    mine_c = mine_c.reshape(stack)
    other_c = swap_cores(mine_c)
    projected, edge, d_five, give_ab = staged(
        backward_kernel,
        (place_at, mine_c, other_c, cp, bias, cotangent, cot_other, normed, unit, scale, u7, s7, r7, w7, act_six)
        + (u6, s6, r6, w6, act_five, *saved_five, w5, unfold, unfold_other, grad_bias),
        [((128, WIDTH), bf16), ((8, CH), f32), ((1024, CH), bf16), ((16, BLOCK, HALF), bf16)],
        [((CH, WIDTH), bf16), ((CH, 8 * HALF), f32), ((1024, CH), f32), (square, f32), ((256, CH), f32)]
        + [((1536, HALF), f32), ((1024, HALF), f32), ((1024, HALF), f32), (square, bf16), ((256, CH), bf16)]
        + [((1024, HALF), bf16), (flat, f32), ((128, CH), f32)],
        flops=2**31,
        moved=16 * 2**20,
    )

    plane_c, give_ab = across_plane(give_c.reshape(16, 4, 32, HALF), give_ab)
    give_ab, plane_c = together(give_ab, plane_c)
    carried = lax.ppermute(edge[7:8], ("zl", "core"), [(0, 1), (1, 2), (2, 3)])
    sum_c = sum_line_by_permutes(sum_plane(plane_c), core)
    grad_proj = proj_rows(sum_c)
    plane_ab, grad_proj, carried = across_plane(give_ab, grad_proj, carried)
    part_ab, d_five = together(by_shard(sum_plane(plane_ab)), d_five)
    (input_grad,) = staged(
        input_kernel,
        (place_at, d_five, w5, carried),
        [((1024, CH), bf16)],
        [(square, f32)] * 3,
        flops=2**30,
        moved=4 * 2**20,
    )
    sum_ab, input_grad = sum_line(part_ab, input_grad)
    grad_five, grad_six, grad_seven, grad_channel, grad_bias = finish(place_at, zh_at, sum_ab, swap_cores(sum_ab))
    return (
        projected[None],
        input_grad[None],
        grad_five,
        grad_six,
        grad_seven,
        grad_channel,
        grad_proj,
        grad_bias.reshape(30),
    )


def solution(mesh):
    fine = Mesh(mesh.devices.reshape(4, 4, 4, 2, 2), ("x", "zh", "y", "zl", "core"))
    dp, seq = ("x", "zh", "y"), ("zl", "core")
    placed = (
        P(dp, seq, None),
        P(dp, None),
        P(dp, None),
        P(dp, None),
        P(dp, None),
        P(dp, None),
        P(dp),
        P(dp, seq, None),
    )
    return jax.shard_map(
        shards,
        mesh=fine,
        in_specs=placed,
        out_specs=(
            P(dp, seq, None),
            P(dp, seq, None),
            P(dp, None),
            P(dp, None),
            P(dp, None),
            P(dp, None),
            P(dp, None),
            P(dp),
        ),
        check_vma=False,
    )
```

```python
import jax
import jax.numpy as jnp
from jax import lax
from jax.experimental import pallas as pl
from jax.experimental.pallas import tpu as pltpu
from jax.sharding import Mesh, PartitionSpec as P

epsilon = 1e-05
f32 = jnp.float32
bf16 = jnp.bfloat16
CH = 512
WIDTH = 1920
HALF = 256
STEP = 128
SEAT = 64
BLOCK = 240
ALL_VMEM = 2**26 - 2**18


def dot(left, right, contract=(1, 0)):
    return lax.dot_general(
        left, right, (((contract[0],), (contract[1],)), ((), ())), preferred_element_type=f32
    )


def staged(body, operands, outs, scratch, flops, moved):
    count, made = len(operands) - 1, len(outs)

    def kernel(place_ref, *refs):
        refs = list(refs)
        groups = []
        for size in (count, made, count, made):
            groups.append(refs[:size])
            refs = refs[size:]
        from_hbm, to_hbm, ins, results = groups
        in_sems, out_sems, *rest = refs
        loads = [pltpu.make_async_copy(a, b, in_sems.at[i]) for i, (a, b) in enumerate(zip(from_hbm, ins))]
        stores = [pltpu.make_async_copy(a, b, out_sems.at[i]) for i, (a, b) in enumerate(zip(results, to_hbm))]
        for load in loads:
            load.start()
        waited, sent = set(), set()

        def need(*which):
            for ref in which:
                index = next(i for i, own in enumerate(ins) if own is ref)
                if index not in waited:
                    waited.add(index)
                    loads[index].wait()

        def give(*which):
            for ref in which:
                index = next(i for i, own in enumerate(results) if own is ref)
                if index not in sent:
                    sent.add(index)
                    stores[index].start()

        body(place_ref, ins, results, rest, need, give)
        need(*ins)
        give(*results)
        for store in stores:
            store.wait()

    hbm = pl.BlockSpec(memory_space=pltpu.HBM)
    return pl.pallas_call(
        kernel,
        out_shape=[jax.ShapeDtypeStruct(shape, kind) for shape, kind in outs],
        in_specs=[pl.BlockSpec(memory_space=pltpu.SMEM)] + [hbm] * count,
        out_specs=[hbm] * made,
        scratch_shapes=[pltpu.VMEM(array.shape, array.dtype) for array in operands[1:]]
        + [pltpu.VMEM(shape, kind) for shape, kind in outs]
        + [pltpu.SemaphoreType.DMA((count,)), pltpu.SemaphoreType.DMA((made,))]
        + [pltpu.VMEM(shape, kind) for shape, kind in scratch],
        compiler_params=pltpu.CompilerParams(vmem_limit_bytes=ALL_VMEM),
        cost_estimate=pl.CostEstimate(flops=flops, bytes_accessed=moved, transcendentals=0),
    )(*operands)


def place(index):
    return (index // 16) * 16 + (index % 4) * 4 + (index // 4) % 4


def seated(values, seat):
    return pltpu.roll(values, SEAT * seat, 1) if seat else values


def unseated(values, seat):
    return pltpu.roll(values, HALF - SEAT * seat, 1) if seat else values


def shard_of(plane, seat):
    return (plane // 4) * 16 + seat * 4 + plane % 4


def rows(index, size):
    return pl.ds(pl.multiple_of(index * size, size), size)


def by_core(core_ref, body):
    @pl.when(core_ref[0] == 0)
    def _():
        body(0, HALF)

    @pl.when(core_ref[0] != 0)
    def _():
        body(HALF, 0)


def row_mean(values):
    return jnp.sum(values, -1, keepdims=True) * (1.0 / CH)


def standard(values):
    centred = values - row_mean(values)
    scale = lax.rsqrt(row_mean(centred * centred) + epsilon)
    return centred * scale, scale


def fold(values):
    return jnp.sum(values.reshape(-1, 8, values.shape[-1]), 0)


def block_forward(pre_ref, cp_ref, first, act_ref, unit_ref, slope_ref, scale_ref):
    offset, gain, shift = (cp_ref[first + i : first + i + 1] for i in range(3))

    def step(i, _):
        at = rows(i, STEP)
        unit, scale = standard(pre_ref[at, :] + offset)
        z = unit * gain + shift
        cdf = 0.5 + 0.5 * lax.erf(z * 0.7071067811865476)
        act_ref[at, :] = (z * cdf).astype(bf16)
        slope_ref[at, :] = cdf + z * (0.3989422804014327 * jnp.exp(-0.5 * z * z))
        unit_ref[at, :] = unit
        scale_ref[at, :] = jnp.broadcast_to(scale, (STEP, 128))
        return 0

    lax.fori_loop(0, pre_ref.shape[0] // STEP, step, 0, unroll=2)


def block_backward(grad_ref, cp_ref, first, unit_ref, slope_ref, scale_ref, out_ref):
    gain = cp_ref[first + 1 : first + 2]

    def step(i, sums):
        at = rows(i, STEP)
        unit = unit_ref[at, :]
        dz = grad_ref[at, :] * slope_ref[at, :]
        dunit = dz * gain
        du = scale_ref[at, :1] * (dunit - row_mean(dunit) - unit * row_mean(dunit * unit))
        out_ref[at, :] = du.astype(bf16)
        return (sums[0] + fold(du), sums[1] + fold(dz * unit), sums[2] + fold(dz))

    zero = jnp.zeros((8, CH), f32)
    return lax.fori_loop(0, grad_ref.shape[0] // STEP, step, (zero, zero, zero), unroll=2)


def total(values):
    return jnp.sum(values, 0, keepdims=True)


def spread(transposed):
    group = lax.broadcasted_iota(jnp.int32, (256, 256), 1 if transposed else 0)
    position = lax.broadcasted_iota(jnp.int32, (256, 256), 0 if transposed else 1)
    return (position == 8 * (group % 32) + group // 32).astype(bf16)


def pack_kernel(place_ref, w5_ref, wp_ref, small_ref, w6_hbm, w7_hbm, out_hbm, w6_ref, w7_ref, out_ref, sems):
    loads = [pltpu.make_async_copy(w6_hbm, w6_ref, sems.at[0]), pltpu.make_async_copy(w7_hbm, w7_ref, sems.at[1])]
    for load in loads:
        load.start()
    for load in loads:
        load.wait()

    def body(at, _):
        both = [w5_ref[:, at : at + HALF].astype(f32), small_ref[:, at : at + HALF].astype(f32)]
        first = jnp.concatenate(both, 0).astype(bf16)
        parts = []
        for b in range(4):
            start = 4 * at + HALF * b
            part = wp_ref[:, start : min(start + HALF, WIDTH)].astype(f32)
            if start + HALF > WIDTH:
                part = jnp.concatenate([part, jnp.zeros((8, start + HALF - WIDTH), f32)], 1)
            parts.append(part)
        last = jnp.concatenate(parts, 0).astype(bf16)
        for k in range(4):
            out_ref[k, :32, :] = first
            out_ref[k, 32:48, :] = w6_ref[:, at : at + HALF]
            out_ref[k, 48:64, :] = w7_ref[:, at : at + HALF]
            out_ref[k, 64:, :] = last

    by_core(place_ref, body)
    store = pltpu.make_async_copy(out_ref, out_hbm, sems.at[2])
    store.start()
    store.wait()


def pack(place_at, w_five, w_proj, small, w_six, w_seven):
    vmem, hbm = pl.BlockSpec(memory_space=pltpu.VMEM), pl.BlockSpec(memory_space=pltpu.HBM)
    return pl.pallas_call(
        pack_kernel,
        out_shape=jax.ShapeDtypeStruct((4, 96, HALF), bf16),
        in_specs=[pl.BlockSpec(memory_space=pltpu.SMEM), vmem, vmem, vmem, hbm, hbm],
        out_specs=hbm,
        scratch_shapes=[pltpu.VMEM((16, CH), bf16), pltpu.VMEM((16, CH), bf16), pltpu.VMEM((4, 96, HALF), bf16)]
        + [pltpu.SemaphoreType.DMA((3,))],
        compiler_params=pltpu.CompilerParams(vmem_limit_bytes=2**23),
        cost_estimate=pl.CostEstimate(flops=0, bytes_accessed=2**18, transcendentals=0),
    )(place_at, w_five, w_proj, small, w_six, w_seven)


def split_kernel(place_ref, ins, outs, scratch, need, give):
    x_ref, next_ref, line_ref = ins
    unfold_ref, spread_c_ref = outs
    (first_ref,) = scratch
    need(*ins)
    for k in range(16):
        spread_c_ref[k] = line_ref[:, 64:]
    give(spread_c_ref)
    matrix = spread(False)
    for j in range(4):
        groups = dot(matrix, x_ref[256 * j : 256 * j + 256, :])
        first_ref[32 * j : 32 * j + 32, :] = groups[:32]
        groups = groups.astype(bf16)
        for r in range(4):
            at = slice(128 * r + 32 * j, 128 * r + 32 * j + 32)
            unfold_ref[0, at, :] = groups[64 * r : 64 * r + 32]
            unfold_ref[1, at, :] = groups[64 * r + 32 : 64 * r + 64]
            if r > 0:
                unfold_ref[2, 128 * r - 128 + 32 * j : 128 * r - 96 + 32 * j, :] = groups[64 * r : 64 * r + 32]
    later = pltpu.roll(first_ref[...], 127, 0)
    last = lax.broadcasted_iota(jnp.int32, (128, CH), 0) == 127
    unfold_ref[2, 384:512, :] = jnp.where(last, next_ref[:1, :].astype(f32), later).astype(bf16)


def forward_kernel(core_ref, ins, outs, scratch, need, give):
    mine_ref, other_ref, unfold_ref, unfold_other_ref, cot_ref, cot_other_ref = ins
    (
        cp_ref, w5_ref, five_ref, unit5_ref, slope5_ref, scale5_ref,
        w6_ref, w7_ref, act6_ref, unit6_ref, slope6_ref, scale6_ref, unit7_ref, slope7_ref, scale7_ref,
        normed_ref, unit_ref, scale_ref, give_ref,
    ) = outs
    wide_ref, small_ref, pre5_ref, pre6_ref, pre7_ref, act7_ref, gp_ref = scratch
    need(mine_ref, other_ref)

    def unpack(mine_at, other_at):
        def step(i, _):
            for ref, at in ((mine_ref, mine_at), (other_ref, other_at)):
                block = ref[i, :112].astype(f32)
                for seat in range(4):
                    to = shard_of(i, seat)
                    low = 112 + 32 * seat
                    wide_ref[rows(to, 24), at : at + HALF] = block[24 * seat : 24 * seat + 24]
                    if at == 0:
                        small_ref[rows(to, 8), :] = unseated(block[96:104], seat)[:, :128]
                    w6_ref[rows(to, 16), at : at + HALF] = ref[i, low : low + 16]
                    w7_ref[rows(to, 16), at : at + HALF] = ref[i, low + 16 : low + 32]
            return 0

        lax.fori_loop(0, 16, step, 0)

    by_core(core_ref, unpack)
    cp_ref[...] = small_ref[...].T[:16]

    def narrow(i, _):
        w5_ref[rows(i, 128), :] = wide_ref[rows(i, 128), :].astype(bf16)
        return 0

    lax.fori_loop(0, 12, narrow, 0)
    give(cp_ref, w5_ref, w6_ref, w7_ref)
    need(unfold_ref, unfold_other_ref)

    for b, ref in enumerate((unfold_ref, unfold_other_ref)):

        def multiply(r, _, b=b, ref=ref):
            at = rows(r, 128)
            pre5_ref[rows(r + 4 * b, 128), :] = (
                dot(ref[0, at, :], w5_ref[:512, :]) + dot(ref[1, at, :], w5_ref[512:1024, :])
            ) + dot(ref[2, at, :], w5_ref[1024:, :])
            return 0

        lax.fori_loop(0, 4, multiply, 0)
    block_forward(pre5_ref, cp_ref, 0, five_ref, unit5_ref, slope5_ref, scale5_ref)
    give(five_ref, unit5_ref, slope5_ref, scale5_ref)
    for s in range(4):
        pre6_ref[128 * s : 128 * s + 128, :] = dot(five_ref[256 * s : 256 * s + 128, :], w6_ref[:512, :]) + dot(
            five_ref[256 * s + 128 : 256 * s + 256, :], w6_ref[512:, :]
        )
    block_forward(pre6_ref, cp_ref, 3, act6_ref, unit6_ref, slope6_ref, scale6_ref)
    give(act6_ref, unit6_ref, slope6_ref, scale6_ref)
    for b in range(2):
        pre7_ref[128 * b : 128 * b + 128, :] = dot(act6_ref[256 * b : 256 * b + 128, :], w7_ref[:512, :]) + dot(
            act6_ref[256 * b + 128 : 256 * b + 256, :], w7_ref[512:, :]
        )
    block_forward(pre7_ref, cp_ref, 6, act7_ref, unit7_ref, slope7_ref, scale7_ref)
    give(unit7_ref, slope7_ref, scale7_ref)

    unit, scale = standard(act7_ref[...].astype(f32))
    normed = (unit * cp_ref[9:10] + cp_ref[10:11]).astype(bf16)
    unit_ref[...] = unit
    scale_ref[...] = jnp.broadcast_to(scale, (256, 128))
    normed_ref[...] = normed
    give(unit_ref, scale_ref, normed_ref)
    flipped = normed.astype(f32).T.astype(bf16)
    need(cot_ref, cot_other_ref)

    def multiply_proj(mine_at, other_at):
        for b in range(4):
            start = 4 * mine_at + HALF * b
            cols = slice(start, min(start + HALF, WIDTH))
            both = jnp.concatenate([cot_ref[:, cols], cot_other_ref[:, cols]], 0)
            gp_ref[:, HALF * b : HALF * b + both.shape[1]] = dot(flipped, both)
            if both.shape[1] < HALF:
                gp_ref[:, HALF * b + both.shape[1] : HALF * (b + 1)] = jnp.zeros((CH, HALF - both.shape[1]), f32)

    by_core(core_ref, multiply_proj)

    def pack(i, _):
        block = gp_ref[rows(place(i), 8), :]
        parts = [block[:, HALF * b : HALF * (b + 1)] for b in range(4)]
        give_ref[i] = jnp.concatenate(parts, 0).astype(bf16)
        return 0

    lax.fori_loop(0, 64, pack, 0, unroll=4)


def backward_kernel(core_ref, ins, outs, scratch, need, give):
    (
        mine_ref, other_ref, cp_ref, bias_ref, cot_ref, cot_other_ref, normed_ref, unit_ref, scale_ref,
        unit7_ref, slope7_ref, scale7_ref, w7_ref, act6_ref, unit6_ref, slope6_ref, scale6_ref, w6_ref, five_ref,
        unit5_ref, slope5_ref, scale5_ref, w5_ref, unfold_ref, unfold_other_ref, gb_ref,
    ) = ins
    out_ref, edge_ref, d5_ref, give_ref = outs
    (
        wp_ref, wide_ref, pre5_ref, pre6_ref, pre7_ref, g5_ref, g6_ref, g7_ref, d6_ref, d7_ref, half_ref, small_ref, sums_ref,
    ) = scratch
    need(mine_ref, other_ref)

    def unpack(mine_at, other_at):
        def step(i, _):
            to = place(i)
            for ref, at in ((mine_ref, mine_at), (other_ref, other_at)):
                block = ref[i].astype(f32)
                for b in range(4):
                    wide_ref[rows(to, 8), 4 * at + HALF * b : 4 * at + HALF * (b + 1)] = block[8 * b : 8 * b + 8]
            return 0

        lax.fori_loop(0, 64, step, 0, unroll=4)

    by_core(core_ref, unpack)

    def narrow(i, _):
        wp_ref[rows(i, 64), :] = wide_ref[rows(i, 64), :WIDTH].astype(bf16)
        return 0

    lax.fori_loop(0, 8, narrow, 0)
    need(cp_ref, bias_ref, cot_ref, cot_other_ref, normed_ref)

    def keep(ref):
        size = ref.shape[0]

        def body(mine_at, other_at):
            half_ref[:size, :] = ref[:, mine_at : mine_at + HALF]

        by_core(core_ref, body)

    normed_grad = jnp.zeros((256, CH), f32)
    for b in range(8):
        cols = slice(HALF * b, min(HALF * (b + 1), WIDTH))
        out_ref[:, cols] = (dot(normed_ref[:128, :], wp_ref[:, cols]) + bias_ref[:, cols]).astype(bf16)
        both = jnp.concatenate([cot_ref[:, cols], cot_other_ref[:, cols]], 0)
        normed_grad = normed_grad + dot(both, wp_ref[:, cols], (1, 1))

    need(unit_ref, scale_ref, unit7_ref, slope7_ref, scale7_ref)
    give(out_ref)
    unit = unit_ref[...]
    dunit = normed_grad * cp_ref[9:10]
    sums_ref[...] = jnp.zeros((128, CH), f32)
    sums_ref[9:10, :] = total(normed_grad * unit)
    sums_ref[10:11, :] = total(normed_grad)
    pre7_ref[...] = scale_ref[:, :1] * (dunit - row_mean(dunit) - unit * row_mean(dunit * unit))

    for i, part in enumerate(block_backward(pre7_ref, cp_ref, 6, unit7_ref, slope7_ref, scale7_ref, d7_ref)):
        sums_ref[6 + i : 7 + i, :] = total(part)
    need(w7_ref, act6_ref)
    keep(d7_ref)
    for s in range(2):
        half = slice(512 * s, 512 * s + 512)
        left = [act6_ref[256 * b + 128 * s : 256 * b + 128 * s + 128, :] for b in range(2)]
        g7_ref[half, :] = dot(jnp.concatenate(left, 0), half_ref[:256, :], (0, 0))
        for b in range(2):
            at = 256 * b + 128 * s
            pre6_ref[at : at + 128, :] = dot(d7_ref[128 * b : 128 * b + 128, :], w7_ref[half, :], (1, 1))
    need(unit6_ref, slope6_ref, scale6_ref)
    for i, part in enumerate(block_backward(pre6_ref, cp_ref, 3, unit6_ref, slope6_ref, scale6_ref, d6_ref)):
        sums_ref[3 + i : 4 + i, :] = total(part)
    need(w6_ref, five_ref)
    keep(d6_ref)
    for r in range(2):
        half = slice(512 * r, 512 * r + 512)
        left = [five_ref[256 * s + 128 * r : 256 * s + 128 * r + 128, :] for s in range(4)]
        g6_ref[half, :] = dot(jnp.concatenate(left, 0), half_ref[:512, :], (0, 0))
        for s in range(4):
            at = 256 * s + 128 * r
            pre5_ref[at : at + 128, :] = dot(d6_ref[128 * s : 128 * s + 128, :], w6_ref[half, :], (1, 1))
    need(unit5_ref, slope5_ref, scale5_ref)
    for i, part in enumerate(block_backward(pre5_ref, cp_ref, 0, unit5_ref, slope5_ref, scale5_ref, d5_ref)):
        sums_ref[i : i + 1, :] = total(part)
    need(*ins)
    give(d5_ref)
    edge_ref[...] = dot(d5_ref[496:512, :], w5_ref[1024:, :], (1, 1))[8:]
    keep(d5_ref)
    for k in range(3):
        g5_ref[512 * k : 512 * k + 512, :] = dot(unfold_ref[k], half_ref[:512, :], (0, 0)) + dot(
            unfold_other_ref[k], half_ref[512:, :], (0, 0)
        )
    small_ref[...] = sums_ref[...].T

    def pack(mine_at, other_at):
        def step(i, _):
            parts, tail = [], jnp.zeros((8, HALF), f32)
            for seat in range(4):
                to = shard_of(i, seat)
                low = 112 + 32 * seat
                parts.append(g5_ref[rows(to, 24), :])
                if mine_at == 0:
                    own = small_ref[rows(to, 8), :] + gb_ref[rows(to, 8), :]
                    tail = tail + seated(jnp.concatenate([own, jnp.zeros((8, HALF - 128), f32)], 1), seat)
                give_ref[i, low : low + 16, :] = g6_ref[rows(to, 16), :].astype(bf16)
                give_ref[i, low + 16 : low + 32, :] = g7_ref[rows(to, 16), :].astype(bf16)
            parts += [tail, jnp.zeros((8, HALF), f32)]
            give_ref[i, :112, :] = jnp.concatenate(parts, 0).astype(bf16)
            return 0

        lax.fori_loop(0, 16, step, 0)

    by_core(core_ref, pack)


def input_kernel(place_ref, ins, outs, scratch, need, give):
    d_ref, w_ref, carried_ref = ins
    (out_ref,) = outs
    even_ref, odd_ref, third_ref = scratch
    need(*ins)

    def multiply(r, _):
        at = rows(r, 128)
        d = d_ref[at, :]
        even_ref[at, :] = dot(d, w_ref[:512, :], (1, 1))
        odd_ref[at, :] = dot(d, w_ref[512:1024, :], (1, 1))
        third_ref[at, :] = dot(d, w_ref[1024:, :], (1, 1))
        return 0

    lax.fori_loop(0, 4, multiply, 0)
    earlier = pltpu.roll(third_ref[384:512, :], 1, 0)
    first = lax.broadcasted_iota(jnp.int32, (128, CH), 0) == 0
    even_ref[:128, :] += jnp.where(first, carried_ref[...], earlier)
    even_ref[128:, :] += third_ref[:384, :]
    matrix = spread(True)
    for j in range(4):
        parts = []
        for r in range(4):
            at = slice(128 * r + 32 * j, 128 * r + 32 * j + 32)
            parts += [even_ref[at, :].astype(bf16), odd_ref[at, :].astype(bf16)]
        out_ref[256 * j : 256 * j + 256, :] = dot(matrix, jnp.concatenate(parts, 0)).astype(bf16)


def finish_kernel(place_ref, zh_ref, mine_ref, other_ref, *refs):
    to_hbm, outs, sems = refs[:5], refs[5:10], refs[10]
    g5_ref, g6_ref, g7_ref, channel_ref, bias_ref = outs

    def body(mine_at, other_at):
        for ref, at in ((mine_ref, mine_at), (other_ref, other_at)):
            g5_ref[:, at : at + HALF] = ref[:24, :]
            g6_ref[:, at : at + HALF] = ref[32:48, :]
            g7_ref[:, at : at + HALF] = ref[48:, :]
            if at == 0:
                small = sum(jnp.where(zh_ref[0] == seat, unseated(ref[24:32, :], seat), 0.0) for seat in range(4))
                channel_ref[...] = small[:, :11]
                bias_ref[...] = small[:1, 16:46]

    by_core(place_ref, body)
    stores = [pltpu.make_async_copy(a, b, sems.at[i]) for i, (a, b) in enumerate(zip(outs, to_hbm))]
    for store in stores:
        store.start()
    for store in stores:
        store.wait()


def finish(place_at, zh_at, mine, other):
    shapes = [(24, CH), (16, CH), (16, CH), (8, 11), (1, 30)]
    vmem = pl.BlockSpec(memory_space=pltpu.VMEM)
    return pl.pallas_call(
        finish_kernel,
        out_shape=[jax.ShapeDtypeStruct(shape, f32) for shape in shapes],
        in_specs=[pl.BlockSpec(memory_space=pltpu.SMEM)] * 2 + [vmem, vmem],
        out_specs=[pl.BlockSpec(memory_space=pltpu.HBM)] * 5,
        scratch_shapes=[pltpu.VMEM(shape, f32) for shape in shapes] + [pltpu.SemaphoreType.DMA((5,))],
        compiler_params=pltpu.CompilerParams(vmem_limit_bytes=2**23),
        cost_estimate=pl.CostEstimate(flops=0, bytes_accessed=2**18, transcendentals=0),
    )(place_at, zh_at, mine, other)


def copies_kernel(line, out_ref, block, out_sems):
    small = sum(seated(line[seat, 16:32, :].astype(f32)[8:], seat) for seat in range(4))
    parts = [line[seat, :32, :].astype(f32)[:24] for seat in range(4)] + [small, jnp.zeros((8, HALF), f32)]
    block[:112, :] = jnp.concatenate(parts, 0).astype(bf16)
    for seat in range(4):
        block[112 + 32 * seat : 144 + 32 * seat, :] = line[seat, 32:64, :]
    stores = [pltpu.make_async_copy(block, out_ref.at[k], out_sems.at[k]) for k in range(16)]
    for store in stores:
        store.start()
    for store in stores:
        store.wait()


def copies(line):
    return pl.pallas_call(
        copies_kernel,
        out_shape=jax.ShapeDtypeStruct((16, BLOCK, HALF), bf16),
        in_specs=[pl.BlockSpec(memory_space=pltpu.VMEM)],
        out_specs=pl.BlockSpec(memory_space=pltpu.HBM),
        scratch_shapes=[pltpu.VMEM((BLOCK, HALF), bf16), pltpu.SemaphoreType.DMA((16,))],
        compiler_params=pltpu.CompilerParams(vmem_limit_bytes=2**23),
        cost_estimate=pl.CostEstimate(flops=0, bytes_accessed=2**21, transcendentals=0),
    )(line)


def swap_cores(value):
    return lax.ppermute(value, "core", [(0, 1), (1, 0)])


def together(*values):
    return lax.optimization_barrier(values)


def around(value, axis, size, back):
    return lax.ppermute(value, axis, [(i, (i + back) % size) for i in range(size)])


def across_plane(value, *meanwhile):
    return together(lax.all_to_all(value, ("x", "y"), 0, 0, tiled=True), *meanwhile)


def sum_plane(plane):
    return jnp.sum(plane.astype(f32), 0).astype(bf16)


def both_halves(summed, core):
    other = swap_cores(summed)
    return jnp.stack([jnp.where(core == 0, summed, other), jnp.where(core == 0, other, summed)])


def by_shard(value):
    parts = [[value[24 * z : 24 * z + 24], value[96:104], value[112 + 32 * z : 144 + 32 * z]] for z in range(4)]
    return jnp.concatenate(sum(parts, []), 0).reshape(4, 64, HALF)


def sum_line(value, meanwhile):
    count = value.shape[1]
    line = jnp.broadcast_to(value[:, None], (4, 2, count, HALF)).reshape(8, count, HALF)
    line, meanwhile = together(lax.all_to_all(line, ("zh", "zl"), 0, 0, tiled=True), meanwhile)
    return jnp.sum(line.astype(f32), 0), meanwhile


def sum_line_by_permutes(value, core):
    zh = lax.axis_index("zh")
    pick = lambda k: lax.dynamic_index_in_dim(value, (zh + k) % 4, 0, False)
    parts = [pick(0)] + [around(pick(k), "zh", 4, k) for k in range(1, 4)]
    summed = sum(part.astype(f32) for part in parts)
    summed = summed + lax.ppermute(summed, "zl", [(0, 1), (1, 0)])
    return both_halves(summed, core)


def proj_rows(halves):
    return halves.reshape(2, 4, 8, HALF).transpose(2, 0, 1, 3).reshape(8, 8 * HALF)[:, :WIDTH]


def shards(features, w_five, w_six, w_seven, channel_params, w_proj, proj_bias, out_cotangent):
    core = lax.axis_index("core")
    place_at = core.astype(jnp.int32).reshape(1)
    zh_at = lax.axis_index("zh").astype(jnp.int32).reshape(1)
    inputs, cotangent = features[0], out_cotangent[0]
    square, flat, stack = (512, CH), (512, 128), (64, 32, HALF)

    small = jnp.pad(channel_params, [(0, 0), (0, 501)]) + jnp.pad(proj_bias[None], [(0, 7), (16, 466)])
    packed = pack(place_at, w_five, w_proj, small, w_six, w_seven)
    line = lax.all_to_all(packed, "zh", 0, 0, tiled=True)
    spread_ab = copies(line)

    line, first_rows, late_cotangent = together(line, inputs[:16], cotangent)
    next_row = lax.ppermute(first_rows, ("zl", "core"), [(1, 0), (2, 1), (3, 2)])
    unfold, spread_c = staged(
        split_kernel,
        (place_at, inputs, next_row, line),
        [((3, 512, CH), bf16), ((16, 4, 32, HALF), bf16)],
        [((128, CH), f32)],
        flops=2**28,
        moved=3 * 2**20,
    )
    unfold_other = swap_cores(unfold)
    cot_other = swap_cores(late_cotangent)
    grad_bias = (jnp.sum(late_cotangent.astype(f32), 0) + jnp.sum(cot_other.astype(f32), 0)).reshape(64, 1, 30)
    grad_bias = jnp.pad(grad_bias, [(0, 0), (0, 7), (16, 82)]).reshape(512, 128)

    mine_ab, spread_c, unfold, unfold_other, cot_other, grad_bias = across_plane(
        spread_ab, spread_c, unfold, unfold_other, cot_other, grad_bias
    )
    other_ab = swap_cores(mine_ab)
    bias = jnp.where(core == 0, mine_ab[:, 96, :], other_ab[:, 96, :])
    bias = bias.reshape(4, 4, 4, SEAT)[..., 16:46].transpose(0, 2, 1, 3).reshape(1, WIDTH).astype(f32)

    saved = lambda n: [((n, CH), f32), ((n, CH), f32), ((n, 128), f32)]
    w_shapes = [((1536, CH), bf16), ((1024, CH), bf16), ((1024, CH), bf16)]
    cp, w5, act_five, *saved_five, w6, w7, act_six, u6, s6, r6, u7, s7, r7, normed, unit, scale, give_c = staged(
        forward_kernel,
        (place_at, mine_ab, other_ab, unfold, unfold_other, cotangent, cot_other),
        [((16, CH), f32), w_shapes[0], ((1024, CH), bf16)]
        + saved(1024)
        + w_shapes[1:]
        + [(square, bf16)]
        + saved(512)
        + saved(256)
        + [((256, CH), bf16), ((256, CH), f32), ((256, 128), f32)]
        + [(stack, bf16)],
        [((1536, CH), f32), (flat, f32), ((1024, CH), f32), (square, f32), ((256, CH), f32), ((256, CH), bf16)]
        + [((CH, 4 * HALF), f32)],
        flops=2**31,
        moved=16 * 2**20,
    )

    mine_c, give_c = across_plane(spread_c, give_c)
    mine_c = mine_c.reshape(stack)
    other_c = swap_cores(mine_c)
    projected, edge, d_five, give_ab = staged(
        backward_kernel,
        (place_at, mine_c, other_c, cp, bias, cotangent, cot_other, normed, unit, scale, u7, s7, r7, w7, act_six)
        + (u6, s6, r6, w6, act_five, *saved_five, w5, unfold, unfold_other, grad_bias),
        [((128, WIDTH), bf16), ((8, CH), f32), ((1024, CH), bf16), ((16, BLOCK, HALF), bf16)],
        [((CH, WIDTH), bf16), ((CH, 8 * HALF), f32), ((1024, CH), f32), (square, f32), ((256, CH), f32)]
        + [((1536, HALF), f32), ((1024, HALF), f32), ((1024, HALF), f32), (square, bf16), ((256, CH), bf16)]
        + [((1024, HALF), bf16), (flat, f32), ((128, CH), f32)],
        flops=2**31,
        moved=16 * 2**20,
    )

    plane_c, give_ab = across_plane(give_c.reshape(16, 4, 32, HALF), give_ab)
    give_ab, plane_c = together(give_ab, plane_c)
    carried = lax.ppermute(edge[7:8], ("zl", "core"), [(0, 1), (1, 2), (2, 3)])
    sum_c = sum_line_by_permutes(sum_plane(plane_c), core)
    grad_proj = proj_rows(sum_c)
    plane_ab, grad_proj, carried = across_plane(give_ab, grad_proj, carried)
    part_ab, d_five = together(by_shard(sum_plane(plane_ab)), d_five)
    (input_grad,) = staged(
        input_kernel,
        (place_at, d_five, w5, carried),
        [((1024, CH), bf16)],
        [(square, f32)] * 3,
        flops=2**30,
        moved=4 * 2**20,
    )
    sum_ab, input_grad = sum_line(part_ab, input_grad)
    grad_five, grad_six, grad_seven, grad_channel, grad_bias = finish(place_at, zh_at, sum_ab, swap_cores(sum_ab))
    return (
        projected[None],
        input_grad[None],
        grad_five,
        grad_six,
        grad_seven,
        grad_channel,
        grad_proj,
        grad_bias.reshape(30),
    )


def solution(mesh):
    fine = Mesh(mesh.devices.reshape(4, 4, 4, 2, 2), ("x", "zh", "y", "zl", "core"))
    dp, seq = ("x", "zh", "y"), ("zl", "core")
    placed = (
        P(dp, seq, None),
        P(dp, None),
        P(dp, None),
        P(dp, None),
        P(dp, None),
        P(dp, None),
        P(dp),
        P(dp, seq, None),
    )
    return jax.shard_map(
        shards,
        mesh=fine,
        in_specs=placed,
        out_specs=(
            P(dp, seq, None),
            P(dp, seq, None),
            P(dp, None),
            P(dp, None),
            P(dp, None),
            P(dp, None),
            P(dp, None),
            P(dp),
        ),
        check_vma=False,
    )
```
